32 devices in a mesh: space: 8 (over y, x, core), mode: 4 (over z).
Axes of the slice: x: 2, y: 2, z: 4, core: 2. Of those that a mesh axis runs over, the one named last changes fastest.
Arguments:
- state: float32 [128, 8, 64, 256], P('mode', 'space'), may hold values from -6 to 6
- control: float32 [128, 8, 64, 256], P('mode', 'space'), may hold values from -6 to 6
- adjoint: float32 [128, 8, 64, 256], P('mode', 'space'), may hold values from -6 to 6
- coefficient: float32 [7, 8, 64, 256], P(None, 'space'), may hold values from 0.1 to 1
- pattern: int32 [7, 128, 4], replicated, may hold values from 0 to 127
- weights: float32 [7, 128, 4], replicated, may hold values from -3 to 3
Outputs:
- state_residual: float32 [128, 8, 64, 256], P('mode', 'space')
- control_residual: float32 [128, 8, 64, 256], P('mode', 'space')
- adjoint_residual: float32 [128, 8, 64, 256], P('mode', 'space')
The draws below stay inside these ranges and needn't reach their ends.
Inputs may be any that keep to these rules, and one draw needn't show every extreme that they name: `pattern`: each entry names a chaos mode.
All inputs are finite; a program needn't handle non-finite values.
Results may differ from the reference program's by a relative error of at most 0.0001.
Values sent between devices are 32-bit elements; how exact they have to be, the bound alone decides.
No kernel may reach another device: no remote copies, remote signals or barrier semaphores. Data moves between devices by JAX's collectives and lax.ppermute only.
A program may use at most 384 MiB of HBM per device.

```python
import math
import jax
import jax.numpy as jnp
from jax import lax

P_SIZE = 128
KL = 7
NNZ = 4
NX = 8
NY = 64
NZ = 256


def plant(entries, own_key, smallest, largest):
    extent = entries.shape
    index_at = [jax.random.randint(jax.random.fold_in(own_key, axis), (), 0, extent[axis]) for axis in range(len(extent))]
    entries = entries.at[tuple(index_at)].set(smallest)
    longest = extent.index(max(extent))
    index_at[longest] = (index_at[longest] + 1) % extent[longest]
    return entries.at[tuple(index_at)].set(largest)


def steps_of(own_key, shape, pieces, least, largest):
    factor_of, own = 1.0, jax.random.fold_in(own_key, 6)
    for axis_at, shards_of in pieces:
        draws = jnp.exp(jax.random.uniform(jax.random.fold_in(own, axis_at), (shards_of,), jnp.float32, least / len(pieces), largest / len(pieces)))
        factor_of = factor_of * jnp.repeat(draws, shape[axis_at] // shards_of).reshape([-1 if axis == axis_at else 1 for axis in range(len(shape))])
    return factor_of


def centred(own_key, shape, scale, bound, pieces=(), kind=jnp.bfloat16):
    array = jax.random.normal(own_key, shape, jnp.float32) * scale
    if len(pieces) > 0:
        array = steps_of(own_key, shape, pieces, -0.22, 0.18) * array
    return jnp.clip(array, min=-bound, max=bound).astype(kind)


def setup_inputs(seed: int = 0) -> dict:
    streams_of = jax.random.split(jax.random.key(seed), 7)
    state = centred(streams_of[0], (P_SIZE, NX, NY, NZ), 1.0, 6.0, ((0, 4), (1, 8)), jnp.float32)
    control = centred(streams_of[1], (P_SIZE, NX, NY, NZ), 1.0, 6.0, ((0, 4), (1, 8)), jnp.float32)
    adjoint = centred(streams_of[2], (P_SIZE, NX, NY, NZ), 1.0, 6.0, ((0, 4), (1, 8)), jnp.float32)
    coefficient = jnp.clip(jnp.exp(math.log(1.0) - 2.3025851 * jax.random.uniform(streams_of[3], (KL, NX, NY, NZ), jnp.float32) ** steps_of(streams_of[3], (KL, NX, NY, NZ), ((1, 8),), -0.2, 0.2)), 0.1, 1.0)
    pattern = plant(jax.random.randint(streams_of[4], (KL, P_SIZE, NNZ), 0, P_SIZE), jax.random.fold_in(streams_of[4], 1), 0, P_SIZE - 1).astype(jnp.int32)
    weights = centred(streams_of[5], (KL, P_SIZE, NNZ), 0.5, 3.0, (), jnp.float32)
    return {"state": state, "control": control, "adjoint": adjoint, "coefficient": coefficient, "pattern": pattern, "weights": weights}


def coupling_matrices(pattern, weights):
    count = pattern.shape[1]
    modes = jnp.arange(count, dtype=jnp.int32)
    onehot = (pattern[..., None] == modes).astype(jnp.float32)
    dense = jnp.einsum("kis,kisj->kij", weights, onehot, precision=lax.Precision.HIGHEST)
    return 0.5 * (dense + jnp.swapaxes(dense, 1, 2))


def diffuse(coef, field):
    coef_pad = jnp.pad(coef, 1)
    field_pad = jnp.pad(field, ((0, 0), (1, 1), (1, 1), (1, 1)))
    total = jnp.zeros(field.shape, jnp.float32)
    shape_x, shape_y, shape_z = coef.shape
    for shift in ((1, 0, 0), (-1, 0, 0), (0, 1, 0), (0, -1, 0), (0, 0, 1), (0, 0, -1)):
        ox, oy, oz = 1 + shift[0], 1 + shift[1], 1 + shift[2]
        coef_next = coef_pad[ox:ox + shape_x, oy:oy + shape_y, oz:oz + shape_z]
        field_next = field_pad[:, ox:ox + shape_x, oy:oy + shape_y, oz:oz + shape_z]
        total = total + 0.5 * (coef + coef_next) * (field - field_next)
    return total


def operator(coupling, coefficient, field):
    total = jnp.zeros(field.shape, jnp.float32)
    for term in range(KL):
        smoothed = diffuse(coefficient[term], field)
        total = total + jnp.einsum("ij,jxyz->ixyz", coupling[term], smoothed, precision=lax.Precision.HIGHEST)
    return total


def reference(state, control, adjoint, coefficient, pattern, weights):
    coupling = coupling_matrices(pattern, weights)
    applied_state = operator(coupling, coefficient, state)
    applied_adjoint = operator(coupling, coefficient, adjoint)
    state_residual = state + applied_adjoint
    control_residual = 0.5 * control - adjoint
    adjoint_residual = applied_state - control
    return state_residual, control_residual, adjoint_residual
```

```python
import functools

import jax
import jax.numpy as jnp
from jax import lax
from jax.experimental import pallas as pl
from jax.experimental.pallas import tpu as pltpu
from jax.sharding import PartitionSpec as P

CHUNK_ROWS = 8
VMEM_LIMIT = 48 * 1024 * 1024


def params():
    return pltpu.CompilerParams(vmem_limit_bytes=VMEM_LIMIT)


def coupling_matrices(pattern, weights):
    count = pattern.shape[1]
    modes = jnp.arange(count, dtype=jnp.int32)
    hits = pattern[..., None] == modes
    dense = jnp.sum(jnp.where(hits, weights[..., None], 0.0), axis=2)
    coupling = 0.5 * (dense + jnp.swapaxes(dense, 1, 2))
    wide = jnp.swapaxes(coupling, 0, 1).reshape(count, -1)
    high = lax.reduce_precision(wide, 8, 7)
    return jnp.concatenate([high, wide - high], 0).astype(jnp.bfloat16)


def face_coefficients(own, below, above, first, rows):
    centre = lax.dynamic_slice_in_dim(own, first, rows, 1)
    tall = jnp.pad(own, ((0, 0), (1, 1), (0, 0)))
    near = lax.dynamic_slice_in_dim(tall, first, rows + 2, 1)
    wide = jnp.pad(centre, ((0, 0), (0, 0), (1, 1)))
    others = [below, above, near[:, :-2], near[:, 2:], wide[:, :, :-2], wide[:, :, 2:]]
    faces = jnp.stack([0.5 * (centre + other) for other in others], 1)
    terms, _, _, width = faces.shape
    return jnp.transpose(faces.reshape(terms * 6, rows, width), (1, 0, 2))


def pack_kernel(edge_rows, state_ref, adjoint_ref, *refs):
    out_ref = refs[-1]
    rows = state_ref.shape[1]
    out_ref[0, 0, :rows] = jnp.swapaxes(state_ref[...], 0, 1)
    out_ref[1, 0, :rows] = jnp.swapaxes(adjoint_ref[...], 0, 1)
    if edge_rows:
        out_ref[:, 0, rows:] = refs[0][:, 0]


def pack(state, adjoint, edges, chunk, rows, halves):
    modes, height, width = state.shape
    per_half = height // halves // rows
    block = pl.BlockSpec((modes, rows, width), lambda h: (0, h * per_half + chunk, 0))
    edge_rows = 0 if edges is None else edges.shape[2]
    in_specs = [block, block]
    operands = [state, adjoint]
    if edge_rows:
        in_specs.append(pl.BlockSpec((2, 1, edge_rows, modes, width), lambda h: (0, h, 0, 0, 0)))
        operands.append(edges)
    total = rows + edge_rows
    return pl.pallas_call(
        functools.partial(pack_kernel, edge_rows),
        grid=(halves,),
        in_specs=in_specs,
        out_specs=pl.BlockSpec((2, 1, total, modes, width), lambda h: (0, h, 0, 0, 0)),
        out_shape=jax.ShapeDtypeStruct((2, halves, total, modes, width), jnp.float32),
        compiler_params=params(),
        name="pack",
    )(*operands)


def edge_rows_of(state, adjoint, halves):
    height = state.shape[1]
    rows = height // halves
    fields = jnp.stack([state, adjoint])
    if halves == 1:
        return None
    if halves == 2:
        picked = jnp.stack([fields[:, :, rows], fields[:, :, rows - 1]], 1)
        return picked[:, :, None]
    tall = jnp.pad(fields, ((0, 0), (0, 0), (1, 1), (0, 0)))
    pairs = [jnp.stack([tall[:, :, h * rows], tall[:, :, (h + 1) * rows + 1]], 1) for h in range(halves)]
    return jnp.stack(pairs, 1)


def operator_kernel(rows, terms, modes, own_ref, before_ref, after_ref, below_ref, above_ref, face_ref, matrix_ref, out_ref, high, low):
    sources, _, part, width = own_ref.shape
    lanes = lax.broadcasted_iota(jnp.int32, (part, width), 1)
    step = 16

    def shifted(block):
        left = jnp.where(lanes[:step] == 0, 0.0, pltpu.roll(block, 1, 1))
        right = jnp.where(lanes[:step] == width - 1, 0.0, pltpu.roll(block, width - 1, 1))
        return left, right

    for row in range(rows):
        for source in range(sources):
            for start in range(0, part, step):
                here = pl.ds(start, step)
                centre = own_ref[source, row, here, :]
                up = own_ref[source, row - 1, here, :] if row else before_ref[source, 0, here, :]
                down = own_ref[source, row + 1, here, :] if row < rows - 1 else after_ref[source, 0, here, :]
                left, right = shifted(centre)
                others = (below_ref[source, row, here, :], above_ref[source, row, here, :], up, down, left, right)
                slopes = [centre - other for other in others]
                for term in range(terms):
                    total = face_ref[row, 6 * term : 6 * term + 1, :] * slopes[0]
                    for side in range(1, 6):
                        total = total + face_ref[row, 6 * term + side : 6 * term + side + 1, :] * slopes[side]
                    rounded = total.astype(jnp.bfloat16)
                    place = pl.ds(term * modes + source * part + start, step)
                    high[place, :] = rounded
                    low[place, :] = (total - rounded.astype(jnp.float32)).astype(jnp.bfloat16)
        both = jnp.dot(matrix_ref[...], high[...], preferred_element_type=jnp.float32)
        rest = jnp.dot(matrix_ref[:modes, :], low[...], preferred_element_type=jnp.float32)
        mixed = both[:modes] + both[modes:] + rest
        for source in range(sources):
            out_ref[source, row] = mixed[source * part : (source + 1) * part]


def apply_operator(own, before, after, below, above, faces, matrix, chunk, rows):
    sources, _, part, width = own.shape
    modes = sources * part
    terms = matrix.shape[1] // modes

    def whole(array):
        return pl.BlockSpec(array.shape, lambda i: (0,) * array.ndim)

    block = pl.BlockSpec((sources, rows, part, width), lambda i: (0, 0, 0, 0))
    edge = pl.BlockSpec((sources, 1, part, width), lambda i: (0, 0, 0, 0))
    return pl.pallas_call(
        functools.partial(operator_kernel, rows, terms, modes),
        grid=(1,),
        in_specs=[
            block,
            edge,
            edge,
            block,
            block,
            pl.BlockSpec((rows, 6 * terms, width), lambda i: (chunk, 0, 0)),
            whole(matrix),
        ],
        out_specs=block,
        out_shape=jax.ShapeDtypeStruct((sources, rows, part, width), jnp.float32),
        scratch_shapes=[
            pltpu.VMEM((terms * modes, width), jnp.bfloat16),
            pltpu.VMEM((terms * modes, width), jnp.bfloat16),
        ],
        compiler_params=params(),
        name="operator",
    )(own, before, after, below, above, faces, matrix)


def finish_kernel(mixed_ref, state_ref, control_ref, adjoint_ref, *refs):
    state_out, control_out, adjoint_out = refs[-3:]
    control = control_ref[...]
    state_out[...] = state_ref[...] + jnp.swapaxes(mixed_ref[1, 0], 0, 1)
    control_out[...] = 0.5 * control - adjoint_ref[...]
    adjoint_out[...] = jnp.swapaxes(mixed_ref[0, 0], 0, 1) - control


def finish(mixed, state, control, adjoint, outputs, chunk, rows, halves):
    modes, height, width = state.shape
    per_half = height // halves // rows
    block = pl.BlockSpec((modes, rows, width), lambda h: (0, h * per_half + chunk, 0))
    mixed = mixed.reshape(2, halves, rows, modes, width)
    in_specs = [pl.BlockSpec((2, 1, rows, modes, width), lambda h: (0, h, 0, 0, 0)), block, block, block]
    operands = [mixed, state, control, adjoint]
    aliases = {}
    if outputs is not None:
        in_specs += [pl.BlockSpec(memory_space=pl.ANY)] * 3
        operands += list(outputs)
        aliases = {4: 0, 5: 1, 6: 2}
    return pl.pallas_call(
        finish_kernel,
        grid=(halves,),
        in_specs=in_specs,
        out_specs=[block] * 3,
        out_shape=[jax.ShapeDtypeStruct(state.shape, jnp.float32)] * 3,
        input_output_aliases=aliases,
        compiler_params=params(),
        name="finish",
    )(*operands)


def shards(state, control, adjoint, coefficient, pattern, weights):
    shape = state.shape
    modes, _, height, width = shape
    state, control, adjoint = (a.reshape(modes, height, width) for a in (state, control, adjoint))
    owners = lax.axis_size("mode")
    halves = owners // 2
    half_rows = height // halves
    rows = min(CHUNK_ROWS, half_rows)
    chunks = half_rows // rows
    planes = lax.axis_size("space")
    forward = [(i, i + 1) for i in range(planes - 1)]
    backward = [(i + 1, i) for i in range(planes - 1)]
    half = lax.rem(lax.axis_index("mode"), halves)

    edges = edge_rows_of(state, adjoint, halves)
    fields = []
    for chunk in range(chunks):
        packed = pack(state, adjoint, edges if chunk == 0 else None, chunk, rows, halves)
        packed = packed.reshape((owners,) + packed.shape[2:])
        fields.append(lax.all_to_all(packed, "mode", 0, 0, tiled=True))

    matrix = coupling_matrices(pattern, weights)
    own = coefficient[:, 0]
    mine = lax.dynamic_slice_in_dim(own, half * half_rows, half_rows, 1)
    faces = face_coefficients(
        own,
        lax.ppermute(mine, "space", forward),
        lax.ppermute(mine, "space", backward),
        half * half_rows,
        half_rows,
    )

    nothing = jnp.zeros((owners, 1, modes, width), jnp.float32)
    first = last = nothing
    if halves == 2:
        edge = fields[0][:, rows : rows + 1]
        first = jnp.where(half == 1, edge, 0.0)
        last = jnp.where(half == 0, edge, 0.0)
    elif halves > 2:
        first = fields[0][:, rows : rows + 1]
        last = fields[0][:, rows + 1 : rows + 2]

    outputs = None
    for chunk in range(chunks):
        block = fields[chunk]
        body = block[:, :rows]
        below = lax.ppermute(body, "space", forward)
        above = lax.ppermute(body, "space", backward)
        before = fields[chunk - 1][:, rows - 1 : rows] if chunk else first
        after = fields[chunk + 1][:, :1] if chunk < chunks - 1 else last
        mixed = apply_operator(block, before, after, below, above, faces, matrix, chunk, rows)
        mixed = lax.all_to_all(mixed, "mode", 0, 0, tiled=True)
        outputs = finish(mixed, state, control, adjoint, outputs, chunk, rows, halves)
    return tuple(out.reshape(shape) for out in outputs)


def solution(mesh):
    split = P("mode", "space", None, None)
    in_specs = (split, split, split, P(None, "space", None, None), P(), P())
    return jax.shard_map(shards, mesh=mesh, in_specs=in_specs, out_specs=(split, split, split), check_vma=False)
```

```python
import functools

import jax
import jax.numpy as jnp
from jax import lax
from jax.experimental import pallas as pl
from jax.experimental.pallas import tpu as pltpu
from jax.sharding import PartitionSpec as P

CHUNK_ROWS = 8
VMEM_LIMIT = 48 * 1024 * 1024
ANYWHERE = pl.BlockSpec(memory_space=pl.ANY)


def params():
    return pltpu.CompilerParams(vmem_limit_bytes=VMEM_LIMIT)


def coupling_matrices(pattern, weights):
    count = pattern.shape[1]
    modes = jnp.arange(count, dtype=jnp.int32)
    hits = pattern[..., None] == modes
    dense = jnp.sum(jnp.where(hits, weights[..., None], 0.0), axis=2)
    coupling = 0.5 * (dense + jnp.swapaxes(dense, 1, 2))
    wide = jnp.swapaxes(coupling, 0, 1).reshape(count, -1)
    high = lax.reduce_precision(wide, 8, 7)
    return jnp.concatenate([high, wide - high], 0).astype(jnp.bfloat16)


def face_coefficients(own, below, above, first, rows):
    centre = lax.dynamic_slice_in_dim(own, first, rows, 1)
    tall = jnp.pad(own, ((0, 0), (1, 1), (0, 0)))
    near = lax.dynamic_slice_in_dim(tall, first, rows + 2, 1)
    wide = jnp.pad(centre, ((0, 0), (0, 0), (1, 1)))
    others = [below, above, near[:, :-2], near[:, 2:], wide[:, :, :-2], wide[:, :, 2:]]
    faces = jnp.stack([0.5 * (centre + other) for other in others], 1)
    terms, _, _, width = faces.shape
    return jnp.transpose(faces.reshape(terms * 6, rows, width), (1, 0, 2))


def pack_kernel(edge_rows, state_ref, adjoint_ref, *refs):
    out_ref = refs[-1]
    rows = state_ref.shape[1]
    out_ref[0, 0, :rows] = jnp.swapaxes(state_ref[...], 0, 1)
    out_ref[1, 0, :rows] = jnp.swapaxes(adjoint_ref[...], 0, 1)
    if edge_rows:
        out_ref[:, 0, rows:] = refs[0][:, 0]


def pack(state, adjoint, edges, chunk, rows, halves, earlier):
    modes, height, width = state.shape
    per_half = height // halves // rows
    block = pl.BlockSpec((modes, rows, width), lambda h: (0, h * per_half + chunk, 0))
    edge_rows = 0 if edges is None else edges.shape[2]
    in_specs = [block, block]
    operands = [state, adjoint]
    if edge_rows:
        in_specs.append(pl.BlockSpec((2, 1, edge_rows, modes, width), lambda h: (0, h, 0, 0, 0)))
        operands.append(edges)
    in_specs += [ANYWHERE] * len(earlier)
    operands += earlier
    total = rows + edge_rows
    return pl.pallas_call(
        functools.partial(pack_kernel, edge_rows),
        grid=(halves,),
        in_specs=in_specs,
        out_specs=pl.BlockSpec((2, 1, total, modes, width), lambda h: (0, h, 0, 0, 0)),
        out_shape=jax.ShapeDtypeStruct((2, halves, total, modes, width), jnp.float32),
        compiler_params=params(),
        name="pack",
    )(*operands)


def edge_rows_of(state, adjoint, halves):
    height = state.shape[1]
    rows = height // halves
    fields = jnp.stack([state, adjoint])
    if halves == 1:
        return None
    if halves == 2:
        picked = jnp.stack([fields[:, :, rows], fields[:, :, rows - 1]], 1)
        return picked[:, :, None]
    tall = jnp.pad(fields, ((0, 0), (0, 0), (1, 1), (0, 0)))
    pairs = [jnp.stack([tall[:, :, h * rows], tall[:, :, (h + 1) * rows + 1]], 1) for h in range(halves)]
    return jnp.stack(pairs, 1)


def operator_kernel(rows, terms, modes, own_ref, before_ref, after_ref, below_ref, above_ref, face_ref, matrix_ref, *refs):
    out_ref, high, low = refs[-3:]
    sources, _, part, width = own_ref.shape
    lanes = lax.broadcasted_iota(jnp.int32, (part, width), 1)
    step = 16

    def shifted(block):
        left = jnp.where(lanes[:step] == 0, 0.0, pltpu.roll(block, 1, 1))
        right = jnp.where(lanes[:step] == width - 1, 0.0, pltpu.roll(block, width - 1, 1))
        return left, right

    for row in range(rows):
        for source in range(sources):
            for start in range(0, part, step):
                here = pl.ds(start, step)
                centre = own_ref[source, row, here, :]
                up = own_ref[source, row - 1, here, :] if row else before_ref[source, 0, here, :]
                down = own_ref[source, row + 1, here, :] if row < rows - 1 else after_ref[source, 0, here, :]
                left, right = shifted(centre)
                others = (below_ref[source, row, here, :], above_ref[source, row, here, :], up, down, left, right)
                slopes = [centre - other for other in others]
                for term in range(terms):
                    total = face_ref[row, 6 * term : 6 * term + 1, :] * slopes[0]
                    for side in range(1, 6):
                        total = total + face_ref[row, 6 * term + side : 6 * term + side + 1, :] * slopes[side]
                    rounded = total.astype(jnp.bfloat16)
                    place = pl.ds(term * modes + source * part + start, step)
                    high[place, :] = rounded
                    low[place, :] = (total - rounded.astype(jnp.float32)).astype(jnp.bfloat16)
        both = jnp.dot(matrix_ref[...], high[...], preferred_element_type=jnp.float32)
        rest = jnp.dot(matrix_ref[:modes, :], low[...], preferred_element_type=jnp.float32)
        mixed = both[:modes] + both[modes:] + rest
        for source in range(sources):
            out_ref[source, row] = mixed[source * part : (source + 1) * part]


def apply_operator(own, before, after, below, above, faces, matrix, chunk, rows, earlier):
    sources, _, part, width = own.shape
    modes = sources * part
    terms = matrix.shape[1] // modes

    def whole(array):
        return pl.BlockSpec(array.shape, lambda i: (0,) * array.ndim)

    block = pl.BlockSpec((sources, rows, part, width), lambda i: (0, 0, 0, 0))
    edge = pl.BlockSpec((sources, 1, part, width), lambda i: (0, 0, 0, 0))
    return pl.pallas_call(
        functools.partial(operator_kernel, rows, terms, modes),
        grid=(1,),
        in_specs=[
            block,
            edge,
            edge,
            block,
            block,
            pl.BlockSpec((rows, 6 * terms, width), lambda i: (chunk, 0, 0)),
            whole(matrix),
        ]
        + [ANYWHERE] * len(earlier),
        out_specs=block,
        out_shape=jax.ShapeDtypeStruct((sources, rows, part, width), jnp.float32),
        scratch_shapes=[
            pltpu.VMEM((terms * modes, width), jnp.bfloat16),
            pltpu.VMEM((terms * modes, width), jnp.bfloat16),
        ],
        compiler_params=params(),
        name="operator",
    )(own, before, after, below, above, faces, matrix, *earlier)


def finish_kernel(mixed_ref, state_ref, control_ref, adjoint_ref, *refs):
    state_out, control_out, adjoint_out = refs[-3:]
    control = control_ref[...]
    state_out[...] = state_ref[...] + jnp.swapaxes(mixed_ref[1, 0], 0, 1)
    control_out[...] = 0.5 * control - adjoint_ref[...]
    adjoint_out[...] = jnp.swapaxes(mixed_ref[0, 0], 0, 1) - control


def finish(mixed, state, control, adjoint, outputs, chunk, rows, halves):
    modes, height, width = state.shape
    per_half = height // halves // rows
    block = pl.BlockSpec((modes, rows, width), lambda h: (0, h * per_half + chunk, 0))
    mixed = mixed.reshape(2, halves, rows, modes, width)
    in_specs = [pl.BlockSpec((2, 1, rows, modes, width), lambda h: (0, h, 0, 0, 0)), block, block, block]
    operands = [mixed, state, control, adjoint]
    aliases = {}
    if outputs is not None:
        in_specs += [pl.BlockSpec(memory_space=pl.ANY)] * 3
        operands += list(outputs)
        aliases = {4: 0, 5: 1, 6: 2}
    return pl.pallas_call(
        finish_kernel,
        grid=(halves,),
        in_specs=in_specs,
        out_specs=[block] * 3,
        out_shape=[jax.ShapeDtypeStruct(state.shape, jnp.float32)] * 3,
        input_output_aliases=aliases,
        compiler_params=params(),
        name="finish",
    )(*operands)


def shards(state, control, adjoint, coefficient, pattern, weights):
    shape = state.shape
    modes, _, height, width = shape
    state, control, adjoint = (a.reshape(modes, height, width) for a in (state, control, adjoint))
    owners = lax.axis_size("mode")
    halves = owners // 2
    half_rows = height // halves
    rows = min(CHUNK_ROWS, half_rows)
    chunks = half_rows // rows
    planes = lax.axis_size("space")
    forward = [(i, i + 1) for i in range(planes - 1)]
    backward = [(i + 1, i) for i in range(planes - 1)]
    half = lax.rem(lax.axis_index("mode"), halves)

    matrix = coupling_matrices(pattern, weights)
    own = coefficient[:, 0]
    mine = lax.dynamic_slice_in_dim(own, half * half_rows, half_rows, 1)
    faces = face_coefficients(
        own,
        lax.ppermute(mine, "space", forward),
        lax.ppermute(mine, "space", backward),
        half * half_rows,
        half_rows,
    )

    edges = edge_rows_of(state, adjoint, halves)
    fields, halos = [], []
    for chunk in range(chunks):
        earlier = list(halos[chunk - 2]) if chunk >= 2 else []
        packed = pack(state, adjoint, edges if chunk == 0 else None, chunk, rows, halves, earlier)
        packed = packed.reshape((owners,) + packed.shape[2:])
        fields.append(lax.all_to_all(packed, "mode", 0, 0, tiled=True))
        body = fields[chunk][:, :rows]
        halos.append((lax.ppermute(body, "space", forward), lax.ppermute(body, "space", backward)))

    nothing = jnp.zeros((owners, 1, modes, width), jnp.float32)
    first = last = nothing
    if halves == 2:
        edge = fields[0][:, rows : rows + 1]
        first = jnp.where(half == 1, edge, 0.0)
        last = jnp.where(half == 0, edge, 0.0)
    elif halves > 2:
        first = fields[0][:, rows : rows + 1]
        last = fields[0][:, rows + 1 : rows + 2]

    outputs = None
    for chunk in range(chunks):
        block = fields[chunk]
        below, above = halos[chunk]
        before = fields[chunk - 1][:, rows - 1 : rows] if chunk else first
        after = fields[chunk + 1][:, :1] if chunk < chunks - 1 else last
        earlier = list(halos[chunk + 2]) if chunk + 2 < chunks else []
        mixed = apply_operator(block, before, after, below, above, faces, matrix, chunk, rows, earlier)
        mixed = lax.all_to_all(mixed, "mode", 0, 0, tiled=True)
        outputs = finish(mixed, state, control, adjoint, outputs, chunk, rows, halves)
    return tuple(out.reshape(shape) for out in outputs)


def solution(mesh):
    split = P("mode", "space", None, None)
    in_specs = (split, split, split, P(None, "space", None, None), P(), P())
    return jax.shard_map(shards, mesh=mesh, in_specs=in_specs, out_specs=(split, split, split), check_vma=False)
```

```python
import functools

import jax
import jax.numpy as jnp
from jax import lax
from jax.experimental import pallas as pl
from jax.experimental.pallas import tpu as pltpu
from jax.sharding import PartitionSpec as P

PARTS = 2
VMEM_LIMIT = 48 * 1024 * 1024
ANYWHERE = pl.BlockSpec(memory_space=pl.ANY)
SCALARS = pl.BlockSpec(memory_space=pltpu.SMEM)


def whole(array):
    return pl.BlockSpec(array.shape, lambda *_: (0,) * array.ndim)


def params():
    return pltpu.CompilerParams(vmem_limit_bytes=VMEM_LIMIT)


def coupling_matrices(pattern, weights):
    count = pattern.shape[1]
    modes = jnp.arange(count, dtype=jnp.int32)
    hits = pattern[..., None] == modes
    dense = jnp.sum(jnp.where(hits, weights[..., None], 0.0), axis=2)
    coupling = 0.5 * (dense + jnp.swapaxes(dense, 1, 2))
    wide = jnp.swapaxes(coupling, 0, 1).reshape(count, -1)
    high = lax.reduce_precision(wide, 8, 7)
    return jnp.concatenate([high, wide - high], 0).astype(jnp.bfloat16)


def face_coefficients(own, below, above, first, rows):
    centre = lax.dynamic_slice_in_dim(own, first, rows, 1)
    tall = jnp.pad(own, ((0, 0), (1, 1), (0, 0)))
    near = lax.dynamic_slice_in_dim(tall, first, rows + 2, 1)
    wide = jnp.pad(centre, ((0, 0), (0, 0), (1, 1)))
    others = [below, above, near[:, :-2], near[:, 2:], wide[:, :, :-2], wide[:, :, 2:]]
    faces = jnp.stack([0.5 * (centre + other) for other in others], 1)
    terms, _, _, width = faces.shape
    return jnp.transpose(faces.reshape(terms * 6, rows, width), (1, 0, 2))


def pack_kernel(shift, owners, me_ref, state_ref, adjoint_ref, *refs):
    out_ref = refs[-1]
    field = lax.rem(me_ref[0] + shift, owners) // (owners // 2)

    @pl.when(field == 0)
    def _():
        out_ref[...] = jnp.swapaxes(state_ref[...], 0, 1)

    @pl.when(field == 1)
    def _():
        out_ref[...] = jnp.swapaxes(adjoint_ref[...], 0, 1)


def pack(me, state, adjoint, shift, part, rows, owners, earlier):
    modes, _, width = state.shape
    halves = owners // 2

    def place(i, me_ref):
        half = lax.rem(lax.rem(me_ref[0] + shift, owners), halves)
        return 0, half * PARTS + part, 0

    block = pl.BlockSpec((modes, rows, width), place)
    return pl.pallas_call(
        functools.partial(pack_kernel, shift, owners),
        grid_spec=pltpu.PrefetchScalarGridSpec(
            num_scalar_prefetch=1,
            grid=(1,),
            in_specs=[block, block] + [ANYWHERE] * len(earlier),
            out_specs=pl.BlockSpec((rows, modes, width), lambda i, me_ref: (0, 0, 0)),
        ),
        out_shape=jax.ShapeDtypeStruct((rows, modes, width), jnp.float32),
        compiler_params=params(),
        name="pack",
    )(me, state, adjoint, *earlier)


def extra_kernel(rows, halves, state_ref, adjoint_ref, out_ref):
    height = state_ref.shape[1]

    def row_of(ref, row):
        if row < 0 or row >= height:
            return jnp.zeros((ref.shape[0], ref.shape[2]), jnp.float32)
        tile = row // 8 * 8
        return jnp.swapaxes(ref[:, tile : tile + 8, :], 0, 1)[row - tile]

    for field, ref in enumerate((state_ref, adjoint_ref)):
        for half in range(halves):
            first = half * rows * PARTS
            places = [first + rows, first - 1, first + rows * PARTS]
            if halves == 2:
                places.pop(1 + half if half == 1 else 1)
            for index, row in enumerate(places):
                out_ref[field * halves + half, index] = row_of(ref, row)


def extra_rows(state, adjoint, rows, halves):
    modes, _, width = state.shape
    count = 2 if halves == 2 else 3
    shape = (2 * halves, count, modes, width)
    return pl.pallas_call(
        functools.partial(extra_kernel, rows, halves),
        grid=(1,),
        in_specs=[whole(state), whole(adjoint)],
        out_specs=pl.BlockSpec(shape, lambda i: (0,) * 4),
        out_shape=jax.ShapeDtypeStruct(shape, jnp.float32),
        compiler_params=params(),
        name="extra_rows",
    )(state, adjoint)


def operator_kernel(rows, terms, owners, part, me_ref, extra_ref, face_ref, matrix_ref, *refs):
    own, below, above, before = (refs[i * owners : (i + 1) * owners] for i in range(4))
    outs = refs[-owners - 3 : -3]
    high, low, mixed = refs[-3:]
    _, block, width = own[0].shape
    modes = owners * block
    halves = owners // 2
    me = me_ref[0]
    half = lax.rem(me, halves)
    step = 16
    lanes = lax.broadcasted_iota(jnp.int32, (step, width), 1)
    last = rows - 1

    def edge(source, which, here):
        if halves == 2:
            return jnp.where(half == 1 - which, extra_ref[source, 1, here, :], 0.0)
        return extra_ref[source, 1 + which, here, :]

    def one_row(row, place):
        for shift in range(owners):
            source = lax.rem(me + owners - shift, owners)
            for start in range(0, block, step):
                here = pl.ds(start, step)
                centre = own[shift][row, here, :]
                if place != "first":
                    up = own[shift][row - 1, here, :]
                elif part == 0:
                    up = edge(source, 0, here)
                else:
                    up = before[shift][0, here, :]
                if place != "last":
                    down = own[shift][row + 1, here, :]
                elif part == 0:
                    down = extra_ref[source, 0, here, :]
                else:
                    down = edge(source, 1, here)
                left = jnp.where(lanes == 0, 0.0, pltpu.roll(centre, 1, 1))
                right = jnp.where(lanes == width - 1, 0.0, pltpu.roll(centre, width - 1, 1))
                others = (below[shift][row, here, :], above[shift][row, here, :], up, down, left, right)
                slopes = [centre - other for other in others]
                for term in range(terms):
                    total = face_ref[row, 6 * term : 6 * term + 1, :] * slopes[0]
                    for side in range(1, 6):
                        total = total + face_ref[row, 6 * term + side : 6 * term + side + 1, :] * slopes[side]
                    rounded = total.astype(jnp.bfloat16)
                    at = pl.ds(pl.multiple_of(source * block + (term * modes + start), step), step)
                    high[at, :] = rounded
                    low[at, :] = (total - rounded.astype(jnp.float32)).astype(jnp.bfloat16)
        both = jnp.dot(matrix_ref[...], high[...], preferred_element_type=jnp.float32)
        rest = jnp.dot(matrix_ref[:modes, :], low[...], preferred_element_type=jnp.float32)
        mixed[...] = both[:modes] + both[modes:] + rest
        for shift in range(owners):
            owner = lax.rem(me + shift, owners)
            outs[shift][row] = mixed[pl.ds(pl.multiple_of(owner * block, block), block), :]

    def middle(row, carry):
        one_row(row, "middle")
        return carry

    one_row(0, "first")
    lax.fori_loop(1, last, middle, 0)
    one_row(last, "last")


def apply_operator(me, extra, faces, matrix, own, below, above, before, part, earlier):
    rows, block, width = own[0].shape
    owners = len(own)
    modes = owners * block
    terms = matrix.shape[1] // modes
    edge = pl.BlockSpec((1, block, width), lambda i: (rows - 1, 0, 0))
    out = whole(own[0])
    return pl.pallas_call(
        functools.partial(operator_kernel, rows, terms, owners, part),
        grid=(1,),
        in_specs=[
            SCALARS,
            whole(extra),
            pl.BlockSpec((rows, 6 * terms, width), lambda i: (part, 0, 0)),
            whole(matrix),
        ]
        + [out] * (3 * owners)
        + [edge] * owners
        + [ANYWHERE] * len(earlier),
        out_specs=[out] * owners,
        out_shape=[jax.ShapeDtypeStruct((rows, block, width), jnp.float32)] * owners,
        scratch_shapes=[
            pltpu.VMEM((terms * modes, width), jnp.bfloat16),
            pltpu.VMEM((terms * modes, width), jnp.bfloat16),
            pltpu.VMEM((modes, width), jnp.float32),
        ],
        compiler_params=params(),
        name="operator",
    )(me, extra, faces, matrix, *own, *below, *above, *before, *earlier)


def finish_kernel(owners, me_ref, *refs):
    mixed = refs[:owners]
    state_ref, control_ref, adjoint_ref = refs[owners : owners + 3]
    state_out, control_out, adjoint_out = refs[-3:]
    halves = owners // 2
    half = pl.program_id(0)
    control_out[...] = 0.5 * control_ref[...] - adjoint_ref[...]
    for shift in range(owners):
        source = lax.rem(me_ref[0] + owners - shift, owners)

        @pl.when(source == half)
        def _(shift=shift):
            adjoint_out[...] = jnp.swapaxes(mixed[shift][...], 0, 1) - control_ref[...]

        @pl.when(source == halves + half)
        def _(shift=shift):
            state_out[...] = state_ref[...] + jnp.swapaxes(mixed[shift][...], 0, 1)


def finish(me, mixed, state, control, adjoint, outputs, part):
    modes, _, width = state.shape
    owners = len(mixed)
    rows = mixed[0].shape[0]
    block = pl.BlockSpec((modes, rows, width), lambda h: (0, h * PARTS + part, 0))
    in_specs = [SCALARS] + [whole(m) for m in mixed] + [block] * 3
    operands = [me, *mixed, state, control, adjoint]
    aliases = {}
    if outputs is not None:
        aliases = {len(operands) + i: i for i in range(3)}
        in_specs += [ANYWHERE] * 3
        operands += list(outputs)
    return pl.pallas_call(
        functools.partial(finish_kernel, owners),
        grid=(owners // 2,),
        in_specs=in_specs,
        out_specs=[block] * 3,
        out_shape=[jax.ShapeDtypeStruct(state.shape, jnp.float32)] * 3,
        input_output_aliases=aliases,
        compiler_params=params(),
        name="finish",
    )(*operands)


def shards(state, control, adjoint, coefficient, pattern, weights):
    shape = state.shape
    modes, _, height, width = shape
    state, control, adjoint = (a.reshape(modes, height, width) for a in (state, control, adjoint))
    owners = lax.axis_size("mode")
    halves = owners // 2
    half_rows = height // halves
    rows = half_rows // PARTS
    planes = lax.axis_size("space")
    forward = [(i, i + 1) for i in range(planes - 1)]
    backward = [(i + 1, i) for i in range(planes - 1)]
    position = lax.axis_index("mode")
    me = position.astype(jnp.int32).reshape(1)
    first = lax.rem(position, halves) * half_rows
    shifts = sorted(range(1, owners), key=lambda s: min(s, owners - s))

    def move(array, shift):
        return lax.ppermute(array, "mode", [(i, (i + shift) % owners) for i in range(owners)])

    def beside(array):
        return lax.ppermute(array, "space", forward), lax.ppermute(array, "space", backward)

    own = coefficient[:, 0]
    below, above = beside(lax.dynamic_slice_in_dim(own, first, half_rows, 1))
    faces = face_coefficients(own, below, above, first, half_rows)
    matrix = coupling_matrices(pattern, weights)

    pieces = [[None] * owners for _ in range(PARTS)]
    halos = [[None] * owners for _ in range(PARTS)]
    order = []
    for part in range(PARTS):
        for shift in [0] + shifts:
            sent = len(order) - part - 1
            earlier = list(order[sent - 2]) if shift and sent >= 2 else []
            piece = pack(me, state, adjoint, shift, part, rows, owners, earlier)
            if shift:
                piece = move(piece, shift)
            pieces[part][shift] = piece
            halos[part][shift] = beside(piece)
            order.append(halos[part][shift])
    extra = lax.all_to_all(extra_rows(state, adjoint, rows, halves), "mode", 0, 0, tiled=True)

    outputs = None
    for part in range(PARTS):
        below, above = zip(*halos[part])
        before = pieces[0]
        earlier = [] if part else list(halos[1][0]) + list(halos[1][shifts[0]])
        mixed = apply_operator(me, extra, faces, matrix, pieces[part], below, above, before, part, earlier)
        mixed = [move(m, shift) if shift else m for shift, m in enumerate(mixed)]
        outputs = finish(me, mixed, state, control, adjoint, outputs, part)
    return tuple(out.reshape(shape) for out in outputs)


def solution(mesh):
    split = P("mode", "space", None, None)
    in_specs = (split, split, split, P(None, "space", None, None), P(), P())
    return jax.shard_map(shards, mesh=mesh, in_specs=in_specs, out_specs=(split, split, split), check_vma=False)
```

```python
import functools

import jax
import jax.numpy as jnp
from jax import lax
from jax.experimental import pallas as pl
from jax.experimental.pallas import tpu as pltpu
from jax.sharding import PartitionSpec as P

PARTS = 2
TILE = 8
ANYWHERE = pl.BlockSpec(memory_space=pl.ANY)
SCALARS = pl.BlockSpec(memory_space=pltpu.SMEM)


def whole(array):
    return pl.BlockSpec(array.shape, lambda *_: (0,) * array.ndim)


def params(mib=48):
    return pltpu.CompilerParams(vmem_limit_bytes=mib * 1024 * 1024)


def matrix_kernel(pattern_ref, weights_ref, out_ref):
    terms, entries, modes = pattern_ref.shape
    rows = lax.broadcasted_iota(jnp.int32, (modes, modes), 0)
    for term in range(terms):
        flipped = jnp.zeros((modes, modes), jnp.float32)
        for entry in range(entries):
            hits = pattern_ref[term, entry : entry + 1, :] == rows
            flipped = flipped + jnp.where(hits, weights_ref[term, entry : entry + 1, :], 0.0)
        coupling = 0.5 * (flipped + flipped.T)
        high = coupling.astype(jnp.bfloat16)
        at = slice(term * modes, (term + 1) * modes)
        out_ref[:modes, at] = high
        out_ref[modes:, at] = (coupling - high.astype(jnp.float32)).astype(jnp.bfloat16)


def coupling_matrices(pattern, weights):
    terms, modes, _ = pattern.shape
    pattern, weights = jnp.swapaxes(pattern, 1, 2), jnp.swapaxes(weights, 1, 2)
    shape = (2 * modes, terms * modes)
    return pl.pallas_call(
        matrix_kernel,
        grid=(1,),
        in_specs=[whole(pattern), whole(weights)],
        out_specs=pl.BlockSpec(shape, lambda i: (0, 0)),
        out_shape=jax.ShapeDtypeStruct(shape, jnp.bfloat16),
        compiler_params=params(),
        name="coupling",
    )(pattern, weights)


def target(me_ref, shift, owners):
    block = lax.rem(me_ref[0] + shift, owners)
    return block // (owners // 2), lax.rem(block, owners // 2)


def edge_count(halves):
    return 1 if halves == 2 else 2


def tile_specs(modes, height, width, shift, owners, part_rows):
    halves = owners // 2
    half_tiles = height // halves // TILE

    def spec(index):
        def place(i, me_ref):
            _, half = target(me_ref, shift, owners)
            return 0, jnp.clip(half * half_tiles + index, 0, height // TILE - 1), 0

        return pl.BlockSpec((modes, TILE, width), place)

    return [spec(part_rows // TILE), spec(-1), spec(half_tiles)]


def write_edges(out_ref, at, half, halves, before_ref, after_ref):
    before = jnp.swapaxes(before_ref[...], 0, 1)[TILE - 1]
    after = jnp.swapaxes(after_ref[...], 0, 1)[0]
    if halves == 2:
        out_ref[at] = jnp.where(half == 1, before, after)
    else:
        out_ref[at] = jnp.where(half > 0, before, 0.0)
        out_ref[at + 1] = jnp.where(half < halves - 1, after, 0.0)


def pack_kernel(shifts, owners, extras, me_ref, *refs):
    halves = owners // 2
    per_field = 4 if extras else 1
    outs = refs[-len(shifts) :]
    for index, shift in enumerate(shifts):
        field, half = target(me_ref, shift, owners)
        out_ref = outs[index]
        for which in range(2):
            mine = refs[(2 * index + which) * per_field : (2 * index + which + 1) * per_field]

            @pl.when(field == which)
            def _(mine=mine, out_ref=out_ref, half=half):
                rows = mine[0].shape[1]
                out_ref[:rows] = jnp.swapaxes(mine[0][...], 0, 1)
                if extras:
                    out_ref[rows] = jnp.swapaxes(mine[1][...], 0, 1)[0]
                    write_edges(out_ref, rows + 1, half, halves, mine[2], mine[3])


def pack(me, state, adjoint, shifts, part, rows, owners, earlier):
    modes, height, width = state.shape
    extras = part == 0
    count = rows + (1 + edge_count(owners // 2) if extras else 0)
    in_specs, operands = [], []
    for shift in shifts:

        def place(i, me_ref, shift=shift):
            return 0, target(me_ref, shift, owners)[1] * PARTS + part, 0

        specs = [pl.BlockSpec((modes, rows, width), place)]
        if extras:
            specs += tile_specs(modes, height, width, shift, owners, rows)
        for array in (state, adjoint):
            in_specs += specs
            operands += [array] * len(specs)
    return pl.pallas_call(
        functools.partial(pack_kernel, shifts, owners, extras),
        grid_spec=pltpu.PrefetchScalarGridSpec(
            num_scalar_prefetch=1,
            grid=(1,),
            in_specs=in_specs + [ANYWHERE] * len(earlier),
            out_specs=[pl.BlockSpec((count, modes, width), lambda i, me_ref: (0, 0, 0))] * len(shifts),
        ),
        out_shape=[jax.ShapeDtypeStruct((count, modes, width), jnp.float32)] * len(shifts),
        compiler_params=params(60),
        name="pack",
    )(me, *operands, *earlier)


def pack_own_kernel(owners, me_ref, *refs):
    coef_ref, out_ref = refs[-2:]
    halves = owners // 2
    field, half = target(me_ref, 0, owners)
    for which in range(2):
        mine = refs[which * 3 : which * 3 + 3]

        @pl.when(field == which)
        def _(mine=mine):
            rows = mine[0].shape[1]
            out_ref[:rows] = jnp.swapaxes(mine[0][...], 0, 1)
            write_edges(out_ref, rows, half, halves, mine[1], mine[2])

    terms = coef_ref.shape[0]
    out_ref[out_ref.shape[0] - terms :] = coef_ref[...]


def pack_own(me, state, adjoint, coef, owners):
    modes, height, width = state.shape
    halves = owners // 2
    half_rows = height // halves
    terms = coef.shape[0]
    count = half_rows + edge_count(halves) + terms

    def place(i, me_ref):
        return 0, target(me_ref, 0, owners)[1], 0

    specs = [pl.BlockSpec((modes, half_rows, width), place)]
    specs += tile_specs(modes, height, width, 0, owners, half_rows // PARTS)[1:]
    return pl.pallas_call(
        functools.partial(pack_own_kernel, owners),
        grid_spec=pltpu.PrefetchScalarGridSpec(
            num_scalar_prefetch=1,
            grid=(1,),
            in_specs=specs + specs + [pl.BlockSpec((terms, half_rows, width), place)],
            out_specs=pl.BlockSpec((count, modes, width), lambda i, me_ref: (0, 0, 0)),
        ),
        out_shape=jax.ShapeDtypeStruct((count, modes, width), jnp.float32),
        compiler_params=params(60),
        name="pack_own",
    )(me, *([state] * 3 + [adjoint] * 3), coef)


def operator_kernel(shifts, rows, terms, part, me_ref, coef_ref, matrix_ref, *refs):
    owners = len(shifts) + 1
    own, own_below, own_above, below, above = refs[:5]
    head = refs[5 : 5 + len(shifts)]
    pieces = refs[5 + part * len(shifts) : 5 + (part + 1) * len(shifts)]
    outs = refs[-owners - 6 : -6]
    slots, mixed, faces = ((refs[-6], refs[-5]), (refs[-4], refs[-3])), refs[-2], refs[-1]
    _, block, width = own.shape
    modes = owners * block
    halves = owners // 2
    half_rows = rows * PARTS
    edges = edge_count(halves)
    me = me_ref[0]
    half = lax.rem(me, halves)
    step = 16
    lanes = lax.broadcasted_iota(jnp.int32, (step, width), 1)
    last = rows - 1

    def with_sides(values, lane):
        left = jnp.where(lane == 0, 0.0, pltpu.roll(values, 1, 1))
        right = jnp.where(lane == width - 1, 0.0, pltpu.roll(values, width - 1, 1))
        return left, right

    first_row = half * half_rows + part * rows
    height = coef_ref.shape[1]
    face_lanes = lax.broadcasted_iota(jnp.int32, (rows, width), 1)
    face_rows = lax.broadcasted_iota(jnp.int32, (rows, width), 0)
    for term in range(terms):
        centre = coef_ref[term, pl.ds(pl.multiple_of(first_row, TILE), rows), :]
        row_before = coef_ref[term, pl.ds(jnp.maximum(first_row - 1, 0), 1), :]
        row_after = coef_ref[term, pl.ds(jnp.minimum(first_row + rows, height - 1), 1), :]
        row_before = jnp.where(first_row > 0, row_before, 0.0)
        row_after = jnp.where(first_row + rows < height, row_after, 0.0)
        up = jnp.where(face_rows == 0, row_before, pltpu.roll(centre, 1, 0))
        down = jnp.where(face_rows == last, row_after, pltpu.roll(centre, last, 0))
        left, right = with_sides(centre, face_lanes)
        at = half_rows + edges + term
        here = slice(part * rows, (part + 1) * rows)
        others = (own_below[at, here, :], own_above[at, here, :], up, down, left, right)
        for side, other in enumerate(others):
            faces[6 * term + side] = 0.5 * (centre + other)

    def edge(index, which, here):
        ref, at = (head[index - 1], rows + 1) if index else (own, half_rows)
        if halves == 2:
            return jnp.where(half == 1 - which, ref[at, here, :], 0.0)
        return ref[at + which, here, :]

    def stencil(row, place, slot):
        high, low = slots[slot]
        for index, shift in enumerate([0] + shifts):
            source = lax.rem(me + owners - shift, owners)
            if index:
                base, near, ref, below_ref, above_ref = 0, (index - 1) * rows, pieces[index - 1], below, above
            else:
                base, near, ref, below_ref, above_ref = part * rows, part * rows, own, own_below, own_above
            for start in range(0, block, step):
                here = pl.ds(start, step)
                centre = ref[base + row, here, :]
                if place != "first":
                    up = ref[base + row - 1, here, :]
                elif part == 0:
                    up = edge(index, 0, here)
                else:
                    up = head[index - 1][last, here, :] if index else own[base - 1, here, :]
                if place != "last":
                    down = ref[base + row + 1, here, :]
                elif part == 0:
                    down = ref[base + rows, here, :]
                else:
                    down = edge(index, 1, here)
                left, right = with_sides(centre, lanes)
                others = (below_ref[near + row, here, :], above_ref[near + row, here, :], up, down, left, right)
                slopes = [centre - other for other in others]
                for term in range(terms):
                    total = faces[6 * term, pl.ds(row, 1), :] * slopes[0]
                    for side in range(1, 6):
                        total = total + faces[6 * term + side, pl.ds(row, 1), :] * slopes[side]
                    rounded = total.astype(jnp.bfloat16)
                    at = pl.ds(pl.multiple_of(source * block + (term * modes + start), step), step)
                    high[at, :] = rounded
                    low[at, :] = (total - rounded.astype(jnp.float32)).astype(jnp.bfloat16)

    def mix(row, slot):
        high, low = slots[slot]
        both = jnp.dot(matrix_ref[...], high[...], preferred_element_type=jnp.float32)
        rest = jnp.dot(matrix_ref[:modes, :], low[...], preferred_element_type=jnp.float32)
        mixed[...] = both[:modes] + both[modes:] + rest
        for index, shift in enumerate([0] + shifts):
            owner = lax.rem(me + shift, owners)
            outs[index][row] = mixed[pl.ds(pl.multiple_of(owner * block, block), block), :]

    def two_rows(pair, carry):
        row = 2 * pair
        stencil(row + 1, "middle", 1)
        mix(row, 0)
        stencil(row + 2, "middle", 0)
        mix(row + 1, 1)
        return carry

    stencil(0, "first", 0)
    lax.fori_loop(0, rows // 2 - 1, two_rows, 0)
    stencil(last, "last", 1)
    mix(last - 1, 0)
    mix(last, 1)


def apply_operator(me, coef, matrix, own, own_near, pieces, near, part, rows, shifts):
    _, block, width = own.shape
    owners = len(shifts) + 1
    modes = owners * block
    terms = coef.shape[0]
    operands = [coef, matrix, own, *own_near, *near]
    for piece in pieces[: part + 1]:
        operands += piece
    shape = (rows, block, width)
    return pl.pallas_call(
        functools.partial(operator_kernel, shifts, rows, terms, part),
        grid=(1,),
        in_specs=[SCALARS] + [whole(array) for array in operands],
        out_specs=[pl.BlockSpec(shape, lambda i: (0, 0, 0))] * owners,
        out_shape=[jax.ShapeDtypeStruct(shape, jnp.float32)] * owners,
        scratch_shapes=[pltpu.VMEM((terms * modes, width), jnp.bfloat16)] * 4
        + [pltpu.VMEM((modes, width), jnp.float32), pltpu.VMEM((6 * terms, rows, width), jnp.float32)],
        compiler_params=params(),
        name="operator",
    )(me, *operands)


def finish_kernel(shifts, me_ref, *refs):
    owners = len(shifts) + 1
    halves = owners // 2
    mixed = refs[:owners]
    state_ref, control_ref = refs[owners : owners + 2]
    state_out, adjoint_out = refs[-2:]
    half = pl.program_id(0)
    for index, shift in enumerate([0] + shifts):
        source = lax.rem(me_ref[0] + owners - shift, owners)

        @pl.when(source == half)
        def _(index=index):
            adjoint_out[...] = jnp.swapaxes(mixed[index][...], 0, 1) - control_ref[...]

        @pl.when(source == halves + half)
        def _(index=index):
            state_out[...] = state_ref[...] + jnp.swapaxes(mixed[index][...], 0, 1)


def finish(me, mixed, state, control, outputs, part, shifts):
    modes, _, width = state.shape
    owners = len(mixed)
    rows = mixed[0].shape[0]
    block = pl.BlockSpec((modes, rows, width), lambda h: (0, h * PARTS + part, 0))
    in_specs = [SCALARS] + [whole(m) for m in mixed] + [block] * 2
    operands = [me, *mixed, state, control]
    aliases = {}
    if outputs is not None:
        aliases = {len(operands) + i: i for i in range(2)}
        in_specs += [ANYWHERE] * 2
        operands += list(outputs)
    return pl.pallas_call(
        functools.partial(finish_kernel, shifts),
        grid=(owners // 2,),
        in_specs=in_specs,
        out_specs=[block] * 2,
        out_shape=[jax.ShapeDtypeStruct(state.shape, jnp.float32)] * 2,
        input_output_aliases=aliases,
        compiler_params=params(60),
        name="finish",
    )(*operands)


def shards(state, control, adjoint, coefficient, pattern, weights):
    shape = state.shape
    modes, _, height, width = shape
    control_residual = 0.5 * control - adjoint
    state, control, adjoint = (a.reshape(modes, height, width) for a in (state, control, adjoint))
    coef = coefficient[:, 0]
    owners = lax.axis_size("mode")
    rows = height // (owners // 2) // PARTS
    planes = lax.axis_size("space")
    forward = [(i, i + 1) for i in range(planes - 1)]
    backward = [(i + 1, i) for i in range(planes - 1)]
    me = lax.axis_index("mode").astype(jnp.int32).reshape(1)
    shifts = sorted(range(1, owners), key=lambda s: min(s, owners - s))

    def move(array, shift):
        return lax.ppermute(array, "mode", [(i, (i + shift) % owners) for i in range(owners)])

    def beside(array):
        return lax.ppermute(array, "space", forward), lax.ppermute(array, "space", backward)

    matrix = coupling_matrices(pattern, weights)
    pieces, near = [], []
    for part in range(PARTS):
        if part:
            own = pack_own(me, state, adjoint, coef, owners)
            own_near = beside(own)
        packed = pack(me, state, adjoint, shifts, part, rows, owners, list(own_near) if part else [])
        arrived = [move(piece, shift) for piece, shift in zip(packed, shifts)]
        pieces.append(arrived)
        near.append(beside(jnp.concatenate([piece[:rows] for piece in arrived])))

    outputs = None
    for part in range(PARTS):
        mixed = apply_operator(me, coef, matrix, own, own_near, pieces, near[part], part, rows, shifts)
        mixed = [mixed[0]] + [move(m, shift) for m, shift in zip(mixed[1:], shifts)]
        outputs = finish(me, mixed, state, control, outputs, part, shifts)
    return outputs[0].reshape(shape), control_residual, outputs[1].reshape(shape)


def solution(mesh):
    split = P("mode", "space", None, None)
    in_specs = (split, split, split, P(None, "space", None, None), P(), P())
    return jax.shard_map(shards, mesh=mesh, in_specs=in_specs, out_specs=(split, split, split), check_vma=False)
```

```python
import functools

import jax
import jax.numpy as jnp
from jax import lax
from jax.experimental import pallas as pl
from jax.experimental.pallas import tpu as pltpu
from jax.sharding import PartitionSpec as P

TILE = 8
ANYWHERE = pl.BlockSpec(memory_space=pl.ANY)
SCALARS = pl.BlockSpec(memory_space=pltpu.SMEM)


def whole(array):
    return pl.BlockSpec(array.shape, lambda *_: (0,) * array.ndim)


def params(mib=48):
    return pltpu.CompilerParams(vmem_limit_bytes=mib * 1024 * 1024)


def matrix_kernel(pattern_ref, weights_ref, out_ref):
    terms, entries, modes = pattern_ref.shape
    rows = lax.broadcasted_iota(jnp.int32, (modes, modes), 0)
    for term in range(terms):
        flipped = jnp.zeros((modes, modes), jnp.float32)
        for entry in range(entries):
            hits = pattern_ref[term, entry : entry + 1, :] == rows
            flipped = flipped + jnp.where(hits, weights_ref[term, entry : entry + 1, :], 0.0)
        coupling = 0.5 * (flipped + flipped.T)
        high = coupling.astype(jnp.bfloat16)
        at = slice(term * modes, (term + 1) * modes)
        out_ref[:modes, at] = high
        out_ref[modes:, at] = (coupling - high.astype(jnp.float32)).astype(jnp.bfloat16)


def coupling_matrices(pattern, weights):
    terms, modes, _ = pattern.shape
    pattern, weights = jnp.swapaxes(pattern, 1, 2), jnp.swapaxes(weights, 1, 2)
    shape = (2 * modes, terms * modes)
    return pl.pallas_call(
        matrix_kernel,
        grid=(1,),
        in_specs=[whole(pattern), whole(weights)],
        out_specs=pl.BlockSpec(shape, lambda i: (0, 0)),
        out_shape=jax.ShapeDtypeStruct(shape, jnp.bfloat16),
        compiler_params=params(),
        name="coupling",
    )(pattern, weights)


def target(me_ref, shift, owners):
    block = lax.rem(me_ref[0] + shift, owners)
    return block // (owners // 2), lax.rem(block, owners // 2)


def edge_count(halves):
    return 1 if halves == 2 else 2


def tile_specs(modes, height, width, shift, owners):
    halves = owners // 2
    half_tiles = height // halves // TILE

    def spec(index):
        def place(i, me_ref):
            _, half = target(me_ref, shift, owners)
            return 0, jnp.clip(half * half_tiles + index, 0, height // TILE - 1), 0

        return pl.BlockSpec((modes, TILE, width), place)

    return [spec(-1), spec(half_tiles)]


def write_edges(out_ref, at, half, halves, before_ref, after_ref):
    before = jnp.swapaxes(before_ref[...], 0, 1)[TILE - 1]
    after = jnp.swapaxes(after_ref[...], 0, 1)[0]
    if halves == 2:
        out_ref[at] = jnp.where(half == 1, before, after)
    else:
        out_ref[at] = jnp.where(half > 0, before, 0.0)
        out_ref[at + 1] = jnp.where(half < halves - 1, after, 0.0)


def pack_kernel(shifts, owners, extras, me_ref, *refs):
    halves = owners // 2
    per_field = 3 if extras else 1
    outs = refs[-len(shifts) :]
    for index, shift in enumerate(shifts):
        field, half = target(me_ref, shift, owners)
        out_ref = outs[index]
        for which in range(2):
            mine = refs[(2 * index + which) * per_field : (2 * index + which + 1) * per_field]

            @pl.when(field == which)
            def _(mine=mine, out_ref=out_ref, half=half):
                rows = mine[0].shape[1]
                out_ref[:rows] = jnp.swapaxes(mine[0][...], 0, 1)
                if extras:
                    write_edges(out_ref, rows, half, halves, mine[1], mine[2])


def pack(me, state, adjoint, shifts, part, rows, owners, earlier):
    modes, height, width = state.shape
    extras = part == 0
    count = rows + (edge_count(owners // 2) if extras else 0)
    parts = height // (owners // 2) // rows
    in_specs, operands = [], []
    for shift in shifts:

        def place(i, me_ref, shift=shift):
            return 0, target(me_ref, shift, owners)[1] * parts + part, 0

        specs = [pl.BlockSpec((modes, rows, width), place)]
        if extras:
            specs += tile_specs(modes, height, width, shift, owners)
        for array in (state, adjoint):
            in_specs += specs
            operands += [array] * len(specs)
    return pl.pallas_call(
        functools.partial(pack_kernel, shifts, owners, extras),
        grid_spec=pltpu.PrefetchScalarGridSpec(
            num_scalar_prefetch=1,
            grid=(1,),
            in_specs=in_specs + [ANYWHERE] * len(earlier),
            out_specs=[pl.BlockSpec((count, modes, width), lambda i, me_ref: (0, 0, 0))] * len(shifts),
        ),
        out_shape=[jax.ShapeDtypeStruct((count, modes, width), jnp.float32)] * len(shifts),
        compiler_params=params(60),
        name="pack",
    )(me, *operands, *earlier)


def pack_own_kernel(owners, me_ref, *refs):
    coef_ref, out_ref = refs[6], refs[-1]
    halves = owners // 2
    field, half = target(me_ref, 0, owners)
    for which in range(2):
        mine = refs[which * 3 : which * 3 + 3]

        @pl.when(field == which)
        def _(mine=mine):
            rows = mine[0].shape[1]
            out_ref[:rows] = jnp.swapaxes(mine[0][...], 0, 1)
            write_edges(out_ref, rows, half, halves, mine[1], mine[2])

    terms = coef_ref.shape[0]
    out_ref[out_ref.shape[0] - terms :] = coef_ref[...]


def pack_own(me, state, adjoint, coef, owners, earlier):
    modes, height, width = state.shape
    halves = owners // 2
    half_rows = height // halves
    terms = coef.shape[0]
    count = half_rows + edge_count(halves) + terms

    def place(i, me_ref):
        return 0, target(me_ref, 0, owners)[1], 0

    specs = [pl.BlockSpec((modes, half_rows, width), place)]
    specs += tile_specs(modes, height, width, 0, owners)
    return pl.pallas_call(
        functools.partial(pack_own_kernel, owners),
        grid_spec=pltpu.PrefetchScalarGridSpec(
            num_scalar_prefetch=1,
            grid=(1,),
            in_specs=specs + specs + [pl.BlockSpec((terms, half_rows, width), place)] + [ANYWHERE] * len(earlier),
            out_specs=pl.BlockSpec((count, modes, width), lambda i, me_ref: (0, 0, 0)),
        ),
        out_shape=jax.ShapeDtypeStruct((count, modes, width), jnp.float32),
        compiler_params=params(60),
        name="pack_own",
    )(me, *([state] * 3 + [adjoint] * 3), coef, *earlier)


def operator_kernel(shifts, rows, terms, part, parts, me_ref, coef_ref, matrix_ref, *refs):
    owners = len(shifts) + 1
    own, own_below, own_above, below, above = refs[:5]
    pieces, before, after = (refs[5 + i * len(shifts) : 5 + (i + 1) * len(shifts)] for i in range(3))
    outs = refs[-owners - 6 : -6]
    slots, mixed, faces = ((refs[-6], refs[-5]), (refs[-4], refs[-3])), refs[-2], refs[-1]
    _, block, width = own.shape
    modes = owners * block
    halves = owners // 2
    half_rows = rows * parts
    edges = edge_count(halves)
    me = me_ref[0]
    half = lax.rem(me, halves)
    step = 16
    lanes = lax.broadcasted_iota(jnp.int32, (step, width), 1)
    last = rows - 1

    def with_sides(values, lane):
        left = jnp.where(lane == 0, 0.0, pltpu.roll(values, 1, 1))
        right = jnp.where(lane == width - 1, 0.0, pltpu.roll(values, width - 1, 1))
        return left, right

    first_row = half * half_rows + part * rows
    height = coef_ref.shape[1]
    face_lanes = lax.broadcasted_iota(jnp.int32, (rows, width), 1)
    face_rows = lax.broadcasted_iota(jnp.int32, (rows, width), 0)
    for term in range(terms):
        centre = coef_ref[term, pl.ds(pl.multiple_of(first_row, TILE), rows), :]
        row_before = coef_ref[term, pl.ds(jnp.maximum(first_row - 1, 0), 1), :]
        row_after = coef_ref[term, pl.ds(jnp.minimum(first_row + rows, height - 1), 1), :]
        row_before = jnp.where(first_row > 0, row_before, 0.0)
        row_after = jnp.where(first_row + rows < height, row_after, 0.0)
        up = jnp.where(face_rows == 0, row_before, pltpu.roll(centre, 1, 0))
        down = jnp.where(face_rows == last, row_after, pltpu.roll(centre, last, 0))
        left, right = with_sides(centre, face_lanes)
        at = half_rows + edges + term
        here = slice(part * rows, (part + 1) * rows)
        others = (own_below[at, here, :], own_above[at, here, :], up, down, left, right)
        for side, other in enumerate(others):
            faces[6 * term + side] = 0.5 * (centre + other)

    def edge(index, which, here):
        ref, at = ((before, after)[which][index - 1], 0) if index else (own, half_rows)
        if halves == 2:
            return jnp.where(half == 1 - which, ref[at, here, :], 0.0)
        return ref[at + which, here, :]

    def stencil(row, place, slot):
        high, low = slots[slot]
        for index, shift in enumerate([0] + shifts):
            source = lax.rem(me + owners - shift, owners)
            if index:
                base, near, ref, below_ref, above_ref = 0, (index - 1) * rows, pieces[index - 1], below, above
            else:
                base, near, ref, below_ref, above_ref = part * rows, part * rows, own, own_below, own_above
            for start in range(0, block, step):
                here = pl.ds(start, step)
                centre = ref[base + row, here, :]
                if place != "first":
                    up = ref[base + row - 1, here, :]
                elif part == 0:
                    up = edge(index, 0, here)
                else:
                    up = before[index - 1][0, here, :] if index else own[base - 1, here, :]
                if place != "last":
                    down = ref[base + row + 1, here, :]
                elif part == parts - 1:
                    down = edge(index, 1, here)
                else:
                    down = after[index - 1][0, here, :] if index else own[base + rows, here, :]
                left, right = with_sides(centre, lanes)
                others = (below_ref[near + row, here, :], above_ref[near + row, here, :], up, down, left, right)
                slopes = [centre - other for other in others]
                for term in range(terms):
                    total = faces[6 * term, pl.ds(row, 1), :] * slopes[0]
                    for side in range(1, 6):
                        total = total + faces[6 * term + side, pl.ds(row, 1), :] * slopes[side]
                    rounded = total.astype(jnp.bfloat16)
                    at = pl.ds(pl.multiple_of(source * block + (term * modes + start), step), step)
                    high[at, :] = rounded
                    low[at, :] = (total - rounded.astype(jnp.float32)).astype(jnp.bfloat16)

    def mix(row, slot):
        high, low = slots[slot]
        both = jnp.dot(matrix_ref[...], high[...], preferred_element_type=jnp.float32)
        rest = jnp.dot(matrix_ref[:modes, :], low[...], preferred_element_type=jnp.float32)
        mixed[...] = both[:modes] + both[modes:] + rest
        for index, shift in enumerate([0] + shifts):
            owner = lax.rem(me + shift, owners)
            outs[index][row] = mixed[pl.ds(pl.multiple_of(owner * block, block), block), :]

    def two_rows(pair, carry):
        row = 2 * pair
        stencil(row + 1, "middle", 1)
        mix(row, 0)
        stencil(row + 2, "middle", 0)
        mix(row + 1, 1)
        return carry

    stencil(0, "first", 0)
    lax.fori_loop(0, rows // 2 - 1, two_rows, 0)
    stencil(last, "last", 1)
    mix(last - 1, 0)
    mix(last, 1)


def apply_operator(me, coef, matrix, own, own_near, pieces, near, part, rows, shifts):
    _, block, width = own.shape
    owners = len(shifts) + 1
    modes = owners * block
    terms = coef.shape[0]
    parts = len(pieces)
    edges = edge_count(owners // 2)
    operands = [coef, matrix, own, *own_near, *near[part], *pieces[part]]
    in_specs = [SCALARS] + [whole(array) for array in operands]
    edge_block = pl.BlockSpec((edges, block, width), lambda i: (rows // edges, 0, 0))
    for other, row in ((part - 1, rows - 1), (part + 1, 0)):
        inside = 0 <= other < parts
        row_block = pl.BlockSpec((1, block, width), lambda i, row=row: (row, 0, 0))
        operands += pieces[other if inside else 0]
        in_specs += [row_block if inside else edge_block] * len(shifts)
    earlier = near[part + 1] if part + 1 < parts else []
    operands += earlier
    in_specs += [ANYWHERE] * len(earlier)
    shape = (rows, block, width)
    return pl.pallas_call(
        functools.partial(operator_kernel, shifts, rows, terms, part, parts),
        grid=(1,),
        in_specs=in_specs,
        out_specs=[pl.BlockSpec(shape, lambda i: (0, 0, 0))] * owners,
        out_shape=[jax.ShapeDtypeStruct(shape, jnp.float32)] * owners,
        scratch_shapes=[pltpu.VMEM((terms * modes, width), jnp.bfloat16)] * 4
        + [pltpu.VMEM((modes, width), jnp.float32), pltpu.VMEM((6 * terms, rows, width), jnp.float32)],
        compiler_params=params(),
        name="operator",
    )(me, *operands)


def finish_kernel(shifts, me_ref, *refs):
    owners = len(shifts) + 1
    halves = owners // 2
    mixed = refs[:owners]
    state_ref, control_ref = refs[owners : owners + 2]
    state_out, adjoint_out = refs[-2:]
    half = pl.program_id(0)
    for index, shift in enumerate([0] + shifts):
        source = lax.rem(me_ref[0] + owners - shift, owners)

        @pl.when(source == half)
        def _(index=index):
            adjoint_out[...] = jnp.swapaxes(mixed[index][...], 0, 1) - control_ref[...]

        @pl.when(source == halves + half)
        def _(index=index):
            state_out[...] = state_ref[...] + jnp.swapaxes(mixed[index][...], 0, 1)


def finish(me, mixed, state, control, outputs, part, shifts):
    modes, _, width = state.shape
    owners = len(mixed)
    rows = mixed[0].shape[0]
    parts = state.shape[1] // (owners // 2) // rows
    block = pl.BlockSpec((modes, rows, width), lambda h: (0, h * parts + part, 0))
    in_specs = [SCALARS] + [whole(m) for m in mixed] + [block] * 2
    operands = [me, *mixed, state, control]
    aliases = {}
    if outputs is not None:
        aliases = {len(operands) + i: i for i in range(2)}
        in_specs += [ANYWHERE] * 2
        operands += list(outputs)
    return pl.pallas_call(
        functools.partial(finish_kernel, shifts),
        grid=(owners // 2,),
        in_specs=in_specs,
        out_specs=[block] * 2,
        out_shape=[jax.ShapeDtypeStruct(state.shape, jnp.float32)] * 2,
        input_output_aliases=aliases,
        compiler_params=params(60),
        name="finish",
    )(*operands)


def shards(state, control, adjoint, coefficient, pattern, weights):
    shape = state.shape
    modes, _, height, width = shape
    control_residual = 0.5 * control - adjoint
    state, control, adjoint = (a.reshape(modes, height, width) for a in (state, control, adjoint))
    coef = coefficient[:, 0]
    owners = lax.axis_size("mode")
    rows = TILE
    parts = height // (owners // 2) // rows
    planes = lax.axis_size("space")
    forward = [(i, i + 1) for i in range(planes - 1)]
    backward = [(i + 1, i) for i in range(planes - 1)]
    me = lax.axis_index("mode").astype(jnp.int32).reshape(1)
    shifts = sorted(range(1, owners), key=lambda s: min(s, owners - s))

    def move(array, shift):
        return lax.ppermute(array, "mode", [(i, (i + shift) % owners) for i in range(owners)])

    def beside(array):
        return lax.ppermute(array, "space", forward), lax.ppermute(array, "space", backward)

    matrix = coupling_matrices(pattern, weights)
    pieces, near = [], []
    for part in range(parts):
        if part == 0:
            earlier = []
        elif part == 1:
            earlier = [own]
        else:
            earlier = near[part - 3] if part > 2 else own_near
        packed = pack(me, state, adjoint, shifts, part, rows, owners, earlier)
        if part == 0:
            own = pack_own(me, state, adjoint, coef, owners, packed)
            own_near = list(beside(own))
        arrived = [move(piece, shift) for piece, shift in zip(packed, shifts)]
        pieces.append(arrived)
        near.append(list(beside(jnp.concatenate([piece[:rows] for piece in arrived]))))

    outputs = None
    for part in range(parts):
        mixed = apply_operator(me, coef, matrix, own, own_near, pieces, near, part, rows, shifts)
        mixed = [mixed[0]] + [move(m, shift) for m, shift in zip(mixed[1:], shifts)]
        outputs = finish(me, mixed, state, control, outputs, part, shifts)
    return outputs[0].reshape(shape), control_residual, outputs[1].reshape(shape)


def solution(mesh):
    split = P("mode", "space", None, None)
    in_specs = (split, split, split, P(None, "space", None, None), P(), P())
    return jax.shard_map(shards, mesh=mesh, in_specs=in_specs, out_specs=(split, split, split), check_vma=False)
```

```python
import functools

import jax
import jax.numpy as jnp
from jax import lax
from jax.experimental import pallas as pl
from jax.experimental.pallas import tpu as pltpu
from jax.sharding import PartitionSpec as P

TILE = 8
ANYWHERE = pl.BlockSpec(memory_space=pl.ANY)
SCALARS = pl.BlockSpec(memory_space=pltpu.SMEM)


def whole(array):
    return pl.BlockSpec(array.shape, lambda *_: (0,) * array.ndim)


def params(mib=48):
    return pltpu.CompilerParams(vmem_limit_bytes=mib * 1024 * 1024)


def matrix_kernel(pattern_ref, weights_ref, out_ref):
    terms, entries, modes = pattern_ref.shape
    rows = lax.broadcasted_iota(jnp.int32, (modes, modes), 0)
    for term in range(terms):
        flipped = jnp.zeros((modes, modes), jnp.float32)
        for entry in range(entries):
            hits = pattern_ref[term, entry : entry + 1, :] == rows
            flipped = flipped + jnp.where(hits, weights_ref[term, entry : entry + 1, :], 0.0)
        coupling = 0.5 * (flipped + flipped.T)
        high = coupling.astype(jnp.bfloat16)
        at = slice(term * modes, (term + 1) * modes)
        out_ref[:modes, at] = high
        out_ref[modes:, at] = (coupling - high.astype(jnp.float32)).astype(jnp.bfloat16)


def coupling_matrices(pattern, weights):
    terms, modes, _ = pattern.shape
    pattern, weights = jnp.swapaxes(pattern, 1, 2), jnp.swapaxes(weights, 1, 2)
    shape = (2 * modes, terms * modes)
    return pl.pallas_call(
        matrix_kernel,
        grid=(1,),
        in_specs=[whole(pattern), whole(weights)],
        out_specs=pl.BlockSpec(shape, lambda i: (0, 0)),
        out_shape=jax.ShapeDtypeStruct(shape, jnp.bfloat16),
        compiler_params=params(),
        name="coupling",
    )(pattern, weights)


def edge_count(halves):
    return 1 if halves == 2 else 2


def pack_kernel(extras, halves, *refs):
    out_ref = refs[-1]
    half = pl.program_id(0)
    per_field = 3 if extras else 1
    for field in range(2):
        rows_ref, *tiles = refs[field * per_field : (field + 1) * per_field]
        rows = rows_ref.shape[1]
        out_ref[field, 0, :rows] = jnp.swapaxes(rows_ref[...], 0, 1)
        if extras:
            before = jnp.swapaxes(tiles[0][...], 0, 1)[TILE - 1]
            after = jnp.swapaxes(tiles[1][...], 0, 1)[0]
            if halves == 2:
                out_ref[field, 0, rows] = jnp.where(half == 1, before, after)
            else:
                out_ref[field, 0, rows] = jnp.where(half > 0, before, 0.0)
                out_ref[field, 0, rows + 1] = jnp.where(half < halves - 1, after, 0.0)


def pack(state, adjoint, group, rows, halves):
    modes, height, width = state.shape
    extras = group == 0
    half_tiles = height // halves // TILE
    groups = height // halves // rows
    total = rows + (edge_count(halves) if extras else 0)

    def tile(index):
        return pl.BlockSpec(
            (modes, TILE, width),
            lambda h: (0, jnp.clip(h * half_tiles + index, 0, height // TILE - 1), 0),
        )

    specs = [pl.BlockSpec((modes, rows, width), lambda h: (0, h * groups + group, 0))]
    if extras:
        specs += [tile(-1), tile(half_tiles)]
    return pl.pallas_call(
        functools.partial(pack_kernel, extras, halves),
        grid=(halves,),
        in_specs=specs * 2,
        out_specs=pl.BlockSpec((2, 1, total, modes, width), lambda h: (0, h, 0, 0, 0)),
        out_shape=jax.ShapeDtypeStruct((2, halves, total, modes, width), jnp.float32),
        compiler_params=params(60),
        name="pack",
    )(*([state] * len(specs) + [adjoint] * len(specs)))


def gather_kernel(part_ref, *refs):
    refs[-1][...] = part_ref[...]


def gather(pieces, rows, index, earlier):
    owners, _, modes, width = pieces.shape
    shape = (owners, rows, modes, width)
    return pl.pallas_call(
        gather_kernel,
        grid=(1,),
        in_specs=[pl.BlockSpec(shape, lambda i: (0, index, 0, 0))] + [ANYWHERE] * len(earlier),
        out_specs=pl.BlockSpec(shape, lambda i: (0, 0, 0, 0)),
        out_shape=jax.ShapeDtypeStruct(shape, jnp.float32),
        compiler_params=params(),
        name="gather",
    )(pieces, *earlier)


def operator_kernel(shifts, terms, part, parts, me_ref, coef_ref, coef_below, coef_above, matrix_ref, *refs):
    below, above, pieces, before, after = refs[:5]
    owners, rows, block, width = pieces.shape
    outs = refs[-owners - 6 : -6]
    slots, mixed, faces = ((refs[-6], refs[-5]), (refs[-4], refs[-3])), refs[-2], refs[-1]
    modes = owners * block
    halves = owners // 2
    me = me_ref[0]
    half = lax.rem(me, halves)
    step = 16
    lanes = lax.broadcasted_iota(jnp.int32, (step, width), 1)
    last = rows - 1

    def with_sides(values, lane):
        left = jnp.where(lane == 0, 0.0, pltpu.roll(values, 1, 1))
        right = jnp.where(lane == width - 1, 0.0, pltpu.roll(values, width - 1, 1))
        return left, right

    first_row = (half * parts + part) * rows
    height = coef_ref.shape[1]
    face_lanes = lax.broadcasted_iota(jnp.int32, (rows, width), 1)
    face_rows = lax.broadcasted_iota(jnp.int32, (rows, width), 0)
    for term in range(terms):
        centre = coef_ref[term, pl.ds(pl.multiple_of(first_row, TILE), rows), :]
        row_before = coef_ref[term, pl.ds(jnp.maximum(first_row - 1, 0), 1), :]
        row_after = coef_ref[term, pl.ds(jnp.minimum(first_row + rows, height - 1), 1), :]
        row_before = jnp.where(first_row > 0, row_before, 0.0)
        row_after = jnp.where(first_row + rows < height, row_after, 0.0)
        up = jnp.where(face_rows == 0, row_before, pltpu.roll(centre, 1, 0))
        down = jnp.where(face_rows == last, row_after, pltpu.roll(centre, last, 0))
        left, right = with_sides(centre, face_lanes)
        others = (coef_below[term], coef_above[term], up, down, left, right)
        for side, other in enumerate(others):
            faces[6 * term + side] = 0.5 * (centre + other)

    def beyond(source, which, here):
        ref = (before, after)[which]
        if part != (0, parts - 1)[which]:
            return ref[source, 0, here, :]
        if halves == 2:
            return jnp.where(half == 1 - which, ref[source, 0, here, :], 0.0)
        return ref[source, which, here, :]

    def stencil(row, slot):
        high, low = slots[slot]
        for source in range(owners):
            for start in range(0, block, step):
                here = pl.ds(start, step)
                centre = pieces[source, row, here, :]
                up = pieces[source, row - 1, here, :] if row > 0 else beyond(source, 0, here)
                down = pieces[source, row + 1, here, :] if row < last else beyond(source, 1, here)
                left, right = with_sides(centre, lanes)
                others = (below[source, row, here, :], above[source, row, here, :], up, down, left, right)
                slopes = [centre - other for other in others]
                for term in range(terms):
                    total = faces[6 * term, row : row + 1, :] * slopes[0]
                    for side in range(1, 6):
                        total = total + faces[6 * term + side, row : row + 1, :] * slopes[side]
                    rounded = total.astype(jnp.bfloat16)
                    at = pl.ds(term * modes + source * block + start, step)
                    high[at, :] = rounded
                    low[at, :] = (total - rounded.astype(jnp.float32)).astype(jnp.bfloat16)

    def mix(row, slot):
        high, low = slots[slot]
        both = jnp.dot(matrix_ref[...], high[...], preferred_element_type=jnp.float32)
        rest = jnp.dot(matrix_ref[:modes, :], low[...], preferred_element_type=jnp.float32)
        mixed[...] = both[:modes] + both[modes:] + rest
        for index, shift in enumerate([0] + shifts):
            owner = lax.rem(me + shift, owners)
            outs[index][row] = mixed[pl.ds(pl.multiple_of(owner * block, block), block), :]

    stencil(0, 0)
    for row in range(rows):
        if row < last:
            stencil(row + 1, (row + 1) % 2)
        mix(row, row % 2)


def apply_operator(me, coef, coef_near, matrix, groups, near, part, rows, shifts):
    owners, _, block, width = near[0].shape
    modes = owners * block
    terms, height, _ = coef.shape
    parts = height // (owners // 2) // rows
    edges = edge_count(owners // 2)
    group_rows = rows * parts // len(groups)

    def at(count, first):
        return pl.BlockSpec((owners, count, block, width), lambda i: (0, first // count, 0, 0))

    operands = [coef, *coef_near, matrix, *near]
    in_specs = [SCALARS, whole(coef)]
    in_specs += [pl.BlockSpec((terms, rows, width), lambda i: (0, part, 0))] * 2 + [whole(matrix), *map(whole, near)]
    for first, count in ((part * rows, rows), (part * rows - 1, 1), ((part + 1) * rows, 1)):
        if 0 <= first < parts * rows:
            operands.append(groups[first // group_rows])
            in_specs.append(at(count, first % group_rows))
        else:
            operands.append(groups[0])
            in_specs.append(at(edges, group_rows))
    shape = (rows, block, width)
    return pl.pallas_call(
        functools.partial(operator_kernel, shifts, terms, part, parts),
        grid=(1,),
        in_specs=in_specs,
        out_specs=[pl.BlockSpec(shape, lambda i: (0, 0, 0))] * owners,
        out_shape=[jax.ShapeDtypeStruct(shape, jnp.float32)] * owners,
        scratch_shapes=[pltpu.VMEM((terms * modes, width), jnp.bfloat16)] * 4
        + [pltpu.VMEM((modes, width), jnp.float32), pltpu.VMEM((6 * terms, rows, width), jnp.float32)],
        compiler_params=params(),
        name="operator",
    )(me, *operands)


def finish_kernel(shifts, me_ref, *refs):
    owners = len(shifts) + 1
    halves = owners // 2
    mixed = refs[:owners]
    state_ref, control_ref = refs[owners : owners + 2]
    state_out, adjoint_out = refs[-2:]
    half = pl.program_id(0)
    for index, shift in enumerate([0] + shifts):
        source = lax.rem(me_ref[0] + owners - shift, owners)

        @pl.when(source == half)
        def _(index=index):
            adjoint_out[...] = jnp.swapaxes(mixed[index][...], 0, 1) - control_ref[...]

        @pl.when(source == halves + half)
        def _(index=index):
            state_out[...] = state_ref[...] + jnp.swapaxes(mixed[index][...], 0, 1)


def finish(me, mixed, state, control, outputs, part, shifts):
    modes, _, width = state.shape
    owners = len(mixed)
    rows = mixed[0].shape[0]
    parts = state.shape[1] // (owners // 2) // rows
    block = pl.BlockSpec((modes, rows, width), lambda h: (0, h * parts + part, 0))
    in_specs = [SCALARS] + [whole(m) for m in mixed] + [block] * 2
    operands = [me, *mixed, state, control]
    aliases = {}
    if outputs is not None:
        aliases = {len(operands) + i: i for i in range(2)}
        in_specs += [ANYWHERE] * 2
        operands += list(outputs)
    return pl.pallas_call(
        functools.partial(finish_kernel, shifts),
        grid=(owners // 2,),
        in_specs=in_specs,
        out_specs=[block] * 2,
        out_shape=[jax.ShapeDtypeStruct(state.shape, jnp.float32)] * 2,
        input_output_aliases=aliases,
        compiler_params=params(60),
        name="finish",
    )(*operands)


def shards(state, control, adjoint, coefficient, pattern, weights):
    shape = state.shape
    modes, _, height, width = shape
    control_residual = 0.5 * control - adjoint
    state, control, adjoint = (a.reshape(modes, height, width) for a in (state, control, adjoint))
    coef = coefficient[:, 0]
    owners = lax.axis_size("mode")
    rows = TILE
    parts = height // (owners // 2) // rows
    planes = lax.axis_size("space")
    forward = [(i, i + 1) for i in range(planes - 1)]
    backward = [(i + 1, i) for i in range(planes - 1)]
    me = lax.axis_index("mode").astype(jnp.int32).reshape(1)
    shifts = sorted(range(1, owners), key=lambda s: min(s, owners - s))

    def move(array, shift):
        return lax.ppermute(array, "mode", [(i, (i + shift) % owners) for i in range(owners)])

    def beside(array):
        return lax.ppermute(array, "space", forward), lax.ppermute(array, "space", backward)

    matrix = coupling_matrices(pattern, weights)
    half_rows = parts * rows
    first = lax.rem(me[0], owners // 2) * half_rows
    coef_near = beside(lax.dynamic_slice_in_dim(coef, first, half_rows, 1))
    per_group = max(parts // 2, 1)
    groups = []
    for group in range(parts // per_group):
        packed = pack(state, adjoint, group, per_group * rows, owners // 2)
        packed = packed.reshape((owners,) + packed.shape[2:])
        groups.append(lax.all_to_all(packed, "mode", 0, 0, tiled=True))

    outputs, mixed, earlier = None, [], list(coef_near)
    for part in range(parts):
        if part >= per_group:
            earlier = earlier + [mixed[part - per_group][0]]
        body = gather(groups[part // per_group], rows, part % per_group, earlier)
        near, earlier = beside(body), [body]
        mixed.append(apply_operator(me, coef, coef_near, matrix, groups, near, part, rows, shifts))
        returned = [mixed[part][0]] + [move(m, shift) for m, shift in zip(mixed[part][1:], shifts)]
        outputs = finish(me, returned, state, control, outputs, part, shifts)
    return outputs[0].reshape(shape), control_residual, outputs[1].reshape(shape)


def solution(mesh):
    split = P("mode", "space", None, None)
    in_specs = (split, split, split, P(None, "space", None, None), P(), P())
    return jax.shard_map(shards, mesh=mesh, in_specs=in_specs, out_specs=(split, split, split), check_vma=False)
```

```python
import functools

import jax
import jax.numpy as jnp
from jax import lax
from jax.experimental import pallas as pl
from jax.experimental.pallas import tpu as pltpu
from jax.sharding import PartitionSpec as P

TILE = 8
ANYWHERE = pl.BlockSpec(memory_space=pl.ANY)
SCALARS = pl.BlockSpec(memory_space=pltpu.SMEM)


def whole(array):
    return pl.BlockSpec(array.shape, lambda *_: (0,) * array.ndim)


def cost(micros):
    return pl.CostEstimate(flops=0, bytes_accessed=int(micros * 3.5e6), transcendentals=0)


def params(mib=48):
    return pltpu.CompilerParams(vmem_limit_bytes=mib * 1024 * 1024)


def matrix_kernel(shifts, me_ref, pattern_ref, weights_ref, out_ref, coupling):
    terms, entries, modes = pattern_ref.shape
    owners = len(shifts) + 1
    block = modes // owners
    rows = lax.broadcasted_iota(jnp.int32, (modes, modes), 0)
    for term in range(terms):
        flipped = jnp.zeros((modes, modes), jnp.float32)
        for entry in range(entries):
            hits = pattern_ref[term, entry : entry + 1, :] == rows
            flipped = flipped + jnp.where(hits, weights_ref[term, entry : entry + 1, :], 0.0)
        coupling[term] = 0.5 * (flipped + flipped.T)
    for term in range(terms):
        picked = []
        for shift in [0] + shifts:
            source = lax.rem(me_ref[0] + owners - shift, owners)
            picked.append(coupling[term, pl.ds(pl.multiple_of(source * block, block), block), :])
        columns = jnp.concatenate(picked, 0).T
        high = columns.astype(jnp.bfloat16)
        at = slice(term * modes, (term + 1) * modes)
        out_ref[:modes, at] = high
        out_ref[modes:, at] = (columns - high.astype(jnp.float32)).astype(jnp.bfloat16)


def coupling_matrices(me, pattern, weights, shifts):
    terms, modes, _ = pattern.shape
    pattern, weights = jnp.swapaxes(pattern, 1, 2), jnp.swapaxes(weights, 1, 2)
    shape = (2 * modes, terms * modes)
    return pl.pallas_call(
        functools.partial(matrix_kernel, shifts),
        grid=(1,),
        in_specs=[SCALARS, whole(pattern), whole(weights)],
        out_specs=pl.BlockSpec(shape, lambda i: (0, 0)),
        out_shape=jax.ShapeDtypeStruct(shape, jnp.bfloat16),
        scratch_shapes=[pltpu.VMEM((terms, modes, modes), jnp.float32)],
        compiler_params=params(),
        cost_estimate=cost(2),
        name="coupling",
    )(me, pattern, weights)


def target(me_ref, shift, owners):
    block = lax.rem(me_ref[0] + shift, owners)
    return block // (owners // 2), lax.rem(block, owners // 2)


def edge_count(halves):
    return 1 if halves == 2 else 2


def head_rows(terms, halves):
    return -(-(terms + edge_count(halves)) // TILE) * TILE


def fetch(me_ref, state_ref, adjoint_ref, shift, owners, first, rows, target_ref, sem):
    field, half = target(me_ref, shift, owners)
    height = state_ref.shape[1]
    half_rows = height // (owners // 2)
    at = pl.ds(pl.multiple_of(jnp.clip(half * half_rows + first(half), 0, height - rows), TILE), rows)
    copies = [pltpu.make_async_copy(ref.at[:, at, :], target_ref, sem) for ref in (state_ref, adjoint_ref)]
    for which in range(2):
        pl.when(field == which)(copies[which].start)
    return copies[0].wait


def fetch_edges(me_ref, state_ref, adjoint_ref, shift, owners, target_ref, sems):
    halves = owners // 2
    half_rows = state_ref.shape[1] // halves
    if halves == 2:
        places = [lambda half: jnp.where(half == 1, -TILE, half_rows)]
    else:
        places = [lambda half: -TILE, lambda half: half_rows]
    return [
        fetch(me_ref, state_ref, adjoint_ref, shift, owners, place, TILE, target_ref.at[i], sems[i])
        for i, place in enumerate(places)
    ]


def write_edges(out_ref, at, half, halves, tiles_ref):
    tiles = [jnp.swapaxes(tiles_ref[i], 0, 1) for i in range(edge_count(halves))]
    if halves == 2:
        out_ref[at] = jnp.where(half == 1, tiles[0][TILE - 1], tiles[0][0])
    else:
        out_ref[at] = jnp.where(half > 0, tiles[0][TILE - 1], 0.0)
        out_ref[at + 1] = jnp.where(half < halves - 1, tiles[1][0], 0.0)


def pack_kernel(shifts, owners, rows, part, me_ref, state_ref, adjoint_ref, *refs):
    buffers, sems = refs[-2:]
    outs = refs[-2 - len(shifts) : -2]
    waits = [
        fetch(me_ref, state_ref, adjoint_ref, shift, owners, lambda half: part * rows, rows, buffers.at[i], sems.at[i])
        for i, shift in enumerate(shifts)
    ]
    for index, wait in enumerate(waits):
        wait()
        outs[index][...] = jnp.swapaxes(buffers[index], 0, 1)


def pack(me, state, adjoint, shifts, part, rows, owners, earlier):
    modes, _, width = state.shape
    shape = (rows, modes, width)
    return pl.pallas_call(
        functools.partial(pack_kernel, shifts, owners, rows, part),
        grid=(1,),
        in_specs=[SCALARS] + [ANYWHERE] * (2 + len(earlier)),
        out_specs=[pl.BlockSpec(shape, lambda i: (0, 0, 0))] * len(shifts),
        out_shape=[jax.ShapeDtypeStruct(shape, jnp.float32)] * len(shifts),
        scratch_shapes=[
            pltpu.VMEM((len(shifts), modes, rows, width), jnp.float32),
            pltpu.SemaphoreType.DMA((len(shifts),)),
        ],
        compiler_params=params(60),
        cost_estimate=cost(3),
        name="pack",
    )(me, state, adjoint, *earlier)


def pack_all_kernel(halves, state_ref, adjoint_ref, out_ref, buffers, sems):
    height = state_ref.shape[1]
    half_rows = height // halves
    rows = buffers.shape[3]
    copies = []
    for field, ref in enumerate((state_ref, adjoint_ref)):
        for half in range(halves):
            first = half * half_rows
            starts = [first, max(first - TILE, 0), min(first + half_rows, height - TILE)]
            if halves == 2:
                starts.pop(2 if half else 1)
            for i, start in enumerate(starts):
                at = (field * halves + half, i)
                copies.append(
                    (at, pltpu.make_async_copy(ref.at[:, pl.ds(start, rows), :], buffers.at[at], sems.at[at]))
                )
    for _, copy in copies:
        copy.start()
    for (block, i), copy in copies:
        copy.wait()
        half = block % halves
        values = jnp.swapaxes(buffers[block, i], 0, 1)
        if i == 0:
            out_ref[block, :rows] = values
        elif halves == 2:
            out_ref[block, rows] = values[TILE - 1 if half else 0]
        else:
            inside = half > 0 if i == 1 else half < halves - 1
            out_ref[block, rows + i - 1] = values[TILE - 1 if i == 1 else 0] if inside else jnp.zeros_like(values[0])


def pack_all(state, adjoint, halves):
    modes, _, width = state.shape
    edges = edge_count(halves)
    shape = (2 * halves, TILE + edges, modes, width)
    return pl.pallas_call(
        functools.partial(pack_all_kernel, halves),
        grid=(1,),
        in_specs=[ANYWHERE] * 2,
        out_specs=pl.BlockSpec(shape, lambda i: (0,) * 4),
        out_shape=jax.ShapeDtypeStruct(shape, jnp.float32),
        scratch_shapes=[
            pltpu.VMEM((2 * halves, 1 + edges, modes, TILE, width), jnp.float32),
            pltpu.SemaphoreType.DMA((2 * halves, 1 + edges)),
        ],
        compiler_params=params(60),
        cost_estimate=cost(3),
        name="pack_all",
    )(state, adjoint)


def pack_own_kernel(owners, me_ref, state_ref, adjoint_ref, coef_ref, *refs):
    out_ref, buffer, tiles, sems = refs[-4:]
    halves = owners // 2
    terms, height, _ = coef_ref.shape
    half_rows = height // halves
    head = head_rows(terms, halves)
    _, half = target(me_ref, 0, owners)
    place = (me_ref, state_ref, adjoint_ref, 0, owners)
    sem = [sems.at[i] for i in range(2 + edge_count(halves))]
    waits = [fetch(*place, lambda half: 0, half_rows, buffer, sem[0])]
    waits += fetch_edges(*place, tiles, sem[2:])
    at = pl.ds(pl.multiple_of(half * half_rows, TILE), half_rows)
    coef_copy = pltpu.make_async_copy(coef_ref.at[:, at, :], out_ref.at[:terms], sem[1])
    coef_copy.start()
    for wait in waits:
        wait()
    out_ref[head:] = jnp.swapaxes(buffer[...], 0, 1)
    write_edges(out_ref, terms, half, halves, tiles)
    coef_copy.wait()


def pack_own(me, state, adjoint, coef, owners, earlier):
    modes, height, width = state.shape
    halves = owners // 2
    half_rows = height // halves
    edges = edge_count(halves)
    terms = coef.shape[0]
    count = head_rows(terms, halves) + half_rows
    return pl.pallas_call(
        functools.partial(pack_own_kernel, owners),
        grid=(1,),
        in_specs=[SCALARS] + [ANYWHERE] * (3 + len(earlier)),
        out_specs=pl.BlockSpec((count, modes, width), lambda i: (0, 0, 0)),
        out_shape=jax.ShapeDtypeStruct((count, modes, width), jnp.float32),
        scratch_shapes=[
            pltpu.VMEM((modes, half_rows, width), jnp.float32),
            pltpu.VMEM((edges, modes, TILE, width), jnp.float32),
            pltpu.SemaphoreType.DMA((2 + edges,)),
        ],
        compiler_params=params(60),
        cost_estimate=cost(3),
        name="pack_own",
    )(me, state, adjoint, coef, *earlier)


def gather_kernel(count, *refs):
    rows = refs[0].shape[0]
    for index in range(count):
        refs[-1][index * rows : (index + 1) * rows] = refs[index][...]


def gather(pieces, rows, index, earlier):
    _, modes, width = pieces[0].shape
    shape = (len(pieces) * rows, modes, width)
    return pl.pallas_call(
        functools.partial(gather_kernel, len(pieces)),
        grid=(1,),
        in_specs=[pl.BlockSpec((rows, modes, width), lambda i: (index, 0, 0))] * len(pieces)
        + [ANYWHERE] * len(earlier),
        out_specs=pl.BlockSpec(shape, lambda i: (0, 0, 0)),
        out_shape=jax.ShapeDtypeStruct(shape, jnp.float32),
        compiler_params=params(),
        cost_estimate=cost(1),
        name="gather",
    )(*pieces, *earlier)


def operator_kernel(shifts, terms, part, parts, by_owner, me_ref, coef_ref, matrix_ref, *refs):
    owners = len(shifts) + 1
    heads, own_near, near, refs = refs[:3], refs[3:5], refs[5:7], refs[7:]
    pieces, before, after = (refs[i * owners : (i + 1) * owners] for i in range(3))
    outs = refs[-7:-6] if by_owner else refs[-owners - 6 : -6]
    slots, mixed, faces = ((refs[-6], refs[-5]), (refs[-4], refs[-3])), refs[-2], refs[-1]
    rows, block, width = pieces[0].shape
    modes = owners * block
    halves = owners // 2
    me = me_ref[0]
    half = lax.rem(me, halves)
    step = 16
    lanes = lax.broadcasted_iota(jnp.int32, (step, width), 1)
    last = rows - 1

    def with_sides(values, lane):
        left = jnp.where(lane == 0, 0.0, pltpu.roll(values, 1, 1))
        right = jnp.where(lane == width - 1, 0.0, pltpu.roll(values, width - 1, 1))
        return left, right

    first_row = (half * parts + part) * rows
    height = coef_ref.shape[1]
    face_lanes = lax.broadcasted_iota(jnp.int32, (rows, width), 1)
    face_rows = lax.broadcasted_iota(jnp.int32, (rows, width), 0)
    here = slice(part * rows, (part + 1) * rows)
    for term in range(terms):
        centre = coef_ref[term, pl.ds(pl.multiple_of(first_row, TILE), rows), :]
        row_before = coef_ref[term, pl.ds(jnp.maximum(first_row - 1, 0), 1), :]
        row_after = coef_ref[term, pl.ds(jnp.minimum(first_row + rows, height - 1), 1), :]
        row_before = jnp.where(first_row > 0, row_before, 0.0)
        row_after = jnp.where(first_row + rows < height, row_after, 0.0)
        up = jnp.where(face_rows == 0, row_before, pltpu.roll(centre, 1, 0))
        down = jnp.where(face_rows == last, row_after, pltpu.roll(centre, last, 0))
        left, right = with_sides(centre, face_lanes)
        others = (heads[1][term, here, :], heads[2][term, here, :], up, down, left, right)
        for side, other in enumerate(others):
            faces[6 * term + side] = 0.5 * (centre + other)

    def beyond(index, which, here):
        if part != (0, parts - 1)[which]:
            return (before, after)[which][index][0, here, :]
        ref, at = ((before, after)[which][index], 0) if index else (heads[0], terms)
        if halves == 2:
            return jnp.where(half == 1 - which, ref[at, here, :], 0.0)
        return ref[at + which, here, :]

    def stencil(row, slot):
        high, low = slots[slot]
        for index in range(owners):
            side_refs, side_row = (near, (index - 1) * rows + row) if index else (own_near, row)
            for start in range(0, block, step):
                here = pl.ds(start, step)
                centre = pieces[index][row, here, :]
                up = pieces[index][row - 1, here, :] if row > 0 else beyond(index, 0, here)
                down = pieces[index][row + 1, here, :] if row < last else beyond(index, 1, here)
                left, right = with_sides(centre, lanes)
                others = (side_refs[0][side_row, here, :], side_refs[1][side_row, here, :], up, down, left, right)
                slopes = [centre - other for other in others]
                for term in range(terms):
                    total = faces[6 * term, row : row + 1, :] * slopes[0]
                    for side in range(1, 6):
                        total = total + faces[6 * term + side, row : row + 1, :] * slopes[side]
                    rounded = total.astype(jnp.bfloat16)
                    at = pl.ds(term * modes + index * block + start, step)
                    high[at, :] = rounded
                    low[at, :] = (total - rounded.astype(jnp.float32)).astype(jnp.bfloat16)

    def mix(row, slot):
        high, low = slots[slot]
        both = jnp.dot(matrix_ref[...], high[...], preferred_element_type=jnp.float32)
        rest = jnp.dot(matrix_ref[:modes, :], low[...], preferred_element_type=jnp.float32)
        total = both[:modes] + both[modes:] + rest
        if by_owner:
            for owner in range(owners):
                outs[0][owner, row] = total[owner * block : (owner + 1) * block]
            return
        mixed[...] = total
        for index, shift in enumerate([0] + shifts):
            owner = lax.rem(me + shift, owners)
            outs[index][row] = mixed[pl.ds(pl.multiple_of(owner * block, block), block), :]

    stencil(0, 0)
    for row in range(rows):
        if row < last:
            stencil(row + 1, (row + 1) % 2)
        mix(row, row % 2)


def apply_operator(me, coef, matrix, own, own_near, groups, near, part, rows, shifts, by_owner):
    _, block, width = own.shape
    owners = len(shifts) + 1
    modes = owners * block
    terms, height, _ = coef.shape
    parts = height // (owners // 2) // rows
    edges = edge_count(owners // 2)
    head = head_rows(terms, owners // 2)

    def at(count, first):
        return pl.BlockSpec((count, block, width), lambda i: (first // count, 0, 0))

    def pieces_at(first, count):
        group, first_in = first // rows, first % rows
        return [own, *groups[group]], [at(count, head + first)] + [at(count, first_in)] * len(shifts)

    def edge_pieces():
        return [own, *groups[0]], [at(1, 0)] + [at(edges, rows)] * len(shifts)

    operands = [coef, matrix, own, *own_near, *own_near, *near]
    in_specs = [SCALARS, whole(coef), whole(matrix)] + [at(head, 0)] * 3
    in_specs += [at(rows, head + part * rows)] * 2 + [whole(array) for array in near]
    for arrays, specs in (
        pieces_at(part * rows, rows),
        pieces_at(part * rows - 1, 1) if part else edge_pieces(),
        pieces_at((part + 1) * rows, 1) if part < parts - 1 else edge_pieces(),
    ):
        operands += arrays
        in_specs += specs
    shape, count = ((owners, rows, block, width), 1) if by_owner else ((rows, block, width), owners)
    return pl.pallas_call(
        functools.partial(operator_kernel, shifts, terms, part, parts, by_owner),
        grid=(1,),
        in_specs=in_specs,
        out_specs=[pl.BlockSpec(shape, lambda i: (0,) * len(shape))] * count,
        out_shape=[jax.ShapeDtypeStruct(shape, jnp.float32)] * count,
        scratch_shapes=[pltpu.VMEM((terms * modes, width), jnp.bfloat16)] * 4
        + [pltpu.VMEM((modes, width), jnp.float32), pltpu.VMEM((6 * terms, rows, width), jnp.float32)],
        compiler_params=params(),
        cost_estimate=cost(6),
        name="operator",
    )(me, *operands)


def finish_kernel(shifts, by_owner, me_ref, *refs):
    owners = len(shifts) + 1
    halves = owners // 2
    mixed = refs[: 2 if by_owner else owners]
    state_ref, control_ref = refs[len(mixed) : len(mixed) + 2]
    state_out, adjoint_out = refs[-2:]
    half = pl.program_id(0)
    if by_owner:
        adjoint_out[...] = jnp.swapaxes(mixed[0][0], 0, 1) - control_ref[...]
        state_out[...] = state_ref[...] + jnp.swapaxes(mixed[1][0], 0, 1)
        return
    for index, shift in enumerate([0] + shifts):
        source = lax.rem(me_ref[0] + owners - shift, owners)

        @pl.when(source == half)
        def _(index=index):
            adjoint_out[...] = jnp.swapaxes(mixed[index][...], 0, 1) - control_ref[...]

        @pl.when(source == halves + half)
        def _(index=index):
            state_out[...] = state_ref[...] + jnp.swapaxes(mixed[index][...], 0, 1)


def finish(me, mixed, state, control, outputs, part, shifts):
    modes, _, width = state.shape
    halves = (len(shifts) + 1) // 2
    rows = mixed[0].shape[-3]
    parts = state.shape[1] // halves // rows
    block = pl.BlockSpec((modes, rows, width), lambda h: (0, h * parts + part, 0))
    by_owner = len(mixed) == 1
    if by_owner:
        sources = [
            pl.BlockSpec((1, rows, modes, width), lambda h, field=field: (field * halves + h, 0, 0, 0))
            for field in range(2)
        ]
        mixed = mixed * 2
    else:
        sources = [whole(m) for m in mixed]
    in_specs = [SCALARS] + sources + [block] * 2
    operands = [me, *mixed, state, control]
    aliases = {}
    if outputs is not None:
        aliases = {len(operands) + i: i for i in range(2)}
        in_specs += [ANYWHERE] * 2
        operands += list(outputs)
    return pl.pallas_call(
        functools.partial(finish_kernel, shifts, by_owner),
        grid=(halves,),
        in_specs=in_specs,
        out_specs=[block] * 2,
        out_shape=[jax.ShapeDtypeStruct(state.shape, jnp.float32)] * 2,
        input_output_aliases=aliases,
        compiler_params=params(60),
        cost_estimate=cost(2.5),
        name="finish",
    )(*operands)


def shards(state, control, adjoint, coefficient, pattern, weights):
    shape = state.shape
    modes, _, height, width = shape
    control_residual = 0.5 * control - adjoint
    state, control, adjoint = (a.reshape(modes, height, width) for a in (state, control, adjoint))
    coef = coefficient[:, 0]
    owners = lax.axis_size("mode")
    rows = TILE
    parts = height // (owners // 2) // rows
    planes = lax.axis_size("space")
    forward = [(i, i + 1) for i in range(planes - 1)]
    backward = [(i + 1, i) for i in range(planes - 1)]
    me = lax.axis_index("mode").astype(jnp.int32).reshape(1)
    shifts = sorted(range(1, owners), key=lambda s: min(s, owners - s))

    def move(array, shift):
        return lax.ppermute(array, "mode", [(i, (i + shift) % owners) for i in range(owners)])

    def beside(array):
        return lax.ppermute(array, "space", forward), lax.ppermute(array, "space", backward)

    matrix = coupling_matrices(me, pattern, weights, shifts)
    groups, bodies, nears, mixed = [], [], [], []

    def exchange(part):
        earlier = [own] if part == 1 else [mixed[part - 3][0]] if part > 2 else [bodies[0]]
        packed = pack(me, state, adjoint, shifts, part, rows, owners, earlier)
        groups.append([move(piece, shift) for piece, shift in zip(packed, shifts)])

    def halo(part):
        earlier = [mixed[part - 2][0]] if part > 1 else [] if part else own_near
        bodies.append(gather(groups[part], rows, 0, earlier))
        nears.append(beside(bodies[part]))

    def operate(part):
        mixed.append(
            apply_operator(me, coef, matrix, own, own_near, groups, nears[part], part, rows, shifts, part == 0)
        )

    packed = pack_all(state, adjoint, owners // 2)
    everyone = lax.all_to_all(packed, "mode", 0, 0, tiled=True)
    groups.append(
        [lax.dynamic_index_in_dim(everyone, lax.rem(me[0] + owners - s, owners), keepdims=False) for s in shifts]
    )
    own = pack_own(me, state, adjoint, coef, owners, [packed])
    own_near = list(beside(own))
    halo(0)
    exchange(1)
    halo(1)
    for part in range(parts):
        if part + 2 < parts:
            exchange(part + 2)
        operate(part)
        if part + 2 < parts:
            halo(part + 2)

    outputs = None
    for part in range(parts):
        if part == 0:
            returned = [lax.all_to_all(mixed[0][0], "mode", 0, 0, tiled=True)]
        else:
            returned = [mixed[part][0]] + [move(m, shift) for m, shift in zip(mixed[part][1:], shifts)]
        outputs = finish(me, returned, state, control, outputs, part, shifts)
    return outputs[0].reshape(shape), control_residual, outputs[1].reshape(shape)


def solution(mesh):
    split = P("mode", "space", None, None)
    in_specs = (split, split, split, P(None, "space", None, None), P(), P())
    return jax.shard_map(shards, mesh=mesh, in_specs=in_specs, out_specs=(split, split, split), check_vma=False)
```

```python
import functools

import jax
import jax.numpy as jnp
from jax import lax
from jax.experimental import pallas as pl
from jax.experimental.pallas import tpu as pltpu
from jax.sharding import PartitionSpec as P

TILE = 8
ANYWHERE = pl.BlockSpec(memory_space=pl.ANY)
SCALARS = pl.BlockSpec(memory_space=pltpu.SMEM)


def whole(array):
    return pl.BlockSpec(array.shape, lambda *_: (0,) * array.ndim)


def cost(micros):
    return pl.CostEstimate(flops=0, bytes_accessed=int(micros * 3.5e6), transcendentals=0)


def params(mib=48):
    return pltpu.CompilerParams(vmem_limit_bytes=mib * 1024 * 1024)


def matrix_kernel(shifts, me_ref, pattern_ref, weights_ref, out_ref, coupling):
    terms, entries, modes = pattern_ref.shape
    owners = len(shifts) + 1
    block = modes // owners
    rows = lax.broadcasted_iota(jnp.int32, (modes, modes), 0)
    for term in range(terms):
        flipped = jnp.zeros((modes, modes), jnp.float32)
        for entry in range(entries):
            hits = pattern_ref[term, entry : entry + 1, :] == rows
            flipped = flipped + jnp.where(hits, weights_ref[term, entry : entry + 1, :], 0.0)
        coupling[term] = 0.5 * (flipped + flipped.T)
    for term in range(terms):
        picked = []
        for shift in [0] + shifts:
            source = lax.rem(me_ref[0] + owners - shift, owners)
            picked.append(coupling[term, pl.ds(pl.multiple_of(source * block, block), block), :])
        columns = jnp.concatenate(picked, 0).T
        high = columns.astype(jnp.bfloat16)
        at = slice(term * modes, (term + 1) * modes)
        out_ref[:modes, at] = high
        out_ref[modes:, at] = (columns - high.astype(jnp.float32)).astype(jnp.bfloat16)


def coupling_matrices(me, pattern, weights, shifts):
    terms, modes, _ = pattern.shape
    pattern, weights = jnp.swapaxes(pattern, 1, 2), jnp.swapaxes(weights, 1, 2)
    shape = (2 * modes, terms * modes)
    return pl.pallas_call(
        functools.partial(matrix_kernel, shifts),
        grid=(1,),
        in_specs=[SCALARS, whole(pattern), whole(weights)],
        out_specs=pl.BlockSpec(shape, lambda i: (0, 0)),
        out_shape=jax.ShapeDtypeStruct(shape, jnp.bfloat16),
        scratch_shapes=[pltpu.VMEM((terms, modes, modes), jnp.float32)],
        compiler_params=params(),
        cost_estimate=cost(2),
        name="coupling",
    )(me, pattern, weights)


def target(me_ref, shift, owners):
    block = lax.rem(me_ref[0] + shift, owners)
    return block // (owners // 2), lax.rem(block, owners // 2)


def edge_count(halves):
    return 1 if halves == 2 else 2


def head_rows(terms, halves):
    return -(-(terms + edge_count(halves)) // TILE) * TILE


def fetch(me_ref, state_ref, adjoint_ref, shift, owners, first, rows, target_ref, sem):
    field, half = target(me_ref, shift, owners)
    height = state_ref.shape[1]
    half_rows = height // (owners // 2)
    at = pl.ds(pl.multiple_of(jnp.clip(half * half_rows + first(half), 0, height - rows), TILE), rows)
    copies = [pltpu.make_async_copy(ref.at[:, at, :], target_ref, sem) for ref in (state_ref, adjoint_ref)]
    for which in range(2):
        pl.when(field == which)(copies[which].start)
    return copies[0].wait


def fetch_edges(me_ref, state_ref, adjoint_ref, shift, owners, target_ref, sems):
    halves = owners // 2
    half_rows = state_ref.shape[1] // halves
    if halves == 2:
        places = [lambda half: jnp.where(half == 1, -TILE, half_rows)]
    else:
        places = [lambda half: -TILE, lambda half: half_rows]
    return [
        fetch(me_ref, state_ref, adjoint_ref, shift, owners, place, TILE, target_ref.at[i], sems[i])
        for i, place in enumerate(places)
    ]


def write_edges(out_ref, at, half, halves, tiles_ref):
    tiles = [jnp.swapaxes(tiles_ref[i], 0, 1) for i in range(edge_count(halves))]
    if halves == 2:
        out_ref[at] = jnp.where(half == 1, tiles[0][TILE - 1], tiles[0][0])
    else:
        out_ref[at] = jnp.where(half > 0, tiles[0][TILE - 1], 0.0)
        out_ref[at + 1] = jnp.where(half < halves - 1, tiles[1][0], 0.0)


def pack_kernel(shifts, owners, first, rows, me_ref, state_ref, adjoint_ref, *refs):
    buffers, sems = refs[-2:]
    outs = refs[-2 - len(shifts) : -2]
    waits = [
        fetch(me_ref, state_ref, adjoint_ref, shift, owners, lambda half: first, rows, buffers.at[i], sems.at[i])
        for i, shift in enumerate(shifts)
    ]
    for index, wait in enumerate(waits):
        wait()
        outs[index][...] = jnp.swapaxes(buffers[index], 0, 1)


def pack(me, state, adjoint, shifts, first, rows, owners, earlier):
    modes, _, width = state.shape
    shape = (rows, modes, width)
    return pl.pallas_call(
        functools.partial(pack_kernel, shifts, owners, first, rows),
        grid=(1,),
        in_specs=[SCALARS] + [ANYWHERE] * (2 + len(earlier)),
        out_specs=[pl.BlockSpec(shape, lambda i: (0, 0, 0))] * len(shifts),
        out_shape=[jax.ShapeDtypeStruct(shape, jnp.float32)] * len(shifts),
        scratch_shapes=[
            pltpu.VMEM((len(shifts), modes, rows, width), jnp.float32),
            pltpu.SemaphoreType.DMA((len(shifts),)),
        ],
        compiler_params=params(60),
        cost_estimate=cost(3),
        name="pack",
    )(me, state, adjoint, *earlier)


def pack_all_kernel(halves, part, state_ref, adjoint_ref, *refs):
    out_ref, buffers, sems = refs[-3:]
    height = state_ref.shape[1]
    half_rows = height // halves
    rows = buffers.shape[3]
    copies = []
    for field, ref in enumerate((state_ref, adjoint_ref)):
        for half in range(halves):
            first = half * half_rows
            starts = [first + part * rows, max(first - TILE, 0), min(first + half_rows, height - TILE)]
            if part:
                del starts[1:]
            elif halves == 2:
                starts.pop(2 if half else 1)
            for i, start in enumerate(starts):
                at = (field * halves + half, i)
                copies.append(
                    (at, pltpu.make_async_copy(ref.at[:, pl.ds(start, rows), :], buffers.at[at], sems.at[at]))
                )
    for _, copy in copies:
        copy.start()
    for (block, i), copy in copies:
        copy.wait()
        half = block % halves
        values = jnp.swapaxes(buffers[block, i], 0, 1)
        if i == 0:
            out_ref[block, :rows] = values
        elif halves == 2:
            out_ref[block, rows] = values[TILE - 1 if half else 0]
        else:
            inside = half > 0 if i == 1 else half < halves - 1
            out_ref[block, rows + i - 1] = values[TILE - 1 if i == 1 else 0] if inside else jnp.zeros_like(values[0])


def pack_all(state, adjoint, halves, part, earlier):
    modes, _, width = state.shape
    edges = 0 if part else edge_count(halves)
    shape = (2 * halves, TILE + edges, modes, width)
    return pl.pallas_call(
        functools.partial(pack_all_kernel, halves, part),
        grid=(1,),
        in_specs=[ANYWHERE] * (2 + len(earlier)),
        out_specs=pl.BlockSpec(shape, lambda i: (0,) * 4),
        out_shape=jax.ShapeDtypeStruct(shape, jnp.float32),
        scratch_shapes=[
            pltpu.VMEM((2 * halves, 1 + edges, modes, TILE, width), jnp.float32),
            pltpu.SemaphoreType.DMA((2 * halves, 1 + edges)),
        ],
        compiler_params=params(60),
        cost_estimate=cost(3),
        name="pack_all",
    )(state, adjoint, *earlier)


def pack_own_kernel(owners, me_ref, state_ref, adjoint_ref, coef_ref, *refs):
    out_ref, buffer, tiles, sems = refs[-4:]
    halves = owners // 2
    terms, height, _ = coef_ref.shape
    half_rows = height // halves
    head = head_rows(terms, halves)
    _, half = target(me_ref, 0, owners)
    place = (me_ref, state_ref, adjoint_ref, 0, owners)
    sem = [sems.at[i] for i in range(2 + edge_count(halves))]
    waits = [fetch(*place, lambda half: 0, half_rows, buffer, sem[0])]
    waits += fetch_edges(*place, tiles, sem[2:])
    at = pl.ds(pl.multiple_of(half * half_rows, TILE), half_rows)
    coef_copy = pltpu.make_async_copy(coef_ref.at[:, at, :], out_ref.at[:terms], sem[1])
    coef_copy.start()
    for wait in waits:
        wait()
    out_ref[head:] = jnp.swapaxes(buffer[...], 0, 1)
    write_edges(out_ref, terms, half, halves, tiles)
    coef_copy.wait()


def pack_own(me, state, adjoint, coef, owners, earlier):
    modes, height, width = state.shape
    halves = owners // 2
    half_rows = height // halves
    edges = edge_count(halves)
    terms = coef.shape[0]
    count = head_rows(terms, halves) + half_rows
    return pl.pallas_call(
        functools.partial(pack_own_kernel, owners),
        grid=(1,),
        in_specs=[SCALARS] + [ANYWHERE] * (3 + len(earlier)),
        out_specs=pl.BlockSpec((count, modes, width), lambda i: (0, 0, 0)),
        out_shape=jax.ShapeDtypeStruct((count, modes, width), jnp.float32),
        scratch_shapes=[
            pltpu.VMEM((modes, half_rows, width), jnp.float32),
            pltpu.VMEM((edges, modes, TILE, width), jnp.float32),
            pltpu.SemaphoreType.DMA((2 + edges,)),
        ],
        compiler_params=params(60),
        cost_estimate=cost(3),
        name="pack_own",
    )(me, state, adjoint, coef, *earlier)


def gather_kernel(count, *refs):
    rows = refs[0].shape[0]
    for index in range(count):
        refs[-1][index * rows : (index + 1) * rows] = refs[index][...]


def gather(pieces, rows, index, earlier):
    _, modes, width = pieces[0].shape
    shape = (len(pieces) * rows, modes, width)
    return pl.pallas_call(
        functools.partial(gather_kernel, len(pieces)),
        grid=(1,),
        in_specs=[pl.BlockSpec((rows, modes, width), lambda i: (index, 0, 0))] * len(pieces)
        + [ANYWHERE] * len(earlier),
        out_specs=pl.BlockSpec(shape, lambda i: (0, 0, 0)),
        out_shape=jax.ShapeDtypeStruct(shape, jnp.float32),
        compiler_params=params(),
        cost_estimate=cost(1),
        name="gather",
    )(*pieces, *earlier)


def operator_kernel(shifts, terms, part, parts, by_owner, me_ref, coef_ref, matrix_ref, *refs):
    owners = len(shifts) + 1
    heads, own_near, near, refs = refs[:3], refs[3:5], refs[5:7], refs[7:]
    pieces, before, after = (refs[i * owners : (i + 1) * owners] for i in range(3))
    outs = refs[-7:-6] if by_owner else refs[-owners - 6 : -6]
    slots, mixed, faces = ((refs[-6], refs[-5]), (refs[-4], refs[-3])), refs[-2], refs[-1]
    rows, block, width = pieces[0].shape
    modes = owners * block
    halves = owners // 2
    me = me_ref[0]
    half = lax.rem(me, halves)
    step = 16
    lanes = lax.broadcasted_iota(jnp.int32, (step, width), 1)
    last = rows - 1

    def with_sides(values, lane):
        left = jnp.where(lane == 0, 0.0, pltpu.roll(values, 1, 1))
        right = jnp.where(lane == width - 1, 0.0, pltpu.roll(values, width - 1, 1))
        return left, right

    first_row = (half * parts + part) * rows
    height = coef_ref.shape[1]
    face_lanes = lax.broadcasted_iota(jnp.int32, (rows, width), 1)
    face_rows = lax.broadcasted_iota(jnp.int32, (rows, width), 0)
    here = slice(part * rows, (part + 1) * rows)
    for term in range(terms):
        centre = coef_ref[term, pl.ds(pl.multiple_of(first_row, TILE), rows), :]
        row_before = coef_ref[term, pl.ds(jnp.maximum(first_row - 1, 0), 1), :]
        row_after = coef_ref[term, pl.ds(jnp.minimum(first_row + rows, height - 1), 1), :]
        row_before = jnp.where(first_row > 0, row_before, 0.0)
        row_after = jnp.where(first_row + rows < height, row_after, 0.0)
        up = jnp.where(face_rows == 0, row_before, pltpu.roll(centre, 1, 0))
        down = jnp.where(face_rows == last, row_after, pltpu.roll(centre, last, 0))
        left, right = with_sides(centre, face_lanes)
        others = (heads[1][term, here, :], heads[2][term, here, :], up, down, left, right)
        for side, other in enumerate(others):
            faces[6 * term + side] = 0.5 * (centre + other)

    def beyond(index, which, here):
        if part != (0, parts - 1)[which]:
            return (before, after)[which][index][0, here, :]
        ref, at = ((before, after)[which][index], 0) if index else (heads[0], terms)
        if halves == 2:
            return jnp.where(half == 1 - which, ref[at, here, :], 0.0)
        return ref[at + which, here, :]

    def stencil(row, slot):
        high, low = slots[slot]
        for index in range(owners):
            side_refs, side_row = (near, (index - 1) * rows + row) if index else (own_near, row)
            for start in range(0, block, step):
                here = pl.ds(start, step)
                centre = pieces[index][row, here, :]
                up = pieces[index][row - 1, here, :] if row > 0 else beyond(index, 0, here)
                down = pieces[index][row + 1, here, :] if row < last else beyond(index, 1, here)
                left, right = with_sides(centre, lanes)
                others = (side_refs[0][side_row, here, :], side_refs[1][side_row, here, :], up, down, left, right)
                slopes = [centre - other for other in others]
                for term in range(terms):
                    total = faces[6 * term, row : row + 1, :] * slopes[0]
                    for side in range(1, 6):
                        total = total + faces[6 * term + side, row : row + 1, :] * slopes[side]
                    rounded = total.astype(jnp.bfloat16)
                    at = pl.ds(term * modes + index * block + start, step)
                    high[at, :] = rounded
                    low[at, :] = (total - rounded.astype(jnp.float32)).astype(jnp.bfloat16)

    def mix(row, slot):
        high, low = slots[slot]
        both = jnp.dot(matrix_ref[...], high[...], preferred_element_type=jnp.float32)
        rest = jnp.dot(matrix_ref[:modes, :], low[...], preferred_element_type=jnp.float32)
        total = both[:modes] + both[modes:] + rest
        if by_owner:
            for owner in range(owners):
                outs[0][owner, row] = total[owner * block : (owner + 1) * block]
            return
        mixed[...] = total
        for index, shift in enumerate([0] + shifts):
            owner = lax.rem(me + shift, owners)
            outs[index][row] = mixed[pl.ds(pl.multiple_of(owner * block, block), block), :]

    stencil(0, 0)
    for row in range(rows):
        if row < last:
            stencil(row + 1, (row + 1) % 2)
        mix(row, row % 2)


def apply_operator(me, coef, matrix, own, own_near, groups, group_of, near, part, rows, shifts, by_owner):
    _, block, width = own.shape
    owners = len(shifts) + 1
    modes = owners * block
    terms, height, _ = coef.shape
    parts = height // (owners // 2) // rows
    edges = edge_count(owners // 2)
    head = head_rows(terms, owners // 2)

    def at(count, first):
        return pl.BlockSpec((count, block, width), lambda i: (first // count, 0, 0))

    def pieces_at(first, count):
        group, skipped = group_of[first // rows]
        first_in = first - skipped * rows
        return [own, *groups[group]], [at(count, head + first)] + [at(count, first_in)] * len(shifts)

    def edge_pieces():
        return [own, *groups[0]], [at(1, 0)] + [at(edges, rows)] * len(shifts)

    operands = [coef, matrix, own, *own_near, *own_near, *near]
    in_specs = [SCALARS, whole(coef), whole(matrix)] + [at(head, 0)] * 3
    in_specs += [at(rows, head + part * rows)] * 2 + [whole(array) for array in near]
    for arrays, specs in (
        pieces_at(part * rows, rows),
        pieces_at(part * rows - 1, 1) if part else edge_pieces(),
        pieces_at((part + 1) * rows, 1) if part < parts - 1 else edge_pieces(),
    ):
        operands += arrays
        in_specs += specs
    shape, count = ((owners, rows, block, width), 1) if by_owner else ((rows, block, width), owners)
    return pl.pallas_call(
        functools.partial(operator_kernel, shifts, terms, part, parts, by_owner),
        grid=(1,),
        in_specs=in_specs,
        out_specs=[pl.BlockSpec(shape, lambda i: (0,) * len(shape))] * count,
        out_shape=[jax.ShapeDtypeStruct(shape, jnp.float32)] * count,
        scratch_shapes=[pltpu.VMEM((terms * modes, width), jnp.bfloat16)] * 4
        + [pltpu.VMEM((modes, width), jnp.float32), pltpu.VMEM((6 * terms, rows, width), jnp.float32)],
        compiler_params=params(),
        cost_estimate=cost(6),
        name="operator",
    )(me, *operands)


def finish_kernel(shifts, by_owner, me_ref, *refs):
    owners = len(shifts) + 1
    halves = owners // 2
    mixed = refs[: 2 if by_owner else owners]
    state_ref, control_ref = refs[len(mixed) : len(mixed) + 2]
    state_out, adjoint_out = refs[-2:]
    half = pl.program_id(0)
    if by_owner:
        adjoint_out[...] = jnp.swapaxes(mixed[0][0], 0, 1) - control_ref[...]
        state_out[...] = state_ref[...] + jnp.swapaxes(mixed[1][0], 0, 1)
        return
    for index, shift in enumerate([0] + shifts):
        source = lax.rem(me_ref[0] + owners - shift, owners)

        @pl.when(source == half)
        def _(index=index):
            adjoint_out[...] = jnp.swapaxes(mixed[index][...], 0, 1) - control_ref[...]

        @pl.when(source == halves + half)
        def _(index=index):
            state_out[...] = state_ref[...] + jnp.swapaxes(mixed[index][...], 0, 1)


def finish(me, mixed, state, control, outputs, part, shifts):
    modes, _, width = state.shape
    halves = (len(shifts) + 1) // 2
    rows = mixed[0].shape[-3]
    parts = state.shape[1] // halves // rows
    block = pl.BlockSpec((modes, rows, width), lambda h: (0, h * parts + part, 0))
    by_owner = len(mixed) == 1
    if by_owner:
        sources = [
            pl.BlockSpec((1, rows, modes, width), lambda h, field=field: (field * halves + h, 0, 0, 0))
            for field in range(2)
        ]
        mixed = mixed * 2
    else:
        sources = [whole(m) for m in mixed]
    in_specs = [SCALARS] + sources + [block] * 2
    operands = [me, *mixed, state, control]
    aliases = {}
    if outputs is not None:
        aliases = {len(operands) + i: i for i in range(2)}
        in_specs += [ANYWHERE] * 2
        operands += list(outputs)
    return pl.pallas_call(
        functools.partial(finish_kernel, shifts, by_owner),
        grid=(halves,),
        in_specs=in_specs,
        out_specs=[block] * 2,
        out_shape=[jax.ShapeDtypeStruct(state.shape, jnp.float32)] * 2,
        input_output_aliases=aliases,
        compiler_params=params(60),
        cost_estimate=cost(2.5),
        name="finish",
    )(*operands)


def shards(state, control, adjoint, coefficient, pattern, weights):
    shape = state.shape
    modes, _, height, width = shape
    control_residual = 0.5 * control - adjoint
    state, control, adjoint = (a.reshape(modes, height, width) for a in (state, control, adjoint))
    coef = coefficient[:, 0]
    owners = lax.axis_size("mode")
    rows = TILE
    parts = height // (owners // 2) // rows
    planes = lax.axis_size("space")
    forward = [(i, i + 1) for i in range(planes - 1)]
    backward = [(i + 1, i) for i in range(planes - 1)]
    me = lax.axis_index("mode").astype(jnp.int32).reshape(1)
    shifts = sorted(range(1, owners), key=lambda s: min(s, owners - s))

    def move(array, shift):
        return lax.ppermute(array, "mode", [(i, (i + shift) % owners) for i in range(owners)])

    def beside(array):
        return lax.ppermute(array, "space", forward), lax.ppermute(array, "space", backward)

    matrix = coupling_matrices(me, pattern, weights, shifts)
    halves = owners // 2
    groups, bodies, nears, mixed = [], [], [], []
    if parts > 2:
        members = [[0], list(range(1, parts - 1)), [parts - 1]]
    else:
        members = [[part] for part in range(parts)]
    group_of = {part: (index, group[0]) for index, group in enumerate(members) for part in group}

    def exchange_all(part, earlier):
        packed = pack_all(state, adjoint, halves, part, earlier)
        arrived = lax.all_to_all(packed, "mode", 0, 0, tiled=True)
        groups.append(
            [lax.dynamic_index_in_dim(arrived, lax.rem(me[0] + owners - s, owners), keepdims=False) for s in shifts]
        )
        return packed

    def exchange(group, earlier):
        packed = pack(me, state, adjoint, shifts, group[0] * rows, len(group) * rows, owners, earlier)
        groups.append([move(piece, shift) for piece, shift in zip(packed, shifts)])

    def halo(part, earlier):
        group, skipped = group_of[part]
        bodies.append(gather(groups[group], rows, part - skipped, earlier))
        nears.append(beside(bodies[part]))

    packed = exchange_all(0, [])
    own = pack_own(me, state, adjoint, coef, owners, [packed])
    own_near = list(beside(own))
    halo(0, own_near)
    for group in members[1:]:
        if group[0] > 1:
            exchange_all(group[0], [bodies[0]])
        else:
            exchange(group, [own])
    for part in range(parts):
        if part:
            halo(part, [mixed[part - 2][0]] if part > 1 else list(nears[0]))
        mixed.append(
            apply_operator(
                me, coef, matrix, own, own_near, groups, group_of, nears[part], part, rows, shifts, part == 0
            )
        )

    outputs = None
    for part in range(parts):
        if part == 0:
            returned = [lax.all_to_all(mixed[0][0], "mode", 0, 0, tiled=True)]
        else:
            returned = [mixed[part][0]] + [move(m, shift) for m, shift in zip(mixed[part][1:], shifts)]
        outputs = finish(me, returned, state, control, outputs, part, shifts)
    return outputs[0].reshape(shape), control_residual, outputs[1].reshape(shape)


def solution(mesh):
    split = P("mode", "space", None, None)
    in_specs = (split, split, split, P(None, "space", None, None), P(), P())
    return jax.shard_map(shards, mesh=mesh, in_specs=in_specs, out_specs=(split, split, split), check_vma=False)
```

```python
import functools

import jax
import jax.numpy as jnp
from jax import lax
from jax.experimental import pallas as pl
from jax.experimental.pallas import tpu as pltpu
from jax.sharding import PartitionSpec as P

TILE = 8
ANYWHERE = pl.BlockSpec(memory_space=pl.ANY)
SCALARS = pl.BlockSpec(memory_space=pltpu.SMEM)


def whole(array):
    return pl.BlockSpec(array.shape, lambda *_: (0,) * array.ndim)


def cost(micros):
    return pl.CostEstimate(flops=0, bytes_accessed=int(micros * 3.5e6), transcendentals=0)


def params(mib=48):
    return pltpu.CompilerParams(vmem_limit_bytes=mib * 1024 * 1024)


def matrix_kernel(shifts, me_ref, pattern_ref, weights_ref, out_ref, coupling):
    terms, entries, modes = pattern_ref.shape
    owners = len(shifts) + 1
    block = modes // owners
    rows = lax.broadcasted_iota(jnp.int32, (modes, modes), 0)
    for term in range(terms):
        flipped = jnp.zeros((modes, modes), jnp.float32)
        for entry in range(entries):
            hits = pattern_ref[term, entry : entry + 1, :] == rows
            flipped = flipped + jnp.where(hits, weights_ref[term, entry : entry + 1, :], 0.0)
        coupling[term] = 0.5 * (flipped + flipped.T)
    for term in range(terms):
        picked = []
        for shift in [0] + shifts:
            source = lax.rem(me_ref[0] + owners - shift, owners)
            picked.append(coupling[term, pl.ds(pl.multiple_of(source * block, block), block), :])
        columns = jnp.concatenate(picked, 0).T
        high = columns.astype(jnp.bfloat16)
        at = slice(term * modes, (term + 1) * modes)
        out_ref[:modes, at] = high
        out_ref[modes:, at] = (columns - high.astype(jnp.float32)).astype(jnp.bfloat16)


def coupling_matrices(me, pattern, weights, shifts):
    terms, modes, _ = pattern.shape
    pattern, weights = jnp.swapaxes(pattern, 1, 2), jnp.swapaxes(weights, 1, 2)
    shape = (2 * modes, terms * modes)
    return pl.pallas_call(
        functools.partial(matrix_kernel, shifts),
        grid=(1,),
        in_specs=[SCALARS, whole(pattern), whole(weights)],
        out_specs=pl.BlockSpec(shape, lambda i: (0, 0)),
        out_shape=jax.ShapeDtypeStruct(shape, jnp.bfloat16),
        scratch_shapes=[pltpu.VMEM((terms, modes, modes), jnp.float32)],
        compiler_params=params(),
        cost_estimate=cost(2),
        name="coupling",
    )(me, pattern, weights)


def target(me_ref, shift, owners):
    block = lax.rem(me_ref[0] + shift, owners)
    return block // (owners // 2), lax.rem(block, owners // 2)


def edge_count(halves):
    return 1 if halves == 2 else 2


def head_rows(terms, halves):
    return -(-(terms + edge_count(halves)) // TILE) * TILE


def fetch(me_ref, state_ref, adjoint_ref, shift, owners, first, rows, target_ref, sem):
    field, half = target(me_ref, shift, owners)
    height = state_ref.shape[1]
    half_rows = height // (owners // 2)
    at = pl.ds(pl.multiple_of(jnp.clip(half * half_rows + first(half), 0, height - rows), TILE), rows)
    copies = [pltpu.make_async_copy(ref.at[:, at, :], target_ref, sem) for ref in (state_ref, adjoint_ref)]
    for which in range(2):
        pl.when(field == which)(copies[which].start)
    return copies[0].wait


def fetch_edges(me_ref, state_ref, adjoint_ref, shift, owners, target_ref, sems):
    halves = owners // 2
    half_rows = state_ref.shape[1] // halves
    if halves == 2:
        places = [lambda half: jnp.where(half == 1, -TILE, half_rows)]
    else:
        places = [lambda half: -TILE, lambda half: half_rows]
    return [
        fetch(me_ref, state_ref, adjoint_ref, shift, owners, place, TILE, target_ref.at[i], sems[i])
        for i, place in enumerate(places)
    ]


def write_edges(out_ref, at, half, halves, tiles_ref):
    tiles = [jnp.swapaxes(tiles_ref[i], 0, 1) for i in range(edge_count(halves))]
    if halves == 2:
        out_ref[at] = jnp.where(half == 1, tiles[0][TILE - 1], tiles[0][0])
    else:
        out_ref[at] = jnp.where(half > 0, tiles[0][TILE - 1], 0.0)
        out_ref[at + 1] = jnp.where(half < halves - 1, tiles[1][0], 0.0)


def pack_kernel(shifts, owners, first, rows, me_ref, state_ref, adjoint_ref, *refs):
    buffers, sems = refs[-2:]
    outs = refs[-2 - len(shifts) : -2]
    waits = [
        fetch(me_ref, state_ref, adjoint_ref, shift, owners, lambda half: first, rows, buffers.at[i], sems.at[i])
        for i, shift in enumerate(shifts)
    ]
    for index, wait in enumerate(waits):
        wait()
        outs[index][...] = jnp.swapaxes(buffers[index], 0, 1)


def pack(me, state, adjoint, shifts, first, rows, owners, earlier):
    modes, _, width = state.shape
    shape = (rows, modes, width)
    return pl.pallas_call(
        functools.partial(pack_kernel, shifts, owners, first, rows),
        grid=(1,),
        in_specs=[SCALARS] + [ANYWHERE] * (2 + len(earlier)),
        out_specs=[pl.BlockSpec(shape, lambda i: (0, 0, 0))] * len(shifts),
        out_shape=[jax.ShapeDtypeStruct(shape, jnp.float32)] * len(shifts),
        scratch_shapes=[
            pltpu.VMEM((len(shifts), modes, rows, width), jnp.float32),
            pltpu.SemaphoreType.DMA((len(shifts),)),
        ],
        compiler_params=params(60),
        cost_estimate=cost(3),
        name="pack",
    )(me, state, adjoint, *earlier)


def pack_all_kernel(halves, part, state_ref, adjoint_ref, *refs):
    out_ref, buffers, sems = refs[-3:]
    height = state_ref.shape[1]
    half_rows = height // halves
    rows = buffers.shape[3]
    copies = []
    for field, ref in enumerate((state_ref, adjoint_ref)):
        for half in range(halves):
            first = half * half_rows
            starts = [first + part * rows, max(first - TILE, 0), min(first + half_rows, height - TILE)]
            if part:
                del starts[1:]
            elif halves == 2:
                starts.pop(2 if half else 1)
            for i, start in enumerate(starts):
                at = (field * halves + half, i)
                copies.append(
                    (at, pltpu.make_async_copy(ref.at[:, pl.ds(start, rows), :], buffers.at[at], sems.at[at]))
                )
    for _, copy in copies:
        copy.start()
    for (block, i), copy in copies:
        copy.wait()
        half = block % halves
        values = jnp.swapaxes(buffers[block, i], 0, 1)
        if i == 0:
            out_ref[block, :rows] = values
        elif halves == 2:
            out_ref[block, rows] = values[TILE - 1 if half else 0]
        else:
            inside = half > 0 if i == 1 else half < halves - 1
            out_ref[block, rows + i - 1] = values[TILE - 1 if i == 1 else 0] if inside else jnp.zeros_like(values[0])


def pack_all(state, adjoint, halves, part, earlier):
    modes, _, width = state.shape
    edges = 0 if part else edge_count(halves)
    shape = (2 * halves, TILE + edges, modes, width)
    return pl.pallas_call(
        functools.partial(pack_all_kernel, halves, part),
        grid=(1,),
        in_specs=[ANYWHERE] * (2 + len(earlier)),
        out_specs=pl.BlockSpec(shape, lambda i: (0,) * 4),
        out_shape=jax.ShapeDtypeStruct(shape, jnp.float32),
        scratch_shapes=[
            pltpu.VMEM((2 * halves, 1 + edges, modes, TILE, width), jnp.float32),
            pltpu.SemaphoreType.DMA((2 * halves, 1 + edges)),
        ],
        compiler_params=params(60),
        cost_estimate=cost(3),
        name="pack_all",
    )(state, adjoint, *earlier)


def pack_own_kernel(owners, me_ref, state_ref, adjoint_ref, coef_ref, *refs):
    out_ref, buffer, tiles, sems = refs[-4:]
    halves = owners // 2
    terms, height, _ = coef_ref.shape
    half_rows = height // halves
    head = head_rows(terms, halves)
    _, half = target(me_ref, 0, owners)
    place = (me_ref, state_ref, adjoint_ref, 0, owners)
    sem = [sems.at[i] for i in range(2 + edge_count(halves))]
    waits = [fetch(*place, lambda half: 0, half_rows, buffer, sem[0])]
    waits += fetch_edges(*place, tiles, sem[2:])
    at = pl.ds(pl.multiple_of(half * half_rows, TILE), half_rows)
    coef_copy = pltpu.make_async_copy(coef_ref.at[:, at, :], out_ref.at[:terms], sem[1])
    coef_copy.start()
    for wait in waits:
        wait()
    out_ref[head:] = jnp.swapaxes(buffer[...], 0, 1)
    write_edges(out_ref, terms, half, halves, tiles)
    coef_copy.wait()


def pack_own(me, state, adjoint, coef, owners, earlier):
    modes, height, width = state.shape
    halves = owners // 2
    half_rows = height // halves
    edges = edge_count(halves)
    terms = coef.shape[0]
    count = head_rows(terms, halves) + half_rows
    return pl.pallas_call(
        functools.partial(pack_own_kernel, owners),
        grid=(1,),
        in_specs=[SCALARS] + [ANYWHERE] * (3 + len(earlier)),
        out_specs=pl.BlockSpec((count, modes, width), lambda i: (0, 0, 0)),
        out_shape=jax.ShapeDtypeStruct((count, modes, width), jnp.float32),
        scratch_shapes=[
            pltpu.VMEM((modes, half_rows, width), jnp.float32),
            pltpu.VMEM((edges, modes, TILE, width), jnp.float32),
            pltpu.SemaphoreType.DMA((2 + edges,)),
        ],
        compiler_params=params(60),
        cost_estimate=cost(3),
        name="pack_own",
    )(me, state, adjoint, coef, *earlier)


def gather_kernel(count, *refs):
    rows = refs[0].shape[0]
    for index in range(count):
        refs[-1][index * rows : (index + 1) * rows] = refs[index][...]


def gather(pieces, rows, index, earlier):
    _, modes, width = pieces[0].shape
    shape = (len(pieces) * rows, modes, width)
    return pl.pallas_call(
        functools.partial(gather_kernel, len(pieces)),
        grid=(1,),
        in_specs=[pl.BlockSpec((rows, modes, width), lambda i: (index, 0, 0))] * len(pieces)
        + [ANYWHERE] * len(earlier),
        out_specs=pl.BlockSpec(shape, lambda i: (0, 0, 0)),
        out_shape=jax.ShapeDtypeStruct(shape, jnp.float32),
        compiler_params=params(),
        cost_estimate=cost(1),
        name="gather",
    )(*pieces, *earlier)


def operator_kernel(shifts, terms, part, parts, by_owner, me_ref, coef_ref, matrix_ref, *refs):
    owners = len(shifts) + 1
    heads, own_near, near, refs = refs[:3], refs[3:5], refs[5:7], refs[7:]
    pieces, before, after = (refs[i * owners : (i + 1) * owners] for i in range(3))
    outs = refs[-7:-6] if by_owner else refs[-owners - 6 : -6]
    slots, mixed, faces = ((refs[-6], refs[-5]), (refs[-4], refs[-3])), refs[-2], refs[-1]
    rows, block, width = pieces[0].shape
    modes = owners * block
    halves = owners // 2
    me = me_ref[0]
    half = lax.rem(me, halves)
    step = 16
    lanes = lax.broadcasted_iota(jnp.int32, (step, width), 1)
    last = rows - 1

    def with_sides(values, lane):
        left = jnp.where(lane == 0, 0.0, pltpu.roll(values, 1, 1))
        right = jnp.where(lane == width - 1, 0.0, pltpu.roll(values, width - 1, 1))
        return left, right

    first_row = (half * parts + part) * rows
    height = coef_ref.shape[1]
    face_lanes = lax.broadcasted_iota(jnp.int32, (rows, width), 1)
    face_rows = lax.broadcasted_iota(jnp.int32, (rows, width), 0)
    here = slice(part * rows, (part + 1) * rows)
    for term in range(terms):
        centre = coef_ref[term, pl.ds(pl.multiple_of(first_row, TILE), rows), :]
        row_before = coef_ref[term, pl.ds(jnp.maximum(first_row - 1, 0), 1), :]
        row_after = coef_ref[term, pl.ds(jnp.minimum(first_row + rows, height - 1), 1), :]
        row_before = jnp.where(first_row > 0, row_before, 0.0)
        row_after = jnp.where(first_row + rows < height, row_after, 0.0)
        up = jnp.where(face_rows == 0, row_before, pltpu.roll(centre, 1, 0))
        down = jnp.where(face_rows == last, row_after, pltpu.roll(centre, last, 0))
        left, right = with_sides(centre, face_lanes)
        others = (heads[1][term, here, :], heads[2][term, here, :], up, down, left, right)
        for side, other in enumerate(others):
            faces[6 * term + side] = 0.5 * (centre + other)

    def beyond(index, which, here):
        if part != (0, parts - 1)[which]:
            return (before, after)[which][index][0, here, :]
        ref, at = ((before, after)[which][index], 0) if index else (heads[0], terms)
        if halves == 2:
            return jnp.where(half == 1 - which, ref[at, here, :], 0.0)
        return ref[at + which, here, :]

    def stencil(row, slot):
        high, low = slots[slot]
        for index in range(owners):
            side_refs, side_row = (near, (index - 1) * rows + row) if index else (own_near, row)
            for start in range(0, block, step):
                here = pl.ds(start, step)
                centre = pieces[index][row, here, :]
                up = pieces[index][row - 1, here, :] if row > 0 else beyond(index, 0, here)
                down = pieces[index][row + 1, here, :] if row < last else beyond(index, 1, here)
                left, right = with_sides(centre, lanes)
                others = (side_refs[0][side_row, here, :], side_refs[1][side_row, here, :], up, down, left, right)
                slopes = [centre - other for other in others]
                for term in range(terms):
                    total = faces[6 * term, row : row + 1, :] * slopes[0]
                    for side in range(1, 6):
                        total = total + faces[6 * term + side, row : row + 1, :] * slopes[side]
                    rounded = total.astype(jnp.bfloat16)
                    at = pl.ds(term * modes + index * block + start, step)
                    high[at, :] = rounded
                    low[at, :] = (total - rounded.astype(jnp.float32)).astype(jnp.bfloat16)

    def mix(row, slot):
        high, low = slots[slot]
        both = jnp.dot(matrix_ref[...], high[...], preferred_element_type=jnp.float32)
        rest = jnp.dot(matrix_ref[:modes, :], low[...], preferred_element_type=jnp.float32)
        total = both[:modes] + both[modes:] + rest
        if by_owner:
            for owner in range(owners):
                outs[0][owner, row] = total[owner * block : (owner + 1) * block]
            return
        mixed[...] = total
        for index, shift in enumerate([0] + shifts):
            owner = lax.rem(me + shift, owners)
            outs[index][row] = mixed[pl.ds(pl.multiple_of(owner * block, block), block), :]

    stencil(0, 0)
    for row in range(rows):
        if row < last:
            stencil(row + 1, (row + 1) % 2)
        mix(row, row % 2)


def apply_operator(me, coef, matrix, own, own_near, groups, group_of, near, part, rows, shifts, by_owner):
    _, block, width = own.shape
    owners = len(shifts) + 1
    modes = owners * block
    terms, height, _ = coef.shape
    parts = height // (owners // 2) // rows
    edges = edge_count(owners // 2)
    head = head_rows(terms, owners // 2)

    def at(count, first):
        return pl.BlockSpec((count, block, width), lambda i: (first // count, 0, 0))

    def pieces_at(first, count):
        group, skipped = group_of[first // rows]
        first_in = first - skipped * rows
        return [own, *groups[group]], [at(count, head + first)] + [at(count, first_in)] * len(shifts)

    def edge_pieces():
        return [own, *groups[0]], [at(1, 0)] + [at(edges, rows)] * len(shifts)

    operands = [coef, matrix, own, *own_near, *own_near, *near]
    in_specs = [SCALARS, whole(coef), whole(matrix)] + [at(head, 0)] * 3
    in_specs += [at(rows, head + part * rows)] * 2 + [whole(array) for array in near]
    for arrays, specs in (
        pieces_at(part * rows, rows),
        pieces_at(part * rows - 1, 1) if part else edge_pieces(),
        pieces_at((part + 1) * rows, 1) if part < parts - 1 else edge_pieces(),
    ):
        operands += arrays
        in_specs += specs
    shape, count = ((owners, rows, block, width), 1) if by_owner else ((rows, block, width), owners)
    return pl.pallas_call(
        functools.partial(operator_kernel, shifts, terms, part, parts, by_owner),
        grid=(1,),
        in_specs=in_specs,
        out_specs=[pl.BlockSpec(shape, lambda i: (0,) * len(shape))] * count,
        out_shape=[jax.ShapeDtypeStruct(shape, jnp.float32)] * count,
        scratch_shapes=[pltpu.VMEM((terms * modes, width), jnp.bfloat16)] * 4
        + [pltpu.VMEM((modes, width), jnp.float32), pltpu.VMEM((6 * terms, rows, width), jnp.float32)],
        compiler_params=params(),
        cost_estimate=cost(6),
        name="operator",
    )(me, *operands)


def finish_kernel(shifts, by_owner, me_ref, *refs):
    owners = len(shifts) + 1
    halves = owners // 2
    mixed = refs[: 2 if by_owner else owners]
    state_ref, control_ref = refs[len(mixed) : len(mixed) + 2]
    state_out, adjoint_out = refs[-2:]
    half = pl.program_id(0)
    if by_owner:
        adjoint_out[...] = jnp.swapaxes(mixed[0][0], 0, 1) - control_ref[...]
        state_out[...] = state_ref[...] + jnp.swapaxes(mixed[1][0], 0, 1)
        return
    for index, shift in enumerate([0] + shifts):
        source = lax.rem(me_ref[0] + owners - shift, owners)

        @pl.when(source == half)
        def _(index=index):
            adjoint_out[...] = jnp.swapaxes(mixed[index][...], 0, 1) - control_ref[...]

        @pl.when(source == halves + half)
        def _(index=index):
            state_out[...] = state_ref[...] + jnp.swapaxes(mixed[index][...], 0, 1)


def finish(me, mixed, state, control, outputs, part, shifts):
    modes, _, width = state.shape
    halves = (len(shifts) + 1) // 2
    rows = mixed[0].shape[-3]
    parts = state.shape[1] // halves // rows
    block = pl.BlockSpec((modes, rows, width), lambda h: (0, h * parts + part, 0))
    by_owner = len(mixed) == 1
    if by_owner:
        sources = [
            pl.BlockSpec((1, rows, modes, width), lambda h, field=field: (field * halves + h, 0, 0, 0))
            for field in range(2)
        ]
        mixed = mixed * 2
    else:
        sources = [whole(m) for m in mixed]
    in_specs = [SCALARS] + sources + [block] * 2
    operands = [me, *mixed, state, control]
    aliases = {}
    if outputs is not None:
        aliases = {len(operands) + i: i for i in range(2)}
        in_specs += [ANYWHERE] * 2
        operands += list(outputs)
    return pl.pallas_call(
        functools.partial(finish_kernel, shifts, by_owner),
        grid=(halves,),
        in_specs=in_specs,
        out_specs=[block] * 2,
        out_shape=[jax.ShapeDtypeStruct(state.shape, jnp.float32)] * 2,
        input_output_aliases=aliases,
        compiler_params=params(60),
        cost_estimate=cost(2.5),
        name="finish",
    )(*operands)


def shards(state, control, adjoint, coefficient, pattern, weights):
    shape = state.shape
    modes, _, height, width = shape
    control_residual = 0.5 * control - adjoint
    state, control, adjoint = (a.reshape(modes, height, width) for a in (state, control, adjoint))
    coef = coefficient[:, 0]
    owners = lax.axis_size("mode")
    rows = TILE
    parts = height // (owners // 2) // rows
    planes = lax.axis_size("space")
    forward = [(i, i + 1) for i in range(planes - 1)]
    backward = [(i + 1, i) for i in range(planes - 1)]
    me = lax.axis_index("mode").astype(jnp.int32).reshape(1)
    shifts = sorted(range(1, owners), key=lambda s: min(s, owners - s))

    def move(array, shift):
        return lax.ppermute(array, "mode", [(i, (i + shift) % owners) for i in range(owners)])

    def beside(array):
        return lax.ppermute(array, "space", forward), lax.ppermute(array, "space", backward)

    matrix = coupling_matrices(me, pattern, weights, shifts)
    halves = owners // 2
    groups, bodies, nears, mixed = [], [], [], []
    members = [[part] for part in range(parts)]
    group_of = {part: (index, group[0]) for index, group in enumerate(members) for part in group}

    def exchange_all(part, earlier):
        packed = pack_all(state, adjoint, halves, part, earlier)
        arrived = lax.all_to_all(packed, "mode", 0, 0, tiled=True)
        groups.append(
            [lax.dynamic_index_in_dim(arrived, lax.rem(me[0] + owners - s, owners), keepdims=False) for s in shifts]
        )
        return packed

    def exchange(group, earlier):
        packed = pack(me, state, adjoint, shifts, group[0] * rows, len(group) * rows, owners, earlier)
        groups.append([move(piece, shift) for piece, shift in zip(packed, shifts)])

    def halo(part, earlier):
        group, skipped = group_of[part]
        bodies.append(gather(groups[group], rows, part - skipped, earlier))
        nears.append(beside(bodies[part]))

    packed = exchange_all(0, [])
    own = pack_own(me, state, adjoint, coef, owners, [packed])
    own_near = list(beside(own))
    halo(0, own_near)
    for part in range(1, parts):
        earlier = [own] if part == 1 else [bodies[0]]
        if 1 < part == parts - 1:
            exchange_all(part, earlier)
        else:
            exchange([part], earlier)
    for part in range(parts):
        if part:
            halo(part, [mixed[part - 2][0]] if part > 1 else [])
        mixed.append(
            apply_operator(
                me, coef, matrix, own, own_near, groups, group_of, nears[part], part, rows, shifts, part == 0
            )
        )

    outputs = None
    for part in range(parts):
        if part == 0:
            returned = [lax.all_to_all(mixed[0][0], "mode", 0, 0, tiled=True)]
        else:
            returned = [mixed[part][0]] + [move(m, shift) for m, shift in zip(mixed[part][1:], shifts)]
        outputs = finish(me, returned, state, control, outputs, part, shifts)
    return outputs[0].reshape(shape), control_residual, outputs[1].reshape(shape)


def solution(mesh):
    split = P("mode", "space", None, None)
    in_specs = (split, split, split, P(None, "space", None, None), P(), P())
    return jax.shard_map(shards, mesh=mesh, in_specs=in_specs, out_specs=(split, split, split), check_vma=False)
```

```python
import functools

import jax
import jax.numpy as jnp
from jax import lax
from jax.experimental import pallas as pl
from jax.experimental.pallas import tpu as pltpu
from jax.sharding import PartitionSpec as P

TILE = 8
ANYWHERE = pl.BlockSpec(memory_space=pl.ANY)
SCALARS = pl.BlockSpec(memory_space=pltpu.SMEM)


def whole(array):
    return pl.BlockSpec(array.shape, lambda *_: (0,) * array.ndim)


def cost(micros):
    return pl.CostEstimate(flops=0, bytes_accessed=int(micros * 3.5e6), transcendentals=0)


def params(mib=48):
    return pltpu.CompilerParams(vmem_limit_bytes=mib * 1024 * 1024)


def matrix_kernel(shifts, me_ref, pattern_ref, weights_ref, out_ref, coupling):
    terms, entries, modes = pattern_ref.shape
    owners = len(shifts) + 1
    block = modes // owners
    rows = lax.broadcasted_iota(jnp.int32, (modes, modes), 0)
    for term in range(terms):
        flipped = jnp.zeros((modes, modes), jnp.float32)
        for entry in range(entries):
            hits = pattern_ref[term, entry : entry + 1, :] == rows
            flipped = flipped + jnp.where(hits, weights_ref[term, entry : entry + 1, :], 0.0)
        coupling[term] = 0.5 * (flipped + flipped.T)
    for term in range(terms):
        picked = []
        for shift in [0] + shifts:
            source = lax.rem(me_ref[0] + owners - shift, owners)
            picked.append(coupling[term, pl.ds(pl.multiple_of(source * block, block), block), :])
        columns = jnp.concatenate(picked, 0).T
        high = columns.astype(jnp.bfloat16)
        at = slice(term * modes, (term + 1) * modes)
        out_ref[:modes, at] = high
        out_ref[modes:, at] = (columns - high.astype(jnp.float32)).astype(jnp.bfloat16)


def coupling_matrices(me, pattern, weights, shifts):
    terms, modes, _ = pattern.shape
    pattern, weights = jnp.swapaxes(pattern, 1, 2), jnp.swapaxes(weights, 1, 2)
    shape = (2 * modes, terms * modes)
    return pl.pallas_call(
        functools.partial(matrix_kernel, shifts),
        grid=(1,),
        in_specs=[SCALARS, whole(pattern), whole(weights)],
        out_specs=pl.BlockSpec(shape, lambda i: (0, 0)),
        out_shape=jax.ShapeDtypeStruct(shape, jnp.bfloat16),
        scratch_shapes=[pltpu.VMEM((terms, modes, modes), jnp.float32)],
        compiler_params=params(),
        cost_estimate=cost(2),
        name="coupling",
    )(me, pattern, weights)


def target(me_ref, shift, owners):
    block = lax.rem(me_ref[0] + shift, owners)
    return block // (owners // 2), lax.rem(block, owners // 2)


def edge_count(halves):
    return 1 if halves == 2 else 2


def head_rows(terms, halves):
    return -(-(terms + edge_count(halves)) // TILE) * TILE


def fetch(me_ref, state_ref, adjoint_ref, shift, owners, first, rows, target_ref, sem):
    field, half = target(me_ref, shift, owners)
    height = state_ref.shape[1]
    half_rows = height // (owners // 2)
    at = pl.ds(pl.multiple_of(jnp.clip(half * half_rows + first(half), 0, height - rows), TILE), rows)
    copies = [pltpu.make_async_copy(ref.at[:, at, :], target_ref, sem) for ref in (state_ref, adjoint_ref)]
    for which in range(2):
        pl.when(field == which)(copies[which].start)
    return copies[0].wait


def fetch_edges(me_ref, state_ref, adjoint_ref, shift, owners, target_ref, sems):
    halves = owners // 2
    half_rows = state_ref.shape[1] // halves
    if halves == 2:
        places = [lambda half: jnp.where(half == 1, -TILE, half_rows)]
    else:
        places = [lambda half: -TILE, lambda half: half_rows]
    return [
        fetch(me_ref, state_ref, adjoint_ref, shift, owners, place, TILE, target_ref.at[i], sems[i])
        for i, place in enumerate(places)
    ]


def write_edges(out_ref, at, half, halves, tiles_ref):
    tiles = [jnp.swapaxes(tiles_ref[i], 0, 1) for i in range(edge_count(halves))]
    if halves == 2:
        out_ref[at] = jnp.where(half == 1, tiles[0][TILE - 1], tiles[0][0])
    else:
        out_ref[at] = jnp.where(half > 0, tiles[0][TILE - 1], 0.0)
        out_ref[at + 1] = jnp.where(half < halves - 1, tiles[1][0], 0.0)


def pack_kernel(shifts, owners, rows, part, me_ref, state_ref, adjoint_ref, *refs):
    buffers, sems = refs[-2:]
    outs = refs[-2 - len(shifts) : -2]
    waits = [
        fetch(me_ref, state_ref, adjoint_ref, shift, owners, lambda half: part * rows, rows, buffers.at[i], sems.at[i])
        for i, shift in enumerate(shifts)
    ]
    for index, wait in enumerate(waits):
        wait()
        outs[index][...] = jnp.swapaxes(buffers[index], 0, 1)


def pack(me, state, adjoint, shifts, part, rows, owners, earlier):
    modes, _, width = state.shape
    shape = (rows, modes, width)
    return pl.pallas_call(
        functools.partial(pack_kernel, shifts, owners, rows, part),
        grid=(1,),
        in_specs=[SCALARS] + [ANYWHERE] * (2 + len(earlier)),
        out_specs=[pl.BlockSpec(shape, lambda i: (0, 0, 0))] * len(shifts),
        out_shape=[jax.ShapeDtypeStruct(shape, jnp.float32)] * len(shifts),
        scratch_shapes=[
            pltpu.VMEM((len(shifts), modes, rows, width), jnp.float32),
            pltpu.SemaphoreType.DMA((len(shifts),)),
        ],
        compiler_params=params(60),
        cost_estimate=cost(3),
        name="pack",
    )(me, state, adjoint, *earlier)


def pack_all_kernel(halves, part, state_ref, adjoint_ref, *refs):
    out_ref, buffers, sems = refs[-3:]
    height = state_ref.shape[1]
    half_rows = height // halves
    rows = buffers.shape[3]
    copies = []
    for field, ref in enumerate((state_ref, adjoint_ref)):
        for half in range(halves):
            first = half * half_rows
            starts = [first + part * rows, max(first - TILE, 0), min(first + half_rows, height - TILE)]
            if part:
                del starts[1:]
            elif halves == 2:
                starts.pop(2 if half else 1)
            for i, start in enumerate(starts):
                at = (field * halves + half, i)
                copies.append(
                    (at, pltpu.make_async_copy(ref.at[:, pl.ds(start, rows), :], buffers.at[at], sems.at[at]))
                )
    for _, copy in copies:
        copy.start()
    for (block, i), copy in copies:
        copy.wait()
        half = block % halves
        values = jnp.swapaxes(buffers[block, i], 0, 1)
        if i == 0:
            out_ref[block, :rows] = values
        elif halves == 2:
            out_ref[block, rows] = values[TILE - 1 if half else 0]
        else:
            inside = half > 0 if i == 1 else half < halves - 1
            out_ref[block, rows + i - 1] = values[TILE - 1 if i == 1 else 0] if inside else jnp.zeros_like(values[0])


def pack_all(state, adjoint, halves, part, earlier):
    modes, _, width = state.shape
    edges = 0 if part else edge_count(halves)
    shape = (2 * halves, TILE + edges, modes, width)
    return pl.pallas_call(
        functools.partial(pack_all_kernel, halves, part),
        grid=(1,),
        in_specs=[ANYWHERE] * (2 + len(earlier)),
        out_specs=pl.BlockSpec(shape, lambda i: (0,) * 4),
        out_shape=jax.ShapeDtypeStruct(shape, jnp.float32),
        scratch_shapes=[
            pltpu.VMEM((2 * halves, 1 + edges, modes, TILE, width), jnp.float32),
            pltpu.SemaphoreType.DMA((2 * halves, 1 + edges)),
        ],
        compiler_params=params(60),
        cost_estimate=cost(3),
        name="pack_all",
    )(state, adjoint, *earlier)


def pack_own_kernel(owners, me_ref, state_ref, adjoint_ref, coef_ref, *refs):
    out_ref, buffer, tiles, sems = refs[-4:]
    halves = owners // 2
    terms, height, _ = coef_ref.shape
    half_rows = height // halves
    head = head_rows(terms, halves)
    _, half = target(me_ref, 0, owners)
    place = (me_ref, state_ref, adjoint_ref, 0, owners)
    sem = [sems.at[i] for i in range(2 + edge_count(halves))]
    waits = [fetch(*place, lambda half: 0, half_rows, buffer, sem[0])]
    waits += fetch_edges(*place, tiles, sem[2:])
    at = pl.ds(pl.multiple_of(half * half_rows, TILE), half_rows)
    coef_copy = pltpu.make_async_copy(coef_ref.at[:, at, :], out_ref.at[:terms], sem[1])
    coef_copy.start()
    for wait in waits:
        wait()
    out_ref[head:] = jnp.swapaxes(buffer[...], 0, 1)
    write_edges(out_ref, terms, half, halves, tiles)
    coef_copy.wait()


def pack_own(me, state, adjoint, coef, owners, earlier):
    modes, height, width = state.shape
    halves = owners // 2
    half_rows = height // halves
    edges = edge_count(halves)
    terms = coef.shape[0]
    count = head_rows(terms, halves) + half_rows
    return pl.pallas_call(
        functools.partial(pack_own_kernel, owners),
        grid=(1,),
        in_specs=[SCALARS] + [ANYWHERE] * (3 + len(earlier)),
        out_specs=pl.BlockSpec((count, modes, width), lambda i: (0, 0, 0)),
        out_shape=jax.ShapeDtypeStruct((count, modes, width), jnp.float32),
        scratch_shapes=[
            pltpu.VMEM((modes, half_rows, width), jnp.float32),
            pltpu.VMEM((edges, modes, TILE, width), jnp.float32),
            pltpu.SemaphoreType.DMA((2 + edges,)),
        ],
        compiler_params=params(60),
        cost_estimate=cost(3),
        name="pack_own",
    )(me, state, adjoint, coef, *earlier)


def gather_kernel(count, *refs):
    rows = refs[0].shape[0]
    for index in range(count):
        refs[-1][index * rows : (index + 1) * rows] = refs[index][...]


def gather(pieces, rows, index, earlier):
    _, modes, width = pieces[0].shape
    shape = (len(pieces) * rows, modes, width)
    return pl.pallas_call(
        functools.partial(gather_kernel, len(pieces)),
        grid=(1,),
        in_specs=[pl.BlockSpec((rows, modes, width), lambda i: (index, 0, 0))] * len(pieces)
        + [ANYWHERE] * len(earlier),
        out_specs=pl.BlockSpec(shape, lambda i: (0, 0, 0)),
        out_shape=jax.ShapeDtypeStruct(shape, jnp.float32),
        compiler_params=params(),
        cost_estimate=cost(1),
        name="gather",
    )(*pieces, *earlier)


def operator_kernel(shifts, terms, part, parts, by_owner, me_ref, coef_ref, matrix_ref, *refs):
    owners = len(shifts) + 1
    heads, own_near, near, refs = refs[:3], refs[3:5], refs[5:7], refs[7:]
    pieces, before, after = (refs[i * owners : (i + 1) * owners] for i in range(3))
    outs = refs[-8:-7] if by_owner else refs[-owners - 7 : -7]
    refs[-7][...] = jnp.zeros_like(refs[-7])
    slots, mixed, faces = ((refs[-6], refs[-5]), (refs[-4], refs[-3])), refs[-2], refs[-1]
    rows, block, width = pieces[0].shape
    modes = owners * block
    halves = owners // 2
    me = me_ref[0]
    half = lax.rem(me, halves)
    step = 16
    lanes = lax.broadcasted_iota(jnp.int32, (step, width), 1)
    last = rows - 1

    def with_sides(values, lane):
        left = jnp.where(lane == 0, 0.0, pltpu.roll(values, 1, 1))
        right = jnp.where(lane == width - 1, 0.0, pltpu.roll(values, width - 1, 1))
        return left, right

    first_row = (half * parts + part) * rows
    height = coef_ref.shape[1]
    face_lanes = lax.broadcasted_iota(jnp.int32, (rows, width), 1)
    face_rows = lax.broadcasted_iota(jnp.int32, (rows, width), 0)
    here = slice(part * rows, (part + 1) * rows)
    for term in range(terms):
        centre = coef_ref[term, pl.ds(pl.multiple_of(first_row, TILE), rows), :]
        row_before = coef_ref[term, pl.ds(jnp.maximum(first_row - 1, 0), 1), :]
        row_after = coef_ref[term, pl.ds(jnp.minimum(first_row + rows, height - 1), 1), :]
        row_before = jnp.where(first_row > 0, row_before, 0.0)
        row_after = jnp.where(first_row + rows < height, row_after, 0.0)
        up = jnp.where(face_rows == 0, row_before, pltpu.roll(centre, 1, 0))
        down = jnp.where(face_rows == last, row_after, pltpu.roll(centre, last, 0))
        left, right = with_sides(centre, face_lanes)
        others = (heads[1][term, here, :], heads[2][term, here, :], up, down, left, right)
        for side, other in enumerate(others):
            faces[6 * term + side] = 0.5 * (centre + other)

    def beyond(index, which, here):
        if part != (0, parts - 1)[which]:
            return (before, after)[which][index][0, here, :]
        ref, at = ((before, after)[which][index], 0) if index else (heads[0], terms)
        if halves == 2:
            return jnp.where(half == 1 - which, ref[at, here, :], 0.0)
        return ref[at + which, here, :]

    def stencil(row, slot):
        high, low = slots[slot]
        for index in range(owners):
            side_refs, side_row = (near, (index - 1) * rows + row) if index else (own_near, row)
            for start in range(0, block, step):
                here = pl.ds(start, step)
                centre = pieces[index][row, here, :]
                up = pieces[index][row - 1, here, :] if row > 0 else beyond(index, 0, here)
                down = pieces[index][row + 1, here, :] if row < last else beyond(index, 1, here)
                left, right = with_sides(centre, lanes)
                others = (side_refs[0][side_row, here, :], side_refs[1][side_row, here, :], up, down, left, right)
                slopes = [centre - other for other in others]
                for term in range(terms):
                    total = faces[6 * term, row : row + 1, :] * slopes[0]
                    for side in range(1, 6):
                        total = total + faces[6 * term + side, row : row + 1, :] * slopes[side]
                    rounded = total.astype(jnp.bfloat16)
                    at = pl.ds(term * modes + index * block + start, step)
                    high[at, :] = rounded
                    low[at, :] = (total - rounded.astype(jnp.float32)).astype(jnp.bfloat16)

    def mix(row, slot):
        high, low = slots[slot]
        both = jnp.dot(matrix_ref[...], high[...], preferred_element_type=jnp.float32)
        rest = jnp.dot(matrix_ref[:modes, :], low[...], preferred_element_type=jnp.float32)
        total = both[:modes] + both[modes:] + rest
        if by_owner:
            for owner in range(owners):
                outs[0][owner, row] = total[owner * block : (owner + 1) * block]
            return
        mixed[...] = total
        for index, shift in enumerate([0] + shifts):
            owner = lax.rem(me + shift, owners)
            outs[index][row] = mixed[pl.ds(pl.multiple_of(owner * block, block), block), :]

    stencil(0, 0)
    for row in range(rows):
        if row < last:
            stencil(row + 1, (row + 1) % 2)
        mix(row, row % 2)


def apply_operator(me, coef, matrix, own, own_near, groups, near, part, rows, shifts, by_owner, filled, after):
    _, block, width = own.shape
    owners = len(shifts) + 1
    modes = owners * block
    terms, height, _ = coef.shape
    parts = height // (owners // 2) // rows
    edges = edge_count(owners // 2)
    head = head_rows(terms, owners // 2)

    def at(count, first):
        return pl.BlockSpec((count, block, width), lambda i: (first // count, 0, 0))

    def pieces_at(first, count):
        group, first_in = first // rows, first % rows
        return [own, *groups[group]], [at(count, head + first)] + [at(count, first_in)] * len(shifts)

    def edge_pieces():
        return [own, *groups[0]], [at(1, 0)] + [at(edges, rows)] * len(shifts)

    operands = [coef, matrix, own, *own_near, *own_near, *near]
    in_specs = [SCALARS, whole(coef), whole(matrix)] + [at(head, 0)] * 3
    in_specs += [at(rows, head + part * rows)] * 2 + [whole(array) for array in near]
    for arrays, specs in (
        pieces_at(part * rows, rows),
        pieces_at(part * rows - 1, 1) if part else edge_pieces(),
        pieces_at((part + 1) * rows, 1) if part < parts - 1 else edge_pieces(),
    ):
        operands += arrays
        in_specs += specs
    aliases = {}
    operands += after
    in_specs += [ANYWHERE] * len(after)
    if filled is not None:
        aliases = {len(operands) + 1: 0}
        operands.append(filled)
        in_specs.append(ANYWHERE)
    if by_owner:
        out_specs = [pl.BlockSpec((owners, rows, block, width), lambda i: (0, part, 0, 0))]
        shapes = [(owners, by_owner * rows, block, width)]
    else:
        out_specs = [pl.BlockSpec((rows, block, width), lambda i: (0, 0, 0))] * owners
        shapes = [(rows, block, width)] * owners
    note = (TILE, width)
    return pl.pallas_call(
        functools.partial(operator_kernel, shifts, terms, part, parts, by_owner),
        grid=(1,),
        in_specs=in_specs,
        out_specs=out_specs + [pl.BlockSpec(note, lambda i: (0, 0))],
        out_shape=[jax.ShapeDtypeStruct(shape, jnp.float32) for shape in shapes + [note]],
        input_output_aliases=aliases,
        scratch_shapes=[pltpu.VMEM((terms * modes, width), jnp.bfloat16)] * 4
        + [pltpu.VMEM((modes, width), jnp.float32), pltpu.VMEM((6 * terms, rows, width), jnp.float32)],
        compiler_params=params(),
        cost_estimate=cost(6),
        name="operator",
    )(me, *operands)


def finish_kernel(shifts, by_owner, me_ref, *refs):
    owners = len(shifts) + 1
    halves = owners // 2
    mixed = refs[: 2 if by_owner else owners]
    state_ref, control_ref = refs[len(mixed) : len(mixed) + 2]
    state_out, adjoint_out = refs[-2:]
    half = pl.program_id(0)
    if by_owner:
        adjoint_out[...] = jnp.swapaxes(mixed[0][0], 0, 1) - control_ref[...]
        state_out[...] = state_ref[...] + jnp.swapaxes(mixed[1][0], 0, 1)
        return
    for index, shift in enumerate([0] + shifts):
        source = lax.rem(me_ref[0] + owners - shift, owners)

        @pl.when(source == half)
        def _(index=index):
            adjoint_out[...] = jnp.swapaxes(mixed[index][...], 0, 1) - control_ref[...]

        @pl.when(source == halves + half)
        def _(index=index):
            state_out[...] = state_ref[...] + jnp.swapaxes(mixed[index][...], 0, 1)


def finish(me, mixed, state, control, outputs, part, rows, shifts):
    modes, _, width = state.shape
    halves = (len(shifts) + 1) // 2
    parts = state.shape[1] // halves // rows
    block = pl.BlockSpec((modes, rows, width), lambda h: (0, h * parts + part, 0))
    by_owner = len(mixed) == 1
    if by_owner:
        sources = [
            pl.BlockSpec((1, rows, modes, width), lambda h, field=field: (field * halves + h, part, 0, 0))
            for field in range(2)
        ]
        mixed = mixed * 2
    else:
        sources = [whole(m) for m in mixed]
    in_specs = [SCALARS] + sources + [block] * 2
    operands = [me, *mixed, state, control]
    aliases = {}
    if outputs is not None:
        aliases = {len(operands) + i: i for i in range(2)}
        in_specs += [ANYWHERE] * 2
        operands += list(outputs)
    return pl.pallas_call(
        functools.partial(finish_kernel, shifts, by_owner),
        grid=(halves,),
        in_specs=in_specs,
        out_specs=[block] * 2,
        out_shape=[jax.ShapeDtypeStruct(state.shape, jnp.float32)] * 2,
        input_output_aliases=aliases,
        compiler_params=params(60),
        cost_estimate=cost(2.5),
        name="finish",
    )(*operands)


def shards(state, control, adjoint, coefficient, pattern, weights):
    shape = state.shape
    modes, _, height, width = shape
    control_residual = 0.5 * control - adjoint
    state, control, adjoint = (a.reshape(modes, height, width) for a in (state, control, adjoint))
    coef = coefficient[:, 0]
    owners = lax.axis_size("mode")
    rows = TILE
    parts = height // (owners // 2) // rows
    planes = lax.axis_size("space")
    forward = [(i, i + 1) for i in range(planes - 1)]
    backward = [(i + 1, i) for i in range(planes - 1)]
    me = lax.axis_index("mode").astype(jnp.int32).reshape(1)
    shifts = sorted(range(1, owners), key=lambda s: min(s, owners - s))

    def move(array, shift):
        return lax.ppermute(array, "mode", [(i, (i + shift) % owners) for i in range(owners)])

    def beside(array):
        return lax.ppermute(array, "space", forward), lax.ppermute(array, "space", backward)

    matrix = coupling_matrices(me, pattern, weights, shifts)
    groups, bodies, nears, mixed = [], [], [], []
    together = min(parts, 2)
    packs = {}

    def relative(arrived):
        return [lax.dynamic_index_in_dim(arrived, lax.rem(me[0] + owners - s, owners), keepdims=False) for s in shifts]

    def exchange(part):
        earlier = [own] if part == 1 else [mixed[part - 3][-1]] if part > 2 else [bodies[0]]
        if part > 2:
            packs[part] = [pack_all(state, adjoint, owners // 2, part, earlier)]
            groups.append(relative(lax.all_to_all(packs[part][0], "mode", 0, 0, tiled=True)))
        else:
            packed = pack(me, state, adjoint, shifts, part, rows, owners, earlier)
            groups.append([move(piece, shift) for piece, shift in zip(packed, shifts)])

    def halo(part):
        earlier = [mixed[min(1, len(mixed) - 1)][-1]] if part > 1 else [] if part else own_near
        bodies.append(gather(groups[part], rows, 0, earlier))
        nears.append(beside(bodies[part]))

    def operate(part):
        by_owner = together if part < together else 0
        filled = mixed[part - 1][0] if 0 < part < together else None
        after = [packs[3][0]] if part == 1 and parts > 3 else []
        mixed.append(
            apply_operator(
                me, coef, matrix, own, own_near, groups, nears[part], part, rows, shifts, by_owner, filled, after
            )
        )

    packed = pack_all(state, adjoint, owners // 2, 0, [])
    everyone = lax.all_to_all(packed, "mode", 0, 0, tiled=True)
    groups.append(
        [lax.dynamic_index_in_dim(everyone, lax.rem(me[0] + owners - s, owners), keepdims=False) for s in shifts]
    )
    own = pack_own(me, state, adjoint, coef, owners, [packed])
    own_near = list(beside(own))
    halo(0)
    exchange(1)
    halo(1)
    if parts > 2:
        exchange(2)
    for part in range(parts):
        operate(part)
        if part + 3 < parts:
            exchange(part + 3)
        if part == 1 or parts < 4 and part + 2 < parts:
            for later in range(part + 1, parts):
                halo(later)

    outputs = None
    first_parts = lax.all_to_all(mixed[together - 1][0], "mode", 0, 0, tiled=True)
    for part in range(parts):
        if part < together:
            returned = [first_parts]
        else:
            returned = [mixed[part][0]] + [move(m, shift) for m, shift in zip(mixed[part][1:-1], shifts)]
        outputs = finish(me, returned, state, control, outputs, part, rows, shifts)
    return outputs[0].reshape(shape), control_residual, outputs[1].reshape(shape)


def solution(mesh):
    split = P("mode", "space", None, None)
    in_specs = (split, split, split, P(None, "space", None, None), P(), P())
    return jax.shard_map(shards, mesh=mesh, in_specs=in_specs, out_specs=(split, split, split), check_vma=False)
```

```python
import functools

import jax
import jax.numpy as jnp
from jax import lax
from jax.experimental import pallas as pl
from jax.experimental.pallas import tpu as pltpu
from jax.sharding import PartitionSpec as P

TILE = 8
ANYWHERE = pl.BlockSpec(memory_space=pl.ANY)
SCALARS = pl.BlockSpec(memory_space=pltpu.SMEM)


def whole(array):
    return pl.BlockSpec(array.shape, lambda *_: (0,) * array.ndim)


def cost(micros):
    return pl.CostEstimate(flops=0, bytes_accessed=int(micros * 3.5e6), transcendentals=0)


def params(mib=48):
    return pltpu.CompilerParams(vmem_limit_bytes=mib * 1024 * 1024)


def matrix_kernel(shifts, me_ref, pattern_ref, weights_ref, out_ref, coupling):
    terms, entries, modes = pattern_ref.shape
    owners = len(shifts) + 1
    block = modes // owners
    rows = lax.broadcasted_iota(jnp.int32, (modes, modes), 0)
    for term in range(terms):
        flipped = jnp.zeros((modes, modes), jnp.float32)
        for entry in range(entries):
            hits = pattern_ref[term, entry : entry + 1, :] == rows
            flipped = flipped + jnp.where(hits, weights_ref[term, entry : entry + 1, :], 0.0)
        coupling[term] = 0.5 * (flipped + flipped.T)
    for term in range(terms):
        picked = []
        for shift in [0] + shifts:
            source = lax.rem(me_ref[0] + owners - shift, owners)
            picked.append(coupling[term, pl.ds(pl.multiple_of(source * block, block), block), :])
        columns = jnp.concatenate(picked, 0).T
        high = columns.astype(jnp.bfloat16)
        at = slice(term * modes, (term + 1) * modes)
        out_ref[:modes, at] = high
        out_ref[modes:, at] = (columns - high.astype(jnp.float32)).astype(jnp.bfloat16)


def coupling_matrices(me, pattern, weights, shifts):
    terms, modes, _ = pattern.shape
    pattern, weights = jnp.swapaxes(pattern, 1, 2), jnp.swapaxes(weights, 1, 2)
    shape = (2 * modes, terms * modes)
    return pl.pallas_call(
        functools.partial(matrix_kernel, shifts),
        grid=(1,),
        in_specs=[SCALARS, whole(pattern), whole(weights)],
        out_specs=pl.BlockSpec(shape, lambda i: (0, 0)),
        out_shape=jax.ShapeDtypeStruct(shape, jnp.bfloat16),
        scratch_shapes=[pltpu.VMEM((terms, modes, modes), jnp.float32)],
        compiler_params=params(),
        cost_estimate=cost(2),
        name="coupling",
    )(me, pattern, weights)


def target(me_ref, shift, owners):
    block = lax.rem(me_ref[0] + shift, owners)
    return block // (owners // 2), lax.rem(block, owners // 2)


def edge_count(halves):
    return 1 if halves == 2 else 2


def head_rows(terms, halves):
    return -(-(terms + edge_count(halves)) // TILE) * TILE


def fetch(me_ref, state_ref, adjoint_ref, shift, owners, first, rows, target_ref, sem):
    field, half = target(me_ref, shift, owners)
    height = state_ref.shape[1]
    half_rows = height // (owners // 2)
    at = pl.ds(pl.multiple_of(jnp.clip(half * half_rows + first(half), 0, height - rows), TILE), rows)
    copies = [pltpu.make_async_copy(ref.at[:, at, :], target_ref, sem) for ref in (state_ref, adjoint_ref)]
    for which in range(2):
        pl.when(field == which)(copies[which].start)
    return copies[0].wait


def fetch_edges(me_ref, state_ref, adjoint_ref, shift, owners, target_ref, sems):
    halves = owners // 2
    half_rows = state_ref.shape[1] // halves
    if halves == 2:
        places = [lambda half: jnp.where(half == 1, -TILE, half_rows)]
    else:
        places = [lambda half: -TILE, lambda half: half_rows]
    return [
        fetch(me_ref, state_ref, adjoint_ref, shift, owners, place, TILE, target_ref.at[i], sems[i])
        for i, place in enumerate(places)
    ]


def write_edges(out_ref, at, half, halves, tiles_ref):
    tiles = [jnp.swapaxes(tiles_ref[i], 0, 1) for i in range(edge_count(halves))]
    if halves == 2:
        out_ref[at] = jnp.where(half == 1, tiles[0][TILE - 1], tiles[0][0])
    else:
        out_ref[at] = jnp.where(half > 0, tiles[0][TILE - 1], 0.0)
        out_ref[at + 1] = jnp.where(half < halves - 1, tiles[1][0], 0.0)


def pack_kernel(shifts, owners, first, rows, me_ref, state_ref, adjoint_ref, *refs):
    buffers, sems = refs[-2:]
    outs = refs[-2 - len(shifts) : -2]
    waits = [
        fetch(me_ref, state_ref, adjoint_ref, shift, owners, lambda half: first, rows, buffers.at[i], sems.at[i])
        for i, shift in enumerate(shifts)
    ]
    for index, wait in enumerate(waits):
        wait()
        outs[index][...] = jnp.swapaxes(buffers[index], 0, 1)


def pack(me, state, adjoint, shifts, first, rows, owners, earlier):
    modes, _, width = state.shape
    shape = (rows, modes, width)
    return pl.pallas_call(
        functools.partial(pack_kernel, shifts, owners, first, rows),
        grid=(1,),
        in_specs=[SCALARS] + [ANYWHERE] * (2 + len(earlier)),
        out_specs=[pl.BlockSpec(shape, lambda i: (0, 0, 0))] * len(shifts),
        out_shape=[jax.ShapeDtypeStruct(shape, jnp.float32)] * len(shifts),
        scratch_shapes=[
            pltpu.VMEM((len(shifts), modes, rows, width), jnp.float32),
            pltpu.SemaphoreType.DMA((len(shifts),)),
        ],
        compiler_params=params(60),
        cost_estimate=cost(3),
        name="pack",
    )(me, state, adjoint, *earlier)


def pack_all_kernel(halves, part, state_ref, adjoint_ref, *refs):
    out_ref, buffers, sems = refs[-3:]
    height = state_ref.shape[1]
    half_rows = height // halves
    rows = buffers.shape[3]
    copies = []
    for field, ref in enumerate((state_ref, adjoint_ref)):
        for half in range(halves):
            first = half * half_rows
            starts = [first + part * rows, max(first - TILE, 0), min(first + half_rows, height - TILE)]
            if part:
                del starts[1:]
            elif halves == 2:
                starts.pop(2 if half else 1)
            for i, start in enumerate(starts):
                at = (field * halves + half, i)
                copies.append(
                    (at, pltpu.make_async_copy(ref.at[:, pl.ds(start, rows), :], buffers.at[at], sems.at[at]))
                )
    for _, copy in copies:
        copy.start()
    for (block, i), copy in copies:
        copy.wait()
        half = block % halves
        values = jnp.swapaxes(buffers[block, i], 0, 1)
        if i == 0:
            out_ref[block, :rows] = values
        elif halves == 2:
            out_ref[block, rows] = values[TILE - 1 if half else 0]
        else:
            inside = half > 0 if i == 1 else half < halves - 1
            out_ref[block, rows + i - 1] = values[TILE - 1 if i == 1 else 0] if inside else jnp.zeros_like(values[0])


def pack_all(state, adjoint, halves, part, earlier):
    modes, _, width = state.shape
    edges = 0 if part else edge_count(halves)
    shape = (2 * halves, TILE + edges, modes, width)
    return pl.pallas_call(
        functools.partial(pack_all_kernel, halves, part),
        grid=(1,),
        in_specs=[ANYWHERE] * (2 + len(earlier)),
        out_specs=pl.BlockSpec(shape, lambda i: (0,) * 4),
        out_shape=jax.ShapeDtypeStruct(shape, jnp.float32),
        scratch_shapes=[
            pltpu.VMEM((2 * halves, 1 + edges, modes, TILE, width), jnp.float32),
            pltpu.SemaphoreType.DMA((2 * halves, 1 + edges)),
        ],
        compiler_params=params(60),
        cost_estimate=cost(3),
        name="pack_all",
    )(state, adjoint, *earlier)


def pack_own_kernel(owners, me_ref, state_ref, adjoint_ref, coef_ref, *refs):
    out_ref, buffer, tiles, sems = refs[-4:]
    halves = owners // 2
    terms, height, _ = coef_ref.shape
    half_rows = height // halves
    head = head_rows(terms, halves)
    _, half = target(me_ref, 0, owners)
    place = (me_ref, state_ref, adjoint_ref, 0, owners)
    sem = [sems.at[i] for i in range(2 + edge_count(halves))]
    waits = [fetch(*place, lambda half: 0, half_rows, buffer, sem[0])]
    waits += fetch_edges(*place, tiles, sem[2:])
    at = pl.ds(pl.multiple_of(half * half_rows, TILE), half_rows)
    coef_copy = pltpu.make_async_copy(coef_ref.at[:, at, :], out_ref.at[:terms], sem[1])
    coef_copy.start()
    for wait in waits:
        wait()
    out_ref[head:] = jnp.swapaxes(buffer[...], 0, 1)
    write_edges(out_ref, terms, half, halves, tiles)
    coef_copy.wait()


def pack_own(me, state, adjoint, coef, owners, earlier):
    modes, height, width = state.shape
    halves = owners // 2
    half_rows = height // halves
    edges = edge_count(halves)
    terms = coef.shape[0]
    count = head_rows(terms, halves) + half_rows
    return pl.pallas_call(
        functools.partial(pack_own_kernel, owners),
        grid=(1,),
        in_specs=[SCALARS] + [ANYWHERE] * (3 + len(earlier)),
        out_specs=pl.BlockSpec((count, modes, width), lambda i: (0, 0, 0)),
        out_shape=jax.ShapeDtypeStruct((count, modes, width), jnp.float32),
        scratch_shapes=[
            pltpu.VMEM((modes, half_rows, width), jnp.float32),
            pltpu.VMEM((edges, modes, TILE, width), jnp.float32),
            pltpu.SemaphoreType.DMA((2 + edges,)),
        ],
        compiler_params=params(60),
        cost_estimate=cost(3),
        name="pack_own",
    )(me, state, adjoint, coef, *earlier)


def gather_kernel(count, *refs):
    rows = refs[0].shape[0]
    for index in range(count):
        refs[-1][index * rows : (index + 1) * rows] = refs[index][...]


def gather(pieces, rows, index, earlier):
    _, modes, width = pieces[0].shape
    shape = (len(pieces) * rows, modes, width)
    return pl.pallas_call(
        functools.partial(gather_kernel, len(pieces)),
        grid=(1,),
        in_specs=[pl.BlockSpec((rows, modes, width), lambda i: (index, 0, 0))] * len(pieces)
        + [ANYWHERE] * len(earlier),
        out_specs=pl.BlockSpec(shape, lambda i: (0, 0, 0)),
        out_shape=jax.ShapeDtypeStruct(shape, jnp.float32),
        compiler_params=params(),
        cost_estimate=cost(1),
        name="gather",
    )(*pieces, *earlier)


def operator_kernel(shifts, terms, part, parts, by_owner, me_ref, coef_ref, matrix_ref, *refs):
    owners = len(shifts) + 1
    heads, own_near, near, refs = refs[:3], refs[3:5], refs[5:7], refs[7:]
    pieces, before, after = (refs[i * owners : (i + 1) * owners] for i in range(3))
    outs = refs[-7:-6] if by_owner else refs[-owners - 6 : -6]
    slots, mixed, faces = ((refs[-6], refs[-5]), (refs[-4], refs[-3])), refs[-2], refs[-1]
    rows, block, width = pieces[0].shape
    modes = owners * block
    halves = owners // 2
    me = me_ref[0]
    half = lax.rem(me, halves)
    step = 16
    lanes = lax.broadcasted_iota(jnp.int32, (step, width), 1)
    last = rows - 1

    def with_sides(values, lane):
        left = jnp.where(lane == 0, 0.0, pltpu.roll(values, 1, 1))
        right = jnp.where(lane == width - 1, 0.0, pltpu.roll(values, width - 1, 1))
        return left, right

    first_row = (half * parts + part) * rows
    height = coef_ref.shape[1]
    face_lanes = lax.broadcasted_iota(jnp.int32, (rows, width), 1)
    face_rows = lax.broadcasted_iota(jnp.int32, (rows, width), 0)
    here = slice(part * rows, (part + 1) * rows)
    for term in range(terms):
        centre = coef_ref[term, pl.ds(pl.multiple_of(first_row, TILE), rows), :]
        row_before = coef_ref[term, pl.ds(jnp.maximum(first_row - 1, 0), 1), :]
        row_after = coef_ref[term, pl.ds(jnp.minimum(first_row + rows, height - 1), 1), :]
        row_before = jnp.where(first_row > 0, row_before, 0.0)
        row_after = jnp.where(first_row + rows < height, row_after, 0.0)
        up = jnp.where(face_rows == 0, row_before, pltpu.roll(centre, 1, 0))
        down = jnp.where(face_rows == last, row_after, pltpu.roll(centre, last, 0))
        left, right = with_sides(centre, face_lanes)
        others = (heads[1][term, here, :], heads[2][term, here, :], up, down, left, right)
        for side, other in enumerate(others):
            faces[6 * term + side] = 0.5 * (centre + other)

    def beyond(index, which, here):
        if part != (0, parts - 1)[which]:
            return (before, after)[which][index][0, here, :]
        ref, at = ((before, after)[which][index], 0) if index else (heads[0], terms)
        if halves == 2:
            return jnp.where(half == 1 - which, ref[at, here, :], 0.0)
        return ref[at + which, here, :]

    def stencil(row, slot):
        high, low = slots[slot]
        for index in range(owners):
            side_refs, side_row = (near, (index - 1) * rows + row) if index else (own_near, row)
            for start in range(0, block, step):
                here = pl.ds(start, step)
                centre = pieces[index][row, here, :]
                up = pieces[index][row - 1, here, :] if row > 0 else beyond(index, 0, here)
                down = pieces[index][row + 1, here, :] if row < last else beyond(index, 1, here)
                left, right = with_sides(centre, lanes)
                others = (side_refs[0][side_row, here, :], side_refs[1][side_row, here, :], up, down, left, right)
                slopes = [centre - other for other in others]
                for term in range(terms):
                    total = faces[6 * term, row : row + 1, :] * slopes[0]
                    for side in range(1, 6):
                        total = total + faces[6 * term + side, row : row + 1, :] * slopes[side]
                    rounded = total.astype(jnp.bfloat16)
                    at = pl.ds(term * modes + index * block + start, step)
                    high[at, :] = rounded
                    low[at, :] = (total - rounded.astype(jnp.float32)).astype(jnp.bfloat16)

    def mix(row, slot):
        high, low = slots[slot]
        both = jnp.dot(matrix_ref[...], high[...], preferred_element_type=jnp.float32)
        rest = jnp.dot(matrix_ref[:modes, :], low[...], preferred_element_type=jnp.float32)
        total = both[:modes] + both[modes:] + rest
        if by_owner:
            for owner in range(owners):
                outs[0][owner, row] = total[owner * block : (owner + 1) * block]
            return
        mixed[...] = total
        for index, shift in enumerate([0] + shifts):
            owner = lax.rem(me + shift, owners)
            outs[index][row] = mixed[pl.ds(pl.multiple_of(owner * block, block), block), :]

    stencil(0, 0)
    for row in range(rows):
        if row < last:
            stencil(row + 1, (row + 1) % 2)
        mix(row, row % 2)


def apply_operator(me, coef, matrix, own, own_near, groups, group_of, near, part, rows, shifts, by_owner):
    _, block, width = own.shape
    owners = len(shifts) + 1
    modes = owners * block
    terms, height, _ = coef.shape
    parts = height // (owners // 2) // rows
    edges = edge_count(owners // 2)
    head = head_rows(terms, owners // 2)

    def at(count, first):
        return pl.BlockSpec((count, block, width), lambda i: (first // count, 0, 0))

    def pieces_at(first, count):
        group, skipped = group_of[first // rows]
        first_in = first - skipped * rows
        return [own, *groups[group]], [at(count, head + first)] + [at(count, first_in)] * len(shifts)

    def edge_pieces():
        return [own, *groups[0]], [at(1, 0)] + [at(edges, rows)] * len(shifts)

    operands = [coef, matrix, own, *own_near, *own_near, *near]
    in_specs = [SCALARS, whole(coef), whole(matrix)] + [at(head, 0)] * 3
    in_specs += [at(rows, head + part * rows)] * 2 + [whole(array) for array in near]
    for arrays, specs in (
        pieces_at(part * rows, rows),
        pieces_at(part * rows - 1, 1) if part else edge_pieces(),
        pieces_at((part + 1) * rows, 1) if part < parts - 1 else edge_pieces(),
    ):
        operands += arrays
        in_specs += specs
    shape, count = ((owners, rows, block, width), 1) if by_owner else ((rows, block, width), owners)
    return pl.pallas_call(
        functools.partial(operator_kernel, shifts, terms, part, parts, by_owner),
        grid=(1,),
        in_specs=in_specs,
        out_specs=[pl.BlockSpec(shape, lambda i: (0,) * len(shape))] * count,
        out_shape=[jax.ShapeDtypeStruct(shape, jnp.float32)] * count,
        scratch_shapes=[pltpu.VMEM((terms * modes, width), jnp.bfloat16)] * 4
        + [pltpu.VMEM((modes, width), jnp.float32), pltpu.VMEM((6 * terms, rows, width), jnp.float32)],
        compiler_params=params(),
        cost_estimate=cost(6),
        name="operator",
    )(me, *operands)


def finish_kernel(shifts, by_owner, me_ref, *refs):
    owners = len(shifts) + 1
    halves = owners // 2
    mixed = refs[: 2 if by_owner else owners]
    state_ref, control_ref = refs[len(mixed) : len(mixed) + 2]
    state_out, adjoint_out = refs[-2:]
    half = pl.program_id(0)
    if by_owner:
        adjoint_out[...] = jnp.swapaxes(mixed[0][0], 0, 1) - control_ref[...]
        state_out[...] = state_ref[...] + jnp.swapaxes(mixed[1][0], 0, 1)
        return
    for index, shift in enumerate([0] + shifts):
        source = lax.rem(me_ref[0] + owners - shift, owners)

        @pl.when(source == half)
        def _(index=index):
            adjoint_out[...] = jnp.swapaxes(mixed[index][...], 0, 1) - control_ref[...]

        @pl.when(source == halves + half)
        def _(index=index):
            state_out[...] = state_ref[...] + jnp.swapaxes(mixed[index][...], 0, 1)


def finish(me, mixed, state, control, outputs, part, shifts):
    modes, _, width = state.shape
    halves = (len(shifts) + 1) // 2
    rows = mixed[0].shape[-3]
    parts = state.shape[1] // halves // rows
    block = pl.BlockSpec((modes, rows, width), lambda h: (0, h * parts + part, 0))
    by_owner = len(mixed) == 1
    if by_owner:
        sources = [
            pl.BlockSpec((1, rows, modes, width), lambda h, field=field: (field * halves + h, 0, 0, 0))
            for field in range(2)
        ]
        mixed = mixed * 2
    else:
        sources = [whole(m) for m in mixed]
    in_specs = [SCALARS] + sources + [block] * 2
    operands = [me, *mixed, state, control]
    aliases = {}
    if outputs is not None:
        aliases = {len(operands) + i: i for i in range(2)}
        in_specs += [ANYWHERE] * 2
        operands += list(outputs)
    return pl.pallas_call(
        functools.partial(finish_kernel, shifts, by_owner),
        grid=(halves,),
        in_specs=in_specs,
        out_specs=[block] * 2,
        out_shape=[jax.ShapeDtypeStruct(state.shape, jnp.float32)] * 2,
        input_output_aliases=aliases,
        compiler_params=params(60),
        cost_estimate=cost(2.5),
        name="finish",
    )(*operands)


def shards(state, control, adjoint, coefficient, pattern, weights):
    shape = state.shape
    modes, _, height, width = shape
    control_residual = 0.5 * control - adjoint
    state, control, adjoint = (a.reshape(modes, height, width) for a in (state, control, adjoint))
    coef = coefficient[:, 0]
    owners = lax.axis_size("mode")
    rows = TILE
    parts = height // (owners // 2) // rows
    planes = lax.axis_size("space")
    forward = [(i, i + 1) for i in range(planes - 1)]
    backward = [(i + 1, i) for i in range(planes - 1)]
    me = lax.axis_index("mode").astype(jnp.int32).reshape(1)
    shifts = sorted(range(1, owners), key=lambda s: min(s, owners - s))

    def move(array, shift):
        return lax.ppermute(array, "mode", [(i, (i + shift) % owners) for i in range(owners)])

    def beside(array):
        return lax.ppermute(array, "space", forward), lax.ppermute(array, "space", backward)

    matrix = coupling_matrices(me, pattern, weights, shifts)
    halves = owners // 2
    groups, bodies, nears, mixed = [], [], [], []
    if parts > 2:
        members = [[0], list(range(1, parts - 1)), [parts - 1]]
    else:
        members = [[part] for part in range(parts)]
    group_of = {part: (index, group[0]) for index, group in enumerate(members) for part in group}

    def exchange_all(part, earlier):
        packed = pack_all(state, adjoint, halves, part, earlier)
        arrived = lax.all_to_all(packed, "mode", 0, 0, tiled=True)
        groups.append(
            [lax.dynamic_index_in_dim(arrived, lax.rem(me[0] + owners - s, owners), keepdims=False) for s in shifts]
        )
        return packed

    def exchange(group, earlier):
        packed = pack(me, state, adjoint, shifts, group[0] * rows, len(group) * rows, owners, earlier)
        groups.append([move(piece, shift) for piece, shift in zip(packed, shifts)])

    def halo(part, earlier):
        group, skipped = group_of[part]
        bodies.append(gather(groups[group], rows, part - skipped, earlier))
        nears.append(beside(bodies[part]))

    packed = exchange_all(0, [])
    own = pack_own(me, state, adjoint, coef, owners, [packed])
    own_near = list(beside(own))
    halo(0, own_near)
    if len(members) > 1:
        exchange(members[1], [own])
    for part in range(parts):
        if part:
            halo(part, [mixed[part - 2][0]] if part > 1 else [bodies[0]])
        mixed.append(
            apply_operator(
                me, coef, matrix, own, own_near, groups, group_of, nears[part], part, rows, shifts, part == 0
            )
        )
        if part == 0 and len(members) > 2:
            exchange(members[2], [bodies[0]])

    outputs = None
    for part in range(parts):
        if part == 0:
            returned = [lax.all_to_all(mixed[0][0], "mode", 0, 0, tiled=True)]
        else:
            returned = [mixed[part][0]] + [move(m, shift) for m, shift in zip(mixed[part][1:], shifts)]
        outputs = finish(me, returned, state, control, outputs, part, shifts)
    return outputs[0].reshape(shape), control_residual, outputs[1].reshape(shape)


def solution(mesh):
    split = P("mode", "space", None, None)
    in_specs = (split, split, split, P(None, "space", None, None), P(), P())
    return jax.shard_map(shards, mesh=mesh, in_specs=in_specs, out_specs=(split, split, split), check_vma=False)
```

```python
import functools

import jax
import jax.numpy as jnp
from jax import lax
from jax.experimental import pallas as pl
from jax.experimental.pallas import tpu as pltpu
from jax.sharding import PartitionSpec as P

TILE = 8
ANYWHERE = pl.BlockSpec(memory_space=pl.ANY)
SCALARS = pl.BlockSpec(memory_space=pltpu.SMEM)


def whole(array):
    return pl.BlockSpec(array.shape, lambda *_: (0,) * array.ndim)


def cost(micros):
    return pl.CostEstimate(flops=0, bytes_accessed=int(micros * 3.5e6), transcendentals=0)


def params(mib=48):
    return pltpu.CompilerParams(vmem_limit_bytes=mib * 1024 * 1024)


def matrix_kernel(shifts, me_ref, pattern_ref, weights_ref, out_ref, coupling):
    terms, entries, modes = pattern_ref.shape
    owners = len(shifts) + 1
    block = modes // owners
    rows = lax.broadcasted_iota(jnp.int32, (modes, modes), 0)
    for term in range(terms):
        flipped = jnp.zeros((modes, modes), jnp.float32)
        for entry in range(entries):
            hits = pattern_ref[term, entry : entry + 1, :] == rows
            flipped = flipped + jnp.where(hits, weights_ref[term, entry : entry + 1, :], 0.0)
        coupling[term] = 0.5 * (flipped + flipped.T)
    for term in range(terms):
        picked = []
        for shift in [0] + shifts:
            source = lax.rem(me_ref[0] + owners - shift, owners)
            picked.append(coupling[term, pl.ds(pl.multiple_of(source * block, block), block), :])
        columns = jnp.concatenate(picked, 0).T
        high = columns.astype(jnp.bfloat16)
        at = slice(term * modes, (term + 1) * modes)
        out_ref[:modes, at] = high
        out_ref[modes:, at] = (columns - high.astype(jnp.float32)).astype(jnp.bfloat16)


def coupling_matrices(me, pattern, weights, shifts):
    terms, modes, _ = pattern.shape
    pattern, weights = jnp.swapaxes(pattern, 1, 2), jnp.swapaxes(weights, 1, 2)
    shape = (2 * modes, terms * modes)
    return pl.pallas_call(
        functools.partial(matrix_kernel, shifts),
        grid=(1,),
        in_specs=[SCALARS, whole(pattern), whole(weights)],
        out_specs=pl.BlockSpec(shape, lambda i: (0, 0)),
        out_shape=jax.ShapeDtypeStruct(shape, jnp.bfloat16),
        scratch_shapes=[pltpu.VMEM((terms, modes, modes), jnp.float32)],
        compiler_params=params(),
        cost_estimate=cost(2),
        name="coupling",
    )(me, pattern, weights)


def target(me_ref, shift, owners):
    block = lax.rem(me_ref[0] + shift, owners)
    return block // (owners // 2), lax.rem(block, owners // 2)


def edge_count(halves):
    return 1 if halves == 2 else 2


def head_rows(terms, halves):
    return -(-(terms + edge_count(halves)) // TILE) * TILE


def fetch(me_ref, state_ref, adjoint_ref, shift, owners, first, rows, target_ref, sem):
    field, half = target(me_ref, shift, owners)
    height = state_ref.shape[1]
    half_rows = height // (owners // 2)
    at = pl.ds(pl.multiple_of(jnp.clip(half * half_rows + first(half), 0, height - rows), TILE), rows)
    copies = [pltpu.make_async_copy(ref.at[:, at, :], target_ref, sem) for ref in (state_ref, adjoint_ref)]
    for which in range(2):
        pl.when(field == which)(copies[which].start)
    return copies[0].wait


def fetch_edges(me_ref, state_ref, adjoint_ref, shift, owners, target_ref, sems):
    halves = owners // 2
    half_rows = state_ref.shape[1] // halves
    if halves == 2:
        places = [lambda half: jnp.where(half == 1, -TILE, half_rows)]
    else:
        places = [lambda half: -TILE, lambda half: half_rows]
    return [
        fetch(me_ref, state_ref, adjoint_ref, shift, owners, place, TILE, target_ref.at[i], sems[i])
        for i, place in enumerate(places)
    ]


def write_edges(out_ref, at, half, halves, tiles_ref):
    tiles = [jnp.swapaxes(tiles_ref[i], 0, 1) for i in range(edge_count(halves))]
    if halves == 2:
        out_ref[at] = jnp.where(half == 1, tiles[0][TILE - 1], tiles[0][0])
    else:
        out_ref[at] = jnp.where(half > 0, tiles[0][TILE - 1], 0.0)
        out_ref[at + 1] = jnp.where(half < halves - 1, tiles[1][0], 0.0)


def pack_kernel(shifts, owners, rows, part, me_ref, state_ref, adjoint_ref, *refs):
    buffers, sems = refs[-2:]
    outs = refs[-2 - len(shifts) : -2]
    waits = [
        fetch(me_ref, state_ref, adjoint_ref, shift, owners, lambda half: part * rows, rows, buffers.at[i], sems.at[i])
        for i, shift in enumerate(shifts)
    ]
    for index, wait in enumerate(waits):
        wait()
        outs[index][...] = jnp.swapaxes(buffers[index], 0, 1)


def pack(me, state, adjoint, shifts, part, rows, owners, earlier):
    modes, _, width = state.shape
    shape = (rows, modes, width)
    return pl.pallas_call(
        functools.partial(pack_kernel, shifts, owners, rows, part),
        grid=(1,),
        in_specs=[SCALARS] + [ANYWHERE] * (2 + len(earlier)),
        out_specs=[pl.BlockSpec(shape, lambda i: (0, 0, 0))] * len(shifts),
        out_shape=[jax.ShapeDtypeStruct(shape, jnp.float32)] * len(shifts),
        scratch_shapes=[
            pltpu.VMEM((len(shifts), modes, rows, width), jnp.float32),
            pltpu.SemaphoreType.DMA((len(shifts),)),
        ],
        compiler_params=params(60),
        cost_estimate=cost(3),
        name="pack",
    )(me, state, adjoint, *earlier)


def pack_all_kernel(halves, state_ref, adjoint_ref, out_ref, buffers, sems):
    height = state_ref.shape[1]
    half_rows = height // halves
    rows = buffers.shape[3]
    copies = []
    for field, ref in enumerate((state_ref, adjoint_ref)):
        for half in range(halves):
            first = half * half_rows
            starts = [first, max(first - TILE, 0), min(first + half_rows, height - TILE)]
            if halves == 2:
                starts.pop(2 if half else 1)
            for i, start in enumerate(starts):
                at = (field * halves + half, i)
                copies.append(
                    (at, pltpu.make_async_copy(ref.at[:, pl.ds(start, rows), :], buffers.at[at], sems.at[at]))
                )
    for _, copy in copies:
        copy.start()
    for (block, i), copy in copies:
        copy.wait()
        half = block % halves
        values = jnp.swapaxes(buffers[block, i], 0, 1)
        if i == 0:
            out_ref[block, :rows] = values
        elif halves == 2:
            out_ref[block, rows] = values[TILE - 1 if half else 0]
        else:
            inside = half > 0 if i == 1 else half < halves - 1
            out_ref[block, rows + i - 1] = values[TILE - 1 if i == 1 else 0] if inside else jnp.zeros_like(values[0])


def pack_all(state, adjoint, halves):
    modes, _, width = state.shape
    edges = edge_count(halves)
    shape = (2 * halves, TILE + edges, modes, width)
    return pl.pallas_call(
        functools.partial(pack_all_kernel, halves),
        grid=(1,),
        in_specs=[ANYWHERE] * 2,
        out_specs=pl.BlockSpec(shape, lambda i: (0,) * 4),
        out_shape=jax.ShapeDtypeStruct(shape, jnp.float32),
        scratch_shapes=[
            pltpu.VMEM((2 * halves, 1 + edges, modes, TILE, width), jnp.float32),
            pltpu.SemaphoreType.DMA((2 * halves, 1 + edges)),
        ],
        compiler_params=params(60),
        cost_estimate=cost(3),
        name="pack_all",
    )(state, adjoint)


def pack_own_kernel(owners, me_ref, state_ref, adjoint_ref, coef_ref, *refs):
    out_ref, buffer, tiles, sems = refs[-4:]
    halves = owners // 2
    terms, height, _ = coef_ref.shape
    half_rows = height // halves
    head = head_rows(terms, halves)
    _, half = target(me_ref, 0, owners)
    place = (me_ref, state_ref, adjoint_ref, 0, owners)
    sem = [sems.at[i] for i in range(2 + edge_count(halves))]
    waits = [fetch(*place, lambda half: 0, half_rows, buffer, sem[0])]
    waits += fetch_edges(*place, tiles, sem[2:])
    at = pl.ds(pl.multiple_of(half * half_rows, TILE), half_rows)
    coef_copy = pltpu.make_async_copy(coef_ref.at[:, at, :], out_ref.at[:terms], sem[1])
    coef_copy.start()
    for wait in waits:
        wait()
    out_ref[head:] = jnp.swapaxes(buffer[...], 0, 1)
    write_edges(out_ref, terms, half, halves, tiles)
    coef_copy.wait()


def pack_own(me, state, adjoint, coef, owners, earlier):
    modes, height, width = state.shape
    halves = owners // 2
    half_rows = height // halves
    edges = edge_count(halves)
    terms = coef.shape[0]
    count = head_rows(terms, halves) + half_rows
    return pl.pallas_call(
        functools.partial(pack_own_kernel, owners),
        grid=(1,),
        in_specs=[SCALARS] + [ANYWHERE] * (3 + len(earlier)),
        out_specs=pl.BlockSpec((count, modes, width), lambda i: (0, 0, 0)),
        out_shape=jax.ShapeDtypeStruct((count, modes, width), jnp.float32),
        scratch_shapes=[
            pltpu.VMEM((modes, half_rows, width), jnp.float32),
            pltpu.VMEM((edges, modes, TILE, width), jnp.float32),
            pltpu.SemaphoreType.DMA((2 + edges,)),
        ],
        compiler_params=params(60),
        cost_estimate=cost(3),
        name="pack_own",
    )(me, state, adjoint, coef, *earlier)


def gather_kernel(count, *refs):
    rows = refs[0].shape[0]
    for index in range(count):
        refs[-1][index * rows : (index + 1) * rows] = refs[index][...]


def gather(pieces, rows, index, earlier):
    _, modes, width = pieces[0].shape
    shape = (len(pieces) * rows, modes, width)
    return pl.pallas_call(
        functools.partial(gather_kernel, len(pieces)),
        grid=(1,),
        in_specs=[pl.BlockSpec((rows, modes, width), lambda i: (index, 0, 0))] * len(pieces)
        + [ANYWHERE] * len(earlier),
        out_specs=pl.BlockSpec(shape, lambda i: (0, 0, 0)),
        out_shape=jax.ShapeDtypeStruct(shape, jnp.float32),
        compiler_params=params(),
        cost_estimate=cost(1),
        name="gather",
    )(*pieces, *earlier)


def operator_kernel(shifts, terms, part, parts, by_owner, me_ref, coef_ref, matrix_ref, *refs):
    owners = len(shifts) + 1
    heads, own_near, near, refs = refs[:3], refs[3:5], refs[5:7], refs[7:]
    pieces, before, after = (refs[i * owners : (i + 1) * owners] for i in range(3))
    outs = refs[-7:-6] if by_owner else refs[-owners - 6 : -6]
    slots, mixed, faces = ((refs[-6], refs[-5]), (refs[-4], refs[-3])), refs[-2], refs[-1]
    rows, block, width = pieces[0].shape
    modes = owners * block
    halves = owners // 2
    me = me_ref[0]
    half = lax.rem(me, halves)
    step = 16
    lanes = lax.broadcasted_iota(jnp.int32, (step, width), 1)
    last = rows - 1

    def with_sides(values, lane):
        left = jnp.where(lane == 0, 0.0, pltpu.roll(values, 1, 1))
        right = jnp.where(lane == width - 1, 0.0, pltpu.roll(values, width - 1, 1))
        return left, right

    first_row = (half * parts + part) * rows
    height = coef_ref.shape[1]
    face_lanes = lax.broadcasted_iota(jnp.int32, (rows, width), 1)
    face_rows = lax.broadcasted_iota(jnp.int32, (rows, width), 0)
    here = slice(part * rows, (part + 1) * rows)
    for term in range(terms):
        centre = coef_ref[term, pl.ds(pl.multiple_of(first_row, TILE), rows), :]
        row_before = coef_ref[term, pl.ds(jnp.maximum(first_row - 1, 0), 1), :]
        row_after = coef_ref[term, pl.ds(jnp.minimum(first_row + rows, height - 1), 1), :]
        row_before = jnp.where(first_row > 0, row_before, 0.0)
        row_after = jnp.where(first_row + rows < height, row_after, 0.0)
        up = jnp.where(face_rows == 0, row_before, pltpu.roll(centre, 1, 0))
        down = jnp.where(face_rows == last, row_after, pltpu.roll(centre, last, 0))
        left, right = with_sides(centre, face_lanes)
        others = (heads[1][term, here, :], heads[2][term, here, :], up, down, left, right)
        for side, other in enumerate(others):
            faces[6 * term + side] = 0.5 * (centre + other)

    def beyond(index, which, here):
        if part != (0, parts - 1)[which]:
            return (before, after)[which][index][0, here, :]
        ref, at = ((before, after)[which][index], 0) if index else (heads[0], terms)
        if halves == 2:
            return jnp.where(half == 1 - which, ref[at, here, :], 0.0)
        return ref[at + which, here, :]

    def stencil(row, slot):
        high, low = slots[slot]
        for index in range(owners):
            side_refs, side_row = (near, (index - 1) * rows + row) if index else (own_near, row)
            for start in range(0, block, step):
                here = pl.ds(start, step)
                centre = pieces[index][row, here, :]
                up = pieces[index][row - 1, here, :] if row > 0 else beyond(index, 0, here)
                down = pieces[index][row + 1, here, :] if row < last else beyond(index, 1, here)
                left, right = with_sides(centre, lanes)
                others = (side_refs[0][side_row, here, :], side_refs[1][side_row, here, :], up, down, left, right)
                slopes = [centre - other for other in others]
                for term in range(terms):
                    total = faces[6 * term, row : row + 1, :] * slopes[0]
                    for side in range(1, 6):
                        total = total + faces[6 * term + side, row : row + 1, :] * slopes[side]
                    rounded = total.astype(jnp.bfloat16)
                    at = pl.ds(term * modes + index * block + start, step)
                    high[at, :] = rounded
                    low[at, :] = (total - rounded.astype(jnp.float32)).astype(jnp.bfloat16)

    def mix(row, slot):
        high, low = slots[slot]
        both = jnp.dot(matrix_ref[...], high[...], preferred_element_type=jnp.float32)
        rest = jnp.dot(matrix_ref[:modes, :], low[...], preferred_element_type=jnp.float32)
        total = both[:modes] + both[modes:] + rest
        if by_owner:
            for owner in range(owners):
                outs[0][owner, row] = total[owner * block : (owner + 1) * block]
            return
        mixed[...] = total
        for index, shift in enumerate([0] + shifts):
            owner = lax.rem(me + shift, owners)
            outs[index][row] = mixed[pl.ds(pl.multiple_of(owner * block, block), block), :]

    stencil(0, 0)
    for row in range(rows):
        if row < last:
            stencil(row + 1, (row + 1) % 2)
        mix(row, row % 2)


def apply_operator(me, coef, matrix, own, own_near, groups, near, part, rows, shifts, by_owner):
    _, block, width = own.shape
    owners = len(shifts) + 1
    modes = owners * block
    terms, height, _ = coef.shape
    parts = height // (owners // 2) // rows
    edges = edge_count(owners // 2)
    head = head_rows(terms, owners // 2)

    def at(count, first):
        return pl.BlockSpec((count, block, width), lambda i: (first // count, 0, 0))

    def pieces_at(first, count):
        group, first_in = first // rows, first % rows
        return [own, *groups[group]], [at(count, head + first)] + [at(count, first_in)] * len(shifts)

    def edge_pieces():
        return [own, *groups[0]], [at(1, 0)] + [at(edges, rows)] * len(shifts)

    operands = [coef, matrix, own, *own_near, *own_near, *near]
    in_specs = [SCALARS, whole(coef), whole(matrix)] + [at(head, 0)] * 3
    in_specs += [at(rows, head + part * rows)] * 2 + [whole(array) for array in near]
    for arrays, specs in (
        pieces_at(part * rows, rows),
        pieces_at(part * rows - 1, 1) if part else edge_pieces(),
        pieces_at((part + 1) * rows, 1) if part < parts - 1 else edge_pieces(),
    ):
        operands += arrays
        in_specs += specs
    shape, count = ((owners, rows, block, width), 1) if by_owner else ((rows, block, width), owners)
    return pl.pallas_call(
        functools.partial(operator_kernel, shifts, terms, part, parts, by_owner),
        grid=(1,),
        in_specs=in_specs,
        out_specs=[pl.BlockSpec(shape, lambda i: (0,) * len(shape))] * count,
        out_shape=[jax.ShapeDtypeStruct(shape, jnp.float32)] * count,
        scratch_shapes=[pltpu.VMEM((terms * modes, width), jnp.bfloat16)] * 4
        + [pltpu.VMEM((modes, width), jnp.float32), pltpu.VMEM((6 * terms, rows, width), jnp.float32)],
        compiler_params=params(),
        cost_estimate=cost(6),
        name="operator",
    )(me, *operands)


def finish_kernel(shifts, by_owner, me_ref, *refs):
    owners = len(shifts) + 1
    halves = owners // 2
    mixed = refs[: 2 if by_owner else owners]
    state_ref, control_ref = refs[len(mixed) : len(mixed) + 2]
    state_out, adjoint_out = refs[-2:]
    half = pl.program_id(0)
    if by_owner:
        adjoint_out[...] = jnp.swapaxes(mixed[0][0], 0, 1) - control_ref[...]
        state_out[...] = state_ref[...] + jnp.swapaxes(mixed[1][0], 0, 1)
        return
    for index, shift in enumerate([0] + shifts):
        source = lax.rem(me_ref[0] + owners - shift, owners)

        @pl.when(source == half)
        def _(index=index):
            adjoint_out[...] = jnp.swapaxes(mixed[index][...], 0, 1) - control_ref[...]

        @pl.when(source == halves + half)
        def _(index=index):
            state_out[...] = state_ref[...] + jnp.swapaxes(mixed[index][...], 0, 1)


def finish(me, mixed, state, control, outputs, part, shifts):
    modes, _, width = state.shape
    halves = (len(shifts) + 1) // 2
    rows = mixed[0].shape[-3]
    parts = state.shape[1] // halves // rows
    block = pl.BlockSpec((modes, rows, width), lambda h: (0, h * parts + part, 0))
    by_owner = len(mixed) == 1
    if by_owner:
        sources = [
            pl.BlockSpec((1, rows, modes, width), lambda h, field=field: (field * halves + h, 0, 0, 0))
            for field in range(2)
        ]
        mixed = mixed * 2
    else:
        sources = [whole(m) for m in mixed]
    in_specs = [SCALARS] + sources + [block] * 2
    operands = [me, *mixed, state, control]
    aliases = {}
    if outputs is not None:
        aliases = {len(operands) + i: i for i in range(2)}
        in_specs += [ANYWHERE] * 2
        operands += list(outputs)
    return pl.pallas_call(
        functools.partial(finish_kernel, shifts, by_owner),
        grid=(halves,),
        in_specs=in_specs,
        out_specs=[block] * 2,
        out_shape=[jax.ShapeDtypeStruct(state.shape, jnp.float32)] * 2,
        input_output_aliases=aliases,
        compiler_params=params(60),
        cost_estimate=cost(2.5),
        name="finish",
    )(*operands)


def shards(state, control, adjoint, coefficient, pattern, weights):
    shape = state.shape
    modes, _, height, width = shape
    control_residual = 0.5 * control - adjoint
    state, control, adjoint = (a.reshape(modes, height, width) for a in (state, control, adjoint))
    coef = coefficient[:, 0]
    owners = lax.axis_size("mode")
    rows = TILE
    parts = height // (owners // 2) // rows
    planes = lax.axis_size("space")
    forward = [(i, i + 1) for i in range(planes - 1)]
    backward = [(i + 1, i) for i in range(planes - 1)]
    me = lax.axis_index("mode").astype(jnp.int32).reshape(1)
    shifts = sorted(range(1, owners), key=lambda s: -min(s, owners - s))

    def move(array, shift):
        return lax.ppermute(array, "mode", [(i, (i + shift) % owners) for i in range(owners)])

    def beside(array):
        return lax.ppermute(array, "space", forward), lax.ppermute(array, "space", backward)

    matrix = coupling_matrices(me, pattern, weights, shifts)
    groups, bodies, nears, mixed = [], [], [], []

    def exchange(part):
        earlier = [own] if part == 1 else [mixed[part - 3][0]] if part > 2 else [bodies[0]]
        packed = pack(me, state, adjoint, shifts, part, rows, owners, earlier)
        groups.append([move(piece, shift) for piece, shift in zip(packed, shifts)])

    def halo(part):
        earlier = [mixed[part - 2][0]] if part > 1 else [] if part else own_near
        bodies.append(gather(groups[part], rows, 0, earlier))
        nears.append(beside(bodies[part]))

    def operate(part):
        mixed.append(
            apply_operator(me, coef, matrix, own, own_near, groups, nears[part], part, rows, shifts, part == 0)
        )

    packed = pack_all(state, adjoint, owners // 2)
    everyone = lax.all_to_all(packed, "mode", 0, 0, tiled=True)
    groups.append(
        [lax.dynamic_index_in_dim(everyone, lax.rem(me[0] + owners - s, owners), keepdims=False) for s in shifts]
    )
    own = pack_own(me, state, adjoint, coef, owners, [packed])
    own_near = list(beside(own))
    halo(0)
    exchange(1)
    halo(1)
    for part in range(parts):
        if part + 2 < parts:
            exchange(part + 2)
        operate(part)
        if part + 2 < parts:
            halo(part + 2)

    outputs = None
    for part in range(parts):
        if part == 0:
            returned = [lax.all_to_all(mixed[0][0], "mode", 0, 0, tiled=True)]
        else:
            returned = [mixed[part][0]] + [move(m, shift) for m, shift in zip(mixed[part][1:], shifts)]
        outputs = finish(me, returned, state, control, outputs, part, shifts)
    return outputs[0].reshape(shape), control_residual, outputs[1].reshape(shape)


def solution(mesh):
    split = P("mode", "space", None, None)
    in_specs = (split, split, split, P(None, "space", None, None), P(), P())
    return jax.shard_map(shards, mesh=mesh, in_specs=in_specs, out_specs=(split, split, split), check_vma=False)
```
